256 devices in a mesh: slab: 16 (over x, y_lo, core), coil: 16 (over z, y_hi).
Axes of the slice: x: 4, y: 4 (y_hi: 2, y_lo: 2; y = y_hi * 2 + y_lo), z: 8, core: 2. Of those that a mesh axis runs over, the one named last changes fastest.
Arguments:
- sensitivity: float32 [16, 2, 32, 256, 128], P('coil', None, 'slab'), may hold values from -2.5 to 2.5
- kspace: float32 [16, 2, 32, 256, 128], P('coil', None, 'slab')
- sampling: int32 [32, 256, 128], P('slab'), may hold values 0 or 1
- prior_image: float32 [2, 32, 256, 128], P(None, 'slab', 'coil')
- w_first: bfloat16 [32, 2, 3, 3, 3], replicated, may hold values from -0.875 to 0.875
- w_middle: bfloat16 [3, 32, 32, 3, 3, 3], replicated, may hold values from -0.21875 to 0.21875
- w_last: bfloat16 [2, 32, 3, 3, 3], replicated, may hold values from -0.21875 to 0.21875
Outputs:
- solution: float32 [2, 32, 256, 128], P(None, 'slab', 'coil')
- refined: float32 [2, 32, 256, 128], P(None, 'slab', 'coil')
The draws below stay inside these ranges and needn't reach their ends.
Inputs may be any that keep to these rules, and one draw needn't show every extreme that they name: sampling marks the measured ky-kz positions of each readout plane.
All inputs are finite; a program needn't handle non-finite values. No bound on the sum of `sampling` on one device may be relied on, other than what follows from the above.
Results may differ from the reference program's by a relative error of at most 0.0015.
Values may be sent and summed in bfloat16 or wider, within the bound.
No kernel may reach another device: no remote copies, remote signals or barrier semaphores. Data moves between devices by JAX's collectives and lax.ppermute only.
A program may use at most 64 MiB of HBM per device.

```python
import math
import jax
import jax.numpy as jnp
from jax import lax

NY = 256
NZ = 128
CHANNELS = 32
LAYERS = 5
ITERS = 2
NX = 32
COILS = 16


def scaled_field(key, lead_shape):
    full_shape = lead_shape + (NX, NY, NZ)
    key_values, key_rows, key_columns = jax.random.split(key, 3)
    positions = jnp.arange(NX, dtype=jnp.float32) / max(NX - 1, 1)
    values_raw = jax.random.truncated_normal(key_values, -4.0, 4.0, full_shape, jnp.float32)
    ramp_x = 3.0 ** (0.5 * positions)
    log_half = 0.5 * math.log(10.0)
    row_scale = jnp.exp(jax.random.uniform(key_rows, (NY,), jnp.float32, -log_half, log_half))
    column_scale = jnp.exp(jax.random.uniform(key_columns, (NZ,), jnp.float32, -log_half, log_half))
    return values_raw * ramp_x[:, None, None] * row_scale[:, None] * column_scale


def draw_kspace(key, part):
    return scaled_field(jax.random.fold_in(key, 11), (COILS, 2))


def draw_prior_image(key, part):
    return scaled_field(jax.random.fold_in(key, 23), (2,))


def touch_ends(values, own_key, low, largest):
    dims = values.shape
    spot = [jax.random.randint(jax.random.fold_in(own_key, axis), (), 0, dims[axis]) for axis in range(len(dims))]
    values = values.at[tuple(spot)].set(low)
    longest = dims.index(max(dims))
    spot[longest] = (spot[longest] + 1) % dims[longest]
    return values.at[tuple(spot)].set(largest)


def steps_of(key, shape, cuts, smallest, high):
    level = 1.0
    for dim, shards_of in cuts:
        draws = jax.random.uniform(jax.random.fold_in(jax.random.fold_in(key, 6), dim), (shards_of,), jnp.float32, smallest / len(cuts), high / len(cuts))
        level = level * jnp.repeat(jnp.exp(draws), shape[dim] // shards_of).reshape((-1,) + (1,) * (len(shape) - 1 - dim))
    return level


def normal_values(rng, dims, spread, limit, cuts=(), kind=jnp.bfloat16):
    entries = jax.random.normal(rng, dims, jnp.float32) * spread
    if len(cuts) > 0:
        entries = steps_of(rng, dims, cuts, -0.22, 0.18) * entries
    return jnp.clip(entries, min=-limit, max=limit).astype(kind)


def setup_inputs(seed: int = 0) -> dict:
    key_of = jax.random.split(jax.random.key(seed), 8)
    return {
        "sensitivity": normal_values(key_of[0], (COILS, 2, NX, NY, NZ), ((2 * COILS) ** -0.5), 2.5, ((0, 16), (2, 16)), jnp.float32),
        "kspace": draw_kspace(jax.random.fold_in(key_of[7], 71), 0),
        "sampling": touch_ends((jax.random.randint(key_of[2], (NX, NY, NZ), 0, 3) < 1).astype(jnp.int32), jax.random.fold_in(key_of[2], 1), 0, 1),
        "prior_image": draw_prior_image(jax.random.fold_in(key_of[7], 71), 0),
        "w_first": normal_values(key_of[4], (CHANNELS, 2, 3, 3, 3), 54 ** -0.5, 0.875),
        "w_middle": normal_values(key_of[5], (LAYERS - 2, CHANNELS, CHANNELS, 3, 3, 3), (27 * CHANNELS) ** -0.5, 0.21875),
        "w_last": normal_values(key_of[6], (2, CHANNELS, 3, 3, 3), (27 * CHANNELS) ** -0.5, 0.21875),
    }


LAMBDA = 0.5


def to_kspace(field):
    values = jnp.fft.fft2(lax.complex(field[0], field[1]), axes=(-2, -1), norm="ortho")
    return jnp.stack([jnp.real(values), jnp.imag(values)])


def to_image(field):
    values = jnp.fft.ifft2(lax.complex(field[0], field[1]), axes=(-2, -1), norm="ortho")
    return jnp.stack([jnp.real(values), jnp.imag(values)])


def conj_apply(coil_maps, field):
    real_part = coil_maps[0] * field[0] + coil_maps[1] * field[1]
    imag_part = coil_maps[0] * field[1] - coil_maps[1] * field[0]
    return jnp.stack([real_part, imag_part])


def normal_image(direction, sensitivity, mask_f):
    def one_coil(total, coil_maps):
        coil_field = jnp.stack([coil_maps[0] * direction[0] - coil_maps[1] * direction[1],
                                coil_maps[0] * direction[1] + coil_maps[1] * direction[0]])
        spectrum = to_kspace(coil_field) * mask_f
        return total + conj_apply(coil_maps, to_image(spectrum)), None

    total, _ = lax.scan(one_coil, jnp.zeros_like(direction), sensitivity)
    return total


def adjoint_image(sensitivity, kspace, mask_f, template):
    def one_coil(total, pieces):
        coil_maps, measured = pieces
        return total + conj_apply(coil_maps, to_image(measured * mask_f)), None

    total, _ = lax.scan(one_coil, jnp.zeros_like(template), (sensitivity, kspace))
    return total


def conv_volume(activation, weight):
    result = lax.conv_general_dilated(activation[None].astype(jnp.float32), weight.astype(jnp.float32),
                                      (1, 1, 1), "SAME", dimension_numbers=("NCDHW", "OIDHW", "NCDHW"),
                                      precision=lax.Precision.HIGHEST)
    return result[0]


def reference(sensitivity, kspace, sampling, prior_image, w_first, w_middle, w_last):
    mask_f = sampling.astype(jnp.float32)
    rhs = adjoint_image(sensitivity, kspace, mask_f, prior_image) + LAMBDA * prior_image
    solution = jnp.zeros_like(prior_image)
    residual = rhs
    direction = rhs
    norm_now = jnp.sum(residual * residual)
    for step_index in range(ITERS):
        image_q = normal_image(direction, sensitivity, mask_f) + LAMBDA * direction
        step_size = norm_now / jnp.sum(direction * image_q)
        solution = solution + step_size * direction
        if step_index + 1 < ITERS:
            residual = residual - step_size * image_q
            norm_next = jnp.sum(residual * residual)
            direction = residual + (norm_next / norm_now) * direction
            norm_now = norm_next
    features = solution.astype(jnp.bfloat16)
    hidden = jax.nn.relu(conv_volume(features, w_first)).astype(jnp.bfloat16)
    for layer_index in range(w_middle.shape[0]):
        hidden = jax.nn.relu(conv_volume(hidden, w_middle[layer_index])).astype(jnp.bfloat16)
    correction = conv_volume(hidden, w_last)
    return solution, solution + correction
```

```python
import functools
import math

import jax
import jax.numpy as jnp
import numpy as np
from jax import lax
from jax.experimental import pallas as pl
from jax.experimental.pallas import tpu as pltpu
from jax.sharding import PartitionSpec as P

LAMBDA = 0.5
HALO = 5
SIDE = 8
GROUP = 3
F32 = jnp.float32
BF16 = jnp.bfloat16
VMEM_BYTES = 48 * 1024 * 1024


def call(kernel, out_shape, args, scratch=(), in_smem=()):
    specs = [
        pl.BlockSpec(memory_space=pltpu.SMEM if i in in_smem else pltpu.VMEM) for i in range(len(args))
    ]
    outs = jax.tree.map(lambda _: pl.BlockSpec(memory_space=pltpu.VMEM), out_shape)
    return pl.pallas_call(
        kernel,
        out_shape=out_shape,
        in_specs=specs,
        out_specs=outs,
        scratch_shapes=list(scratch),
        compiler_params=pltpu.CompilerParams(vmem_limit_bytes=VMEM_BYTES),
    )(*args)


def struct(shape, dtype=F32):
    return jax.ShapeDtypeStruct(shape, dtype)


def halves(table):
    high = table.astype(np.float32).astype(jnp.bfloat16)
    low = (table.astype(np.float32) - high.astype(np.float32)).astype(jnp.bfloat16)
    return high, low


def dft_pair(length, sign):
    positions = np.arange(length)
    angles = 2.0 * math.pi / length * (positions[:, None] * positions[None, :] % length)
    scaling = 1.0 / math.sqrt(length)
    return np.cos(angles) * scaling, sign * scaling * np.sin(angles)


def left_table(length, sign):
    cosine, sine = dft_pair(length, sign)
    high, low = halves(np.block([[cosine, -sine], [sine, cosine]]))
    return np.concatenate([high, high, low], axis=1)


def right_table(length, sign):
    cosine, sine = dft_pair(length, sign)
    high, low = halves(np.block([[cosine, sine], [-sine, cosine]]))
    return np.concatenate([high, high, low], axis=0)


def split(values):
    high = values.astype(BF16)
    low = (values - high.astype(F32)).astype(BF16)
    return high, low


def dft_rows(values, table_ref):
    high, low = split(values)
    return jnp.dot(table_ref[...], jnp.concatenate([high, low, high], axis=0), preferred_element_type=F32)


def dft_columns(values, table_ref):
    high, low = split(values)
    return jnp.dot(jnp.concatenate([high, low, high], axis=1), table_ref[...], preferred_element_type=F32)


def by_rows(field):
    return jnp.concatenate([jnp.concatenate(field[0], axis=1), jnp.concatenate(field[1], axis=1)], axis=0)


def by_columns(field):
    planes = range(len(field[0]))
    return jnp.concatenate([jnp.concatenate([field[0][p], field[1][p]], axis=1) for p in planes], axis=0)


def from_rows(values):
    rows, columns = values.shape[0] // 2, values.shape[1] // 2
    return [[values[a * rows : (a + 1) * rows, p * columns : (p + 1) * columns] for p in range(2)] for a in range(2)]


def from_columns(values):
    rows, columns = values.shape[0] // 2, values.shape[1] // 2
    return [[values[p * rows : (p + 1) * rows, a * columns : (a + 1) * columns] for p in range(2)] for a in range(2)]


def load_image(blocks_ref):
    count, _, columns = blocks_ref.shape
    rows = 16

    def one(a, p):
        start = (2 * a + p) * rows
        return blocks_ref[:, start : start + rows, :].reshape(count * rows, columns)

    return [[one(a, p) for p in range(2)] for a in range(2)]


def store_image(blocks_ref, image):
    count, _, columns = blocks_ref.shape
    rows = 16
    for a in range(2):
        for p in range(2):
            start = (2 * a + p) * rows
            blocks_ref[:, start : start + rows, :] = image[a][p].reshape(count, rows, columns)


def coil_field(maps_ref, image):
    real = [maps_ref[0, p] * image[0][p] - maps_ref[1, p] * image[1][p] for p in range(2)]
    imag = [maps_ref[0, p] * image[1][p] + maps_ref[1, p] * image[0][p] for p in range(2)]
    return [real, imag]


def coil_term(maps_ref, field):
    real = [maps_ref[0, p] * field[0][p] + maps_ref[1, p] * field[1][p] for p in range(2)]
    imag = [maps_ref[0, p] * field[1][p] - maps_ref[1, p] * field[0][p] for p in range(2)]
    return [real, imag]


def mask_rows(mask_ref):
    mask = jnp.concatenate([mask_ref[0].astype(F32), mask_ref[1].astype(F32)], axis=1)
    return jnp.concatenate([mask, mask], axis=0)


def row_sum(values):
    folded = jnp.sum(values.reshape(-1, 8, values.shape[-1]), axis=0)
    folded = jnp.sum(folded, axis=0, keepdims=True)
    while folded.shape[1] > 128:
        half = folded.shape[1] // 2
        folded = folded[:, :half] + folded[:, half:]
    return folded


def tile_of(rows):
    blank = jnp.zeros((1, 128), F32)
    return jnp.concatenate(list(rows) + [blank] * (8 - len(rows)), axis=0)


def scalar_of(tile, row):
    return jnp.sum(tile[row : row + 1, :])


def store_near(near_ref, blocks_ref, at):
    count = blocks_ref.shape[0]
    for a in range(2):
        for p in range(2):
            start = (2 * a + p) * 16
            near_ref[p, a, 8:24, :] = blocks_ref[at, start : start + 16, :]
            before = blocks_ref[jnp.maximum(at - 1, 0), start + 8 : start + 16, :]
            after = blocks_ref[jnp.minimum(at + 1, count - 1), start : start + 8, :]
            near_ref[p, a, 0:8, :] = jnp.where(at > 0, before, 0.0)
            near_ref[p, a, 24:32, :] = jnp.where(at < count - 1, after, 0.0)


def adjoint_kernel(kspace_ref, mask_ref, maps_ref, rows_ref, columns_ref, out_ref):
    field = [[kspace_ref[a, p] for p in range(2)] for a in range(2)]
    field = from_rows(dft_rows(by_rows(field) * mask_rows(mask_ref), rows_ref))
    field = from_columns(dft_columns(by_columns(field), columns_ref))
    store_image(out_ref, coil_term(maps_ref, field))


def rows_kernel(blocks_ref, prior_ref, rows_ref, copies_ref):
    count = blocks_ref.shape[0]
    total = jnp.sum(blocks_ref[...], axis=0)
    prior = jnp.concatenate([prior_ref[a, p] for a in range(2) for p in range(2)], axis=0)
    total = total + LAMBDA * prior
    rows_ref[...] = total
    for k in range(count):
        copies_ref[k] = total


def normal_kernel(
    at_ref, blocks_ref, mask_ref, maps_ref, rows_f, columns_f, rows_b, columns_b, out_ref, spectrum_ref, tile_ref, near_ref
):
    store_near(near_ref, blocks_ref, at_ref[0])
    image = load_image(blocks_ref)
    norm = sum(row_sum(image[a][p] * image[a][p]) for a in range(2) for p in range(2))
    field = from_columns(dft_columns(by_columns(coil_field(maps_ref, image)), columns_f))
    spectrum = dft_rows(by_rows(field), rows_f) * mask_rows(mask_ref)
    spectrum_ref[...] = spectrum
    energy = row_sum(spectrum * spectrum)
    field = from_rows(dft_rows(spectrum, rows_b))
    field = from_columns(dft_columns(by_columns(field), columns_b))
    store_image(out_ref, coil_term(maps_ref, field))
    tile_ref[...] = tile_of([norm])
    energies = tile_of([energy])
    for k in range(blocks_ref.shape[0]):
        out_ref[k, 64:72, :] = energies


def image_kernel(blocks_ref, rhs_rows_ref, norms_ref, copies_ref, sums_ref):
    count = blocks_ref.shape[0]
    total = jnp.sum(blocks_ref[...], axis=0)
    rows = total[:64] + LAMBDA * rhs_rows_ref[...]
    sums = tile_of([norms_ref[0:1, :], total[64:65]])
    for k in range(count):
        copies_ref[k] = rows
        sums_ref[k] = sums


def first_step(sums_ref):
    tile = jnp.sum(sums_ref[...], axis=0)
    norm, energy = scalar_of(tile, 0), scalar_of(tile, 1)
    return norm, energy, norm / (energy + LAMBDA * norm)


def last_kernel(
    at_ref, sums_ref, blocks_ref, rhs_ref, spectrum_ref, mask_ref, maps_ref, rows_f, columns_f, out_ref, near_ref
):
    store_near(near_ref, blocks_ref, at_ref[0])
    step = first_step(sums_ref)[2]
    image = load_image(blocks_ref)
    rhs = load_image(rhs_ref)
    norm = jnp.zeros((1, 128), F32)
    cross = jnp.zeros((1, 128), F32)
    for a in range(2):
        for p in range(2):
            residual = rhs[a][p] - step * image[a][p]
            norm = norm + row_sum(residual * residual)
            cross = cross + row_sum(residual * rhs[a][p])
    field = from_columns(dft_columns(by_columns(coil_field(maps_ref, image)), columns_f))
    spectrum = dft_rows(by_rows(field), rows_f) * mask_rows(mask_ref)
    spectrum = spectrum_ref[...] - step * spectrum
    tile = tile_of([row_sum(spectrum * spectrum), row_sum(spectrum * spectrum_ref[...]), norm, cross])
    for k in range(out_ref.shape[0]):
        out_ref[k] = tile


def spread_kernel(tiles_ref, out_ref):
    total = jnp.sum(tiles_ref[...], axis=0)
    for k in range(out_ref.shape[0]):
        out_ref[k] = total


def starts_of(rows):
    starts = list(range(0, rows - GROUP + 1, GROUP))
    if starts[-1] + GROUP < rows:
        starts.append(rows - GROUP)
    return starts


def shifted_sum(parts):
    before, here, after = parts
    lane = lax.broadcasted_iota(jnp.int32, before.shape[:1] + (128,), 1)
    outs = []
    for h in range(2):
        cut = slice(128 * h, 128 * (h + 1))
        low = jnp.where(lane > 0, pltpu.roll(before[:, cut], 1, 1), 0.0)
        high = jnp.where(lane < 127, pltpu.roll(after[:, cut], 127, 1), 0.0)
        outs.append(here[:, cut] + low + high)
    return jnp.concatenate(outs, axis=1)


def denoise_kernel(coil_count, slab_count, *refs):
    at_ref, sums_ref, last_ref = refs[:3]
    rhs_refs = refs[3:10]
    image_refs = refs[10:17]
    w_first_ref, w_middle_ref, w_last_ref, solution_ref, refined_ref = refs[17:22]
    features_ref = refs[22]
    hidden_refs = refs[23:]
    coil_at = at_ref[0]
    slab_at = at_ref[1]

    norm_first, energy_first, step_first = first_step(sums_ref)
    tile = jnp.sum(last_ref[...], axis=0)
    copies = 1.0 / coil_count
    norm, cross = scalar_of(tile, 2) * copies, scalar_of(tile, 3) * copies
    ratio = norm / norm_first
    curvature = scalar_of(tile, 0) + ratio * (2.0 * scalar_of(tile, 1) + ratio * energy_first)
    curvature = curvature + LAMBDA * (norm + ratio * (2.0 * cross + ratio * norm_first))
    step_last = norm / curvature
    scale_rhs = step_first + step_last * ratio

    lane = lax.broadcasted_iota(jnp.int32, (48, 128), 1)
    plane = 0
    brick = None
    for rhs_ref, image_ref in zip(rhs_refs, image_refs):
        for p in range(rhs_ref.shape[0]):
            full = []
            for a in range(2):
                rhs = rhs_ref[p, a]
                full.append(scale_rhs * rhs + step_last * (rhs - step_first * image_ref[p, a]))
            if 5 <= plane < 7:
                for a in range(2):
                    solution_ref[a, plane - 5] = full[a][8:24]
            for h in range(2):
                window = jnp.concatenate([f[8 * h : 8 * h + 24] for f in full], axis=0)
                cut = slice(128 * h, 128 * (h + 1))
                low = jnp.where(lane > 0, pltpu.roll(window, 1, 1), 0.0)
                high = jnp.where(lane < 127, pltpu.roll(window, 127, 1), 0.0)
                features_ref[plane, 0:48, cut] = low.astype(BF16)
                features_ref[plane, 48:96, cut] = window.astype(BF16)
                features_ref[plane, 96:144, cut] = high.astype(BF16)
            plane += 1

    def outside(out_ref, depth):
        planes, cells, _ = out_ref.shape
        extra = 4 - depth
        first = 2 * slab_at - extra

        @pl.when(coil_at == 0)
        def _():
            out_ref[:, 0 : extra * 32, 0:128] = jnp.zeros((planes, extra * 32, 128), BF16)

        @pl.when(coil_at == coil_count - 1)
        def _():
            out_ref[:, cells - extra * 32 : cells, 128:256] = jnp.zeros((planes, extra * 32, 128), BF16)

        for p in list(range(extra)) + list(range(planes - extra, planes)):

            @pl.when((first + p < 0) | (first + p >= 2 * slab_count))
            def _():
                out_ref[p] = jnp.zeros(out_ref.shape[1:], BF16)

    first_out = hidden_refs[0]

    def first_plane(p, carry):
        taps = jnp.concatenate([features_ref[p + u] for u in range(3)], axis=0)
        values = jnp.dot(w_first_ref[...], taps, preferred_element_type=F32)
        first_out[p] = jnp.maximum(values, 0.0).astype(BF16)
        return carry

    lax.fori_loop(0, first_out.shape[0], first_plane, 0)
    outside(first_out, 0)

    for m in range(len(hidden_refs) - 1):
        in_ref, out_ref = hidden_refs[m], hidden_refs[m + 1]
        starts = starts_of(out_ref.shape[1] // 32)

        def middle_plane(p, carry, m=m, in_ref=in_ref, out_ref=out_ref, starts=starts):
            for start in starts:
                rows = slice(start * 32, (start + GROUP + 2) * 32)
                taps = jnp.concatenate([in_ref[p + u, rows] for u in range(3)], axis=0)
                sums = jnp.dot(w_middle_ref[m], taps, preferred_element_type=F32)
                cells = GROUP * 32
                values = shifted_sum([sums[t * cells : (t + 1) * cells] for t in range(3)])
                out_ref[p, start * 32 : (start + GROUP) * 32] = jnp.maximum(values, 0.0).astype(BF16)
            return carry

        lax.fori_loop(0, out_ref.shape[0], middle_plane, 0)
        outside(out_ref, m + 1)

    in_ref = hidden_refs[-1]
    for p in range(2):
        taps = jnp.concatenate([in_ref[p + u] for u in range(3)], axis=0)
        sums = jnp.dot(w_last_ref[...], taps, preferred_element_type=F32)
        values = shifted_sum([sums[t * 16 : (t + 1) * 16] for t in range(3)])
        for a in range(2):
            for h in range(2):
                piece = values[8 * a : 8 * a + 8, 128 * h : 128 * h + 128]
                refined_ref[a, p, 8 * h : 8 * h + 8] = solution_ref[a, p, 8 * h : 8 * h + 8] + piece


def banded(weight, rows):
    taps = jnp.transpose(weight, (4, 0, 2, 3, 1))
    bands = [jnp.pad(taps, ((0, 0), (0, 0), (0, 0), (r, rows - 1 - r), (0, 0))) for r in range(rows)]
    return jnp.stack(bands, axis=1)


def first_table(weight):
    taps = jnp.transpose(weight, (0, 2, 4, 1, 3))
    bands = [
        jnp.pad(taps, ((0, 0), (0, 0), (0, 0), (0, 0), (r + SIDE - HALO, 24 - 3 - r - SIDE + HALO))) for r in range(16)
    ]
    return jnp.stack(bands, axis=0).reshape(16 * weight.shape[0], 3 * 3 * 2 * 24)


def middle_table(weight):
    bands = banded(weight, GROUP)
    return bands.reshape(3 * GROUP * 32, 3 * (GROUP + 2) * 32)


def last_table(weight):
    bands = jnp.transpose(banded(weight, 8), (0, 2, 1, 3, 4, 5))
    return bands.reshape(3 * 2 * 8, 3 * 10 * 32)


def swap(blocks, axis):
    return lax.all_to_all(blocks, axis, 0, 0, tiled=True)


def near_planes(near):
    count = lax.axis_size("slab")

    def shifted(part, step):
        pairs = [(i, i + step) for i in range(count) if 0 <= i + step < count]
        return lax.ppermute(part, "slab", pairs)

    below = [shifted(near[1:], 3), shifted(near, 2), shifted(near, 1)]
    above = [shifted(near, -1), shifted(near, -2), shifted(near[:1], -3)]
    return below + [near] + above


def body(sensitivity, kspace, sampling, prior_image, w_first, w_middle, w_last):
    maps = sensitivity[0]
    len_y, len_z = maps.shape[2:]
    coils, slabs = lax.axis_size("coil"), lax.axis_size("slab")
    at = jnp.stack([lax.axis_index("coil"), lax.axis_index("slab")]).astype(jnp.int32)
    rows_f, rows_b = left_table(len_y, -1.0), left_table(len_y, 1.0)
    columns_f, columns_b = right_table(len_z, -1.0), right_table(len_z, 1.0)

    term = call(adjoint_kernel, struct((coils, 64, 128)), (kspace[0], sampling, maps, rows_b, columns_b))
    rhs_rows, copies = call(
        rows_kernel, (struct((64, 128)), struct((coils, 64, 128))), (swap(term, "coil"), prior_image)
    )
    rhs = swap(copies, "coil")
    near_shape = struct((2, 2, 32, 128))
    term, spectrum, norms, rhs_near = call(
        normal_kernel,
        (struct((coils, 72, 128)), struct((2 * len_y, 2 * len_z)), struct((8, 128)), near_shape),
        (at, rhs, sampling, maps, rows_f, columns_f, rows_b, columns_b),
        in_smem=(0,),
    )
    rhs_parts = near_planes(rhs_near)
    copies, sums = call(
        image_kernel,
        (struct((coils, 64, 128)), struct((slabs, 8, 128))),
        (swap(term, "coil"), rhs_rows, norms),
    )
    image = swap(copies, "coil")
    sums = swap(sums, "slab")
    tiles, image_near = call(
        last_kernel,
        (struct((coils, 8, 128)), near_shape),
        (at, sums, image, rhs, spectrum, sampling, maps, rows_f, columns_f),
        in_smem=(0,),
    )
    image_parts = near_planes(image_near)
    tiles = call(spread_kernel, struct((slabs, 8, 128)), (swap(tiles, "coil"),))
    last = swap(tiles, "slab")
    middle = jnp.stack([middle_table(w_middle[m]) for m in range(w_middle.shape[0])])
    scratch = [pltpu.VMEM((12, 144, 256), BF16)]
    scratch += [pltpu.VMEM((10 - 2 * m, (16 - 2 * m) * 32, 256), BF16) for m in range(4)]
    return call(
        functools.partial(denoise_kernel, coils, slabs),
        (struct(prior_image.shape), struct(prior_image.shape)),
        (at, sums, last, *rhs_parts, *image_parts, first_table(w_first), middle, last_table(w_last)),
        scratch=scratch,
        in_smem=(0,),
    )


def solution(mesh):
    placed = (
        P("coil", None, "slab", None, None),
        P("coil", None, "slab", None, None),
        P("slab", None, None),
        P(None, "slab", "coil", None),
        P(),
        P(),
        P(),
    )
    return jax.shard_map(
        body,
        mesh=mesh,
        in_specs=placed,
        out_specs=(P(None, "slab", "coil", None), P(None, "slab", "coil", None)),
        check_vma=False,
    )
```

```python
import functools
import math

import jax
import jax.numpy as jnp
import numpy as np
from jax import lax
from jax.experimental import pallas as pl
from jax.experimental.pallas import tpu as pltpu
from jax.sharding import PartitionSpec as P

LAMBDA = 0.5
HALO = 5
SIDE = 8
GROUP = 3
F32 = jnp.float32
BF16 = jnp.bfloat16
VMEM_BYTES = 48 * 1024 * 1024


def call(kernel, out_shape, args, scratch=(), in_smem=()):
    specs = [
        pl.BlockSpec(memory_space=pltpu.SMEM if i in in_smem else pltpu.VMEM) for i in range(len(args))
    ]
    outs = jax.tree.map(lambda _: pl.BlockSpec(memory_space=pltpu.VMEM), out_shape)
    return pl.pallas_call(
        kernel,
        out_shape=out_shape,
        in_specs=specs,
        out_specs=outs,
        scratch_shapes=list(scratch),
        compiler_params=pltpu.CompilerParams(vmem_limit_bytes=VMEM_BYTES),
    )(*args)


def struct(shape, dtype=F32):
    return jax.ShapeDtypeStruct(shape, dtype)


def halves(table):
    high = table.astype(np.float32).astype(jnp.bfloat16)
    low = (table.astype(np.float32) - high.astype(np.float32)).astype(jnp.bfloat16)
    return high, low


def dft_pair(length):
    positions = np.arange(length)
    angles = 2.0 * math.pi / length * (positions[:, None] * positions[None, :] % length)
    scaling = 1.0 / math.sqrt(length)
    return np.cos(angles) * scaling, scaling * np.sin(angles)


def left_table(length):
    cosine, sine = dft_pair(length)
    parts = [np.concatenate(halves(part), axis=1) for part in (cosine, sine)]
    return np.concatenate(parts, axis=0)


def right_table(length):
    cosine, sine = dft_pair(length)
    return np.concatenate(halves(cosine) + halves(sine), axis=1)


def split(values):
    high = values.astype(BF16)
    low = (values - high.astype(F32)).astype(BF16)
    return high, low


def dft_rows(field, table_ref, sign):
    values = jnp.concatenate(field[0] + field[1], axis=1)
    high, low = split(values)
    size = values.shape[0]
    table_high, table_low = table_ref[:, :size], table_ref[:, size:]
    table = jnp.concatenate([table_high, table_high, table_low], axis=1)
    products = jnp.dot(table, jnp.concatenate([high, low, high], axis=0), preferred_element_type=F32)
    half = values.shape[1] // 2
    cosine, sine = products[:size], products[size:]
    real = cosine[:, :half] - sign * sine[:, half:]
    imag = cosine[:, half:] + sign * sine[:, :half]
    columns = half // 2
    return [[part[:, p * columns : (p + 1) * columns] for p in range(2)] for part in (real, imag)]


def dft_columns(field, table_ref, sign):
    values = by_columns(field)
    high, low = split(values)
    size = table_ref.shape[0]
    cosine_high, cosine_low, sine_high, sine_low = [table_ref[:, i * size : (i + 1) * size] for i in range(4)]

    def block(cosine, sine):
        plus, minus = (sine, -sine) if sign > 0 else (-sine, sine)
        return jnp.concatenate(
            [jnp.concatenate([cosine, plus], axis=1), jnp.concatenate([minus, cosine], axis=1)], axis=0
        )

    table_high = block(cosine_high, sine_high)
    table = jnp.concatenate([table_high, table_high, block(cosine_low, sine_low)], axis=0)
    return from_columns(jnp.dot(jnp.concatenate([high, low, high], axis=1), table, preferred_element_type=F32))


def by_columns(field):
    planes = range(len(field[0]))
    return jnp.concatenate([jnp.concatenate([field[0][p], field[1][p]], axis=1) for p in planes], axis=0)


def from_columns(values):
    rows, columns = values.shape[0] // 2, values.shape[1] // 2
    return [[values[p * rows : (p + 1) * rows, a * columns : (a + 1) * columns] for p in range(2)] for a in range(2)]


def load_image(blocks_ref):
    count, _, columns = blocks_ref.shape
    rows = 16

    def one(a, p):
        start = (2 * a + p) * rows
        return blocks_ref[:, start : start + rows, :].reshape(count * rows, columns)

    return [[one(a, p) for p in range(2)] for a in range(2)]


def store_image(blocks_ref, image):
    count, _, columns = blocks_ref.shape
    rows = 16
    for a in range(2):
        for p in range(2):
            start = (2 * a + p) * rows
            blocks_ref[:, start : start + rows, :] = image[a][p].reshape(count, rows, columns)


def coil_field(maps_ref, image):
    real = [maps_ref[0, p] * image[0][p] - maps_ref[1, p] * image[1][p] for p in range(2)]
    imag = [maps_ref[0, p] * image[1][p] + maps_ref[1, p] * image[0][p] for p in range(2)]
    return [real, imag]


def coil_term(maps_ref, field):
    real = [maps_ref[0, p] * field[0][p] + maps_ref[1, p] * field[1][p] for p in range(2)]
    imag = [maps_ref[0, p] * field[1][p] - maps_ref[1, p] * field[0][p] for p in range(2)]
    return [real, imag]


def masked(field, mask_ref):
    masks = [mask_ref[p].astype(F32) for p in range(2)]
    return [[field[a][p] * masks[p] for p in range(2)] for a in range(2)]


def inner(first, second):
    return sum(row_sum(first[a][p] * second[a][p]) for a in range(2) for p in range(2))


def row_sum(values):
    folded = jnp.sum(values.reshape(-1, 8, values.shape[-1]), axis=0)
    folded = jnp.sum(folded, axis=0, keepdims=True)
    return folded


def tile_of(rows):
    blank = jnp.zeros((1, 128), F32)
    return jnp.concatenate(list(rows) + [blank] * (8 - len(rows)), axis=0)


def store_near(near_ref, blocks_ref, at):
    count = blocks_ref.shape[0]
    for a in range(2):
        for p in range(2):
            start = (2 * a + p) * 16
            near_ref[p, a, 8:24, :] = blocks_ref[at, start : start + 16, :]
            before = blocks_ref[jnp.maximum(at - 1, 0), start + 8 : start + 16, :]
            after = blocks_ref[jnp.minimum(at + 1, count - 1), start : start + 8, :]
            near_ref[p, a, 0:8, :] = jnp.where(at > 0, before, 0.0)
            near_ref[p, a, 24:32, :] = jnp.where(at < count - 1, after, 0.0)


def adjoint_kernel(kspace_ref, mask_ref, rows_ref, columns_ref, maps_ref, out_ref):
    field = masked([[kspace_ref[a, p] for p in range(2)] for a in range(2)], mask_ref)
    field = dft_columns(dft_rows(field, rows_ref, 1.0), columns_ref, 1.0)
    store_image(out_ref, coil_term(maps_ref, field))


def rows_kernel(blocks_ref, prior_ref, rows_ref, copies_ref):
    count = blocks_ref.shape[0]
    total = jnp.sum(blocks_ref[...], axis=0)
    prior = jnp.concatenate([prior_ref[a, p] for a in range(2) for p in range(2)], axis=0)
    total = total + LAMBDA * prior
    rows_ref[...] = total
    for k in range(count):
        copies_ref[k] = total


def normal_kernel(
    at_ref, blocks_ref, mask_ref, maps_ref, rows_ref, columns_ref, out_ref, spectrum_ref, tile_ref, near_ref
):
    store_near(near_ref, blocks_ref, at_ref[0])
    image = load_image(blocks_ref)
    field = dft_columns(coil_field(maps_ref, image), columns_ref, -1.0)
    spectrum = masked(dft_rows(field, rows_ref, -1.0), mask_ref)
    for a in range(2):
        for p in range(2):
            spectrum_ref[a, p] = spectrum[a][p]
    field = dft_columns(dft_rows(spectrum, rows_ref, 1.0), columns_ref, 1.0)
    store_image(out_ref, coil_term(maps_ref, field))
    tile_ref[...] = tile_of([inner(image, image)])
    energies = tile_of([inner(spectrum, spectrum)])
    for k in range(blocks_ref.shape[0]):
        out_ref[k, 64:72, :] = energies


def image_kernel(blocks_ref, rhs_rows_ref, norms_ref, copies_ref, sums_ref):
    total = jnp.sum(blocks_ref[...], axis=0)
    rows = total[:64] + LAMBDA * rhs_rows_ref[...]
    for k in range(blocks_ref.shape[0]):
        copies_ref[k] = rows
    sums_ref[...] = tile_of([norms_ref[0:1, :], total[64:65]])


def lane_sum(values):
    return jnp.sum(values, axis=-1, keepdims=True)


def slab_step(norm, energy):
    curved = energy + LAMBDA * norm
    return jnp.where(curved > 0.0, norm / jnp.where(curved > 0.0, curved, 1.0), 1.0)


def last_kernel(
    at_ref, sums_ref, blocks_ref, rhs_ref, spectrum_ref, mask_ref, maps_ref, rows_ref, columns_ref, out_ref, near_ref
):
    store_near(near_ref, blocks_ref, at_ref[0])
    norm, energy = sums_ref[0:1, :], sums_ref[1:2, :]
    step = slab_step(lane_sum(norm), lane_sum(energy))
    image = load_image(blocks_ref)
    rhs = load_image(rhs_ref)
    field = dft_columns(coil_field(maps_ref, image), columns_ref, -1.0)
    spectrum = masked(dft_rows(field, rows_ref, -1.0), mask_ref)
    before = [[spectrum_ref[a, p] for p in range(2)] for a in range(2)]
    residual = [[rhs[a][p] - step * image[a][p] for p in range(2)] for a in range(2)]
    spectrum = [[before[a][p] - step * spectrum[a][p] for p in range(2)] for a in range(2)]
    share = 1.0 / out_ref.shape[0]
    local = [inner(residual, residual), inner(residual, rhs), norm, energy]
    tile = tile_of([inner(spectrum, spectrum), inner(spectrum, before)] + [share * value for value in local])
    for k in range(out_ref.shape[0]):
        out_ref[k] = tile


def spread_kernel(tiles_ref, out_ref):
    total = jnp.sum(tiles_ref[...], axis=0)
    for k in range(out_ref.shape[0]):
        out_ref[k] = total


def final_scales(tiles_ref):
    curve, curve_cross, norm, cross, norm_first, energy_first = [
        lane_sum(tiles_ref[:, i, :]) for i in range(6)
    ]

    def over_slabs(values):
        return jnp.sum(values, axis=0, keepdims=True)

    all_norm, all_energy = over_slabs(norm_first), over_slabs(energy_first)
    step_first = all_norm / (all_energy + LAMBDA * all_norm)
    here = step_first / slab_step(norm_first, energy_first)
    rest = 1.0 - here
    curve = over_slabs(here * here * curve + rest * (2.0 * here * curve_cross + rest * energy_first))
    curve_cross = over_slabs(here * curve_cross + rest * energy_first)
    norm = over_slabs(here * here * norm + rest * (2.0 * here * cross + rest * norm_first))
    cross = over_slabs(here * cross + rest * norm_first)
    ratio = norm / all_norm
    curvature = curve + ratio * (2.0 * curve_cross + ratio * all_energy)
    curvature = curvature + LAMBDA * (norm + ratio * (2.0 * cross + ratio * all_norm))
    return step_first, norm / curvature, ratio


def starts_of(rows):
    starts = list(range(0, rows - GROUP + 1, GROUP))
    if starts[-1] + GROUP < rows:
        starts.append(rows - GROUP)
    return starts


def shifted_sum(parts):
    before, here, after = parts
    lane = lax.broadcasted_iota(jnp.int32, before.shape[:1] + (128,), 1)
    outs = []
    for h in range(2):
        cut = slice(128 * h, 128 * (h + 1))
        low = jnp.where(lane > 0, pltpu.roll(before[:, cut], 1, 1), 0.0)
        high = jnp.where(lane < 127, pltpu.roll(after[:, cut], 127, 1), 0.0)
        outs.append(here[:, cut] + low + high)
    return jnp.concatenate(outs, axis=1)


def denoise_kernel(coil_count, slab_count, *refs):
    at_ref, last_ref = refs[:2]
    rhs_refs = refs[2:9]
    image_refs = refs[9:16]
    w_first_ref, w_middle_ref, w_last_ref, solution_ref, refined_ref = refs[16:21]
    features_ref = refs[21]
    hidden_refs = refs[22:]
    coil_at = at_ref[0]
    slab_at = at_ref[1]

    step_first, step_last, ratio = final_scales(last_ref)
    scale_rhs = step_first + step_last * ratio

    lane = lax.broadcasted_iota(jnp.int32, (48, 128), 1)
    plane = 0
    brick = None
    for rhs_ref, image_ref in zip(rhs_refs, image_refs):
        for p in range(rhs_ref.shape[0]):
            full = []
            for a in range(2):
                rhs = rhs_ref[p, a]
                full.append(scale_rhs * rhs + step_last * (rhs - step_first * image_ref[p, a]))
            if 5 <= plane < 7:
                for a in range(2):
                    solution_ref[a, plane - 5] = full[a][8:24]
            for h in range(2):
                window = jnp.concatenate([f[8 * h : 8 * h + 24] for f in full], axis=0)
                cut = slice(128 * h, 128 * (h + 1))
                low = jnp.where(lane > 0, pltpu.roll(window, 1, 1), 0.0)
                high = jnp.where(lane < 127, pltpu.roll(window, 127, 1), 0.0)
                features_ref[plane, 0:48, cut] = low.astype(BF16)
                features_ref[plane, 48:96, cut] = window.astype(BF16)
                features_ref[plane, 96:144, cut] = high.astype(BF16)
            plane += 1

    def outside(out_ref, depth):
        planes, cells, _ = out_ref.shape
        extra = 4 - depth
        first = 2 * slab_at - extra

        @pl.when(coil_at == 0)
        def _():
            out_ref[:, 0 : extra * 32, 0:128] = jnp.zeros((planes, extra * 32, 128), BF16)

        @pl.when(coil_at == coil_count - 1)
        def _():
            out_ref[:, cells - extra * 32 : cells, 128:256] = jnp.zeros((planes, extra * 32, 128), BF16)

        for p in list(range(extra)) + list(range(planes - extra, planes)):

            @pl.when((first + p < 0) | (first + p >= 2 * slab_count))
            def _():
                out_ref[p] = jnp.zeros(out_ref.shape[1:], BF16)

    first_out = hidden_refs[0]

    def first_plane(p, carry):
        taps = jnp.concatenate([features_ref[p + u] for u in range(3)], axis=0)
        values = jnp.dot(w_first_ref[:, :432], taps, preferred_element_type=F32)
        first_out[p] = jnp.maximum(values, 0.0).astype(BF16)
        return carry

    lax.fori_loop(0, first_out.shape[0], first_plane, 0)
    outside(first_out, 0)

    for m in range(len(hidden_refs) - 1):
        in_ref, out_ref = hidden_refs[m], hidden_refs[m + 1]
        starts = starts_of(out_ref.shape[1] // 32)

        def middle_plane(p, carry, m=m, in_ref=in_ref, out_ref=out_ref, starts=starts):
            for start in starts:
                rows = slice(start * 32, (start + GROUP + 2) * 32)
                taps = jnp.concatenate([in_ref[p + u, rows] for u in range(3)], axis=0)
                sums = jnp.dot(w_middle_ref[m, :, : (GROUP + 2) * 96], taps, preferred_element_type=F32)
                cells = GROUP * 32
                values = shifted_sum([sums[t * cells : (t + 1) * cells] for t in range(3)])
                out_ref[p, start * 32 : (start + GROUP) * 32] = jnp.maximum(values, 0.0).astype(BF16)
            return carry

        lax.fori_loop(0, out_ref.shape[0], middle_plane, 0)
        outside(out_ref, m + 1)

    in_ref = hidden_refs[-1]
    for p in range(2):
        taps = jnp.concatenate([in_ref[p + u] for u in range(3)], axis=0)
        sums = jnp.dot(w_last_ref[:, :960], taps, preferred_element_type=F32)
        lane = lax.broadcasted_iota(jnp.int32, (64, 128), 1)
        for h in range(2):
            part = sums[:, 128 * h : 128 * (h + 1)]
            low = jnp.where(lane > 0, pltpu.roll(part, 1, 1), 0.0)
            high = jnp.where(lane < 127, pltpu.roll(part, 127, 1), 0.0)
            for a in range(2):
                rows = []
                for r in range(8):
                    at = 8 * r + a
                    rows.append(low[at : at + 1] + part[at + 2 : at + 3] + high[at + 4 : at + 5])
                piece = jnp.concatenate(rows, axis=0)
                refined_ref[a, p, 8 * h : 8 * h + 8] = solution_ref[a, p, 8 * h : 8 * h + 8] + piece


def tables_kernel(first_ref, middle_ref, last_ref, w_first_ref, w_middle_ref, w_last_ref):
    def spots(size, target, count=512):
        column = lax.broadcasted_iota(jnp.int32, (size, count), 1)
        return jnp.where(column == target(lax.broadcasted_iota(jnp.int32, (size, count), 0)), 1.0, 0.0).astype(BF16)

    def first_target(source):
        channel, u, v, t = source // 27, source // 9 % 3, source // 3 % 3, source % 3
        return ((u * 3 + t) * 2 + channel) * 24 + SIDE - HALO + v

    base = jnp.dot(first_ref[...], spots(54, first_target), preferred_element_type=F32)
    for r in range(16):
        w_first_ref[32 * r : 32 * r + 32] = (pltpu.roll(base, r, 1) if r else base).astype(BF16)
    for m in range(middle_ref.shape[0]):
        base = jnp.zeros((96, 512), F32)
        for u in range(3):
            for v in range(3):
                place = spots(32, lambda source: source + (u * (GROUP + 2) + v) * 32)
                taps = jnp.concatenate([middle_ref[m, u, v, t] for t in range(3)], axis=0)
                base = base + jnp.dot(taps, place, preferred_element_type=F32)
        for r in range(GROUP):
            band = (pltpu.roll(base, 32 * r, 1) if r else base).astype(BF16)
            for t in range(3):
                start = (t * GROUP + r) * 32
                w_middle_ref[m, start : start + 32] = band[32 * t : 32 * t + 32]
    bands = []
    for r in range(8):
        bands.append(pltpu.roll(last_ref[...], 32 * r, 1) if r else last_ref[...])
    w_last_ref[...] = jnp.concatenate(bands, axis=0).astype(BF16)


def tables(w_first, w_middle, w_last):
    first = w_first.reshape(w_first.shape[0], 54)
    middle = jnp.transpose(w_middle, (0, 3, 4, 5, 1, 2))
    last = jnp.pad(jnp.transpose(w_last, (4, 0, 2, 3, 1)), ((0, 0), (0, 0), (0, 0), (0, 7), (0, 0)))
    last = jnp.pad(last.reshape(6, 960), ((0, 2), (0, 64))).astype(F32)
    return call(
        tables_kernel,
        (struct((512, 512), BF16), struct((3, 96 * GROUP, 512), BF16), struct((64, 1024), BF16)),
        (first, middle, last),
    )


def swap(blocks, axis):
    return lax.all_to_all(blocks, axis, 0, 0, tiled=True)


def near_planes(near):
    count = lax.axis_size("slab")

    def shifted(part, step):
        pairs = [(i, i + step) for i in range(count) if 0 <= i + step < count]
        return lax.ppermute(part, "slab", pairs)

    below = [shifted(near[1:], 3), shifted(near, 2), shifted(near, 1)]
    above = [shifted(near, -1), shifted(near, -2), shifted(near[:1], -3)]
    return below + [near] + above


def body(sensitivity, kspace, sampling, prior_image, w_first, w_middle, w_last):
    maps = sensitivity[0]
    len_y, len_z = maps.shape[2:]
    coils, slabs = lax.axis_size("coil"), lax.axis_size("slab")
    at = jnp.stack([lax.axis_index("coil"), lax.axis_index("slab")]).astype(jnp.int32)
    rows, columns = left_table(len_y), right_table(len_z)
    weights = tables(w_first, w_middle, w_last)

    term = call(adjoint_kernel, struct((coils, 64, 128)), (kspace[0], sampling, rows, columns, maps))
    rhs_rows, copies = call(
        rows_kernel, (struct((64, 128)), struct((coils, 64, 128))), (swap(term, "coil"), prior_image)
    )
    rhs = swap(copies, "coil")
    near_shape = struct((2, 2, 32, 128))
    term, spectrum, norms, rhs_near = call(
        normal_kernel,
        (struct((coils, 72, 128)), struct((2, 2, len_y, len_z)), struct((8, 128)), near_shape),
        (at, rhs, sampling, maps, rows, columns),
        in_smem=(0,),
    )
    rhs_parts = near_planes(rhs_near)
    copies, sums = call(
        image_kernel,
        (struct((coils, 64, 128)), struct((8, 128))),
        (swap(term, "coil"), rhs_rows, norms),
    )
    image = swap(copies, "coil")
    tiles, image_near = call(
        last_kernel,
        (struct((coils, 8, 128)), near_shape),
        (at, sums, image, rhs, spectrum, sampling, maps, rows, columns),
        in_smem=(0,),
    )
    image_parts = near_planes(image_near)
    tiles = call(spread_kernel, struct((slabs, 8, 128)), (swap(tiles, "coil"),))
    last = swap(tiles, "slab")
    scratch = [pltpu.VMEM((12, 144, 256), BF16)]
    scratch += [pltpu.VMEM((10 - 2 * m, (16 - 2 * m) * 32, 256), BF16) for m in range(4)]
    return call(
        functools.partial(denoise_kernel, coils, slabs),
        (struct(prior_image.shape), struct(prior_image.shape)),
        (at, last, *rhs_parts, *image_parts, *weights),
        scratch=scratch,
        in_smem=(0,),
    )


def solution(mesh):
    placed = (
        P("coil", None, "slab", None, None),
        P("coil", None, "slab", None, None),
        P("slab", None, None),
        P(None, "slab", "coil", None),
        P(),
        P(),
        P(),
    )
    return jax.shard_map(
        body,
        mesh=mesh,
        in_specs=placed,
        out_specs=(P(None, "slab", "coil", None), P(None, "slab", "coil", None)),
        check_vma=False,
    )
```

```python
import functools
import math

import jax
import jax.numpy as jnp
import numpy as np
from jax import lax
from jax.experimental import pallas as pl
from jax.experimental.pallas import tpu as pltpu
from jax.sharding import PartitionSpec as P

LAMBDA = 0.5
HALO = 5
SIDE = 8
GROUP = 2
F32 = jnp.float32
BF16 = jnp.bfloat16
VMEM_BYTES = 20 * 1024 * 1024


def call(kernel, out_shape, args, scratch=(), in_smem=(), after=()):
    specs = [
        pl.BlockSpec(memory_space=pltpu.SMEM if i in in_smem else pltpu.VMEM) for i in range(len(args))
    ]
    specs += [pl.BlockSpec(memory_space=pl.ANY)] * len(after)
    if after:
        inner_kernel, count = kernel, len(args)

        def kernel(*refs):
            inner_kernel(*refs[:count], *refs[count + len(after) :])

    outs = jax.tree.map(lambda _: pl.BlockSpec(memory_space=pltpu.VMEM), out_shape)
    return pl.pallas_call(
        kernel,
        out_shape=out_shape,
        in_specs=specs,
        out_specs=outs,
        scratch_shapes=list(scratch),
        compiler_params=pltpu.CompilerParams(vmem_limit_bytes=VMEM_BYTES),
    )(*args, *after)


def struct(shape, dtype=F32):
    return jax.ShapeDtypeStruct(shape, dtype)


def halves(table):
    high = table.astype(np.float32).astype(jnp.bfloat16)
    low = (table.astype(np.float32) - high.astype(np.float32)).astype(jnp.bfloat16)
    return high, low


def dft_pair(length):
    positions = np.arange(length)
    angles = 2.0 * math.pi / length * (positions[:, None] * positions[None, :] % length)
    scaling = 1.0 / math.sqrt(length)
    return np.cos(angles) * scaling, scaling * np.sin(angles)


def left_table(length):
    cosine, sine = dft_pair(length)
    parts = [np.concatenate(halves(part), axis=1) for part in (cosine, sine)]
    return np.concatenate(parts, axis=0)


def right_table(length):
    cosine, sine = dft_pair(length)
    return np.concatenate(halves(cosine) + halves(sine), axis=1)


def split(values):
    high = values.astype(BF16)
    low = (values - high.astype(F32)).astype(BF16)
    return high, low


def dft_rows(field, table_ref, sign):
    values = jnp.concatenate(field[0] + field[1], axis=1)
    high, low = split(values)
    size = values.shape[0]
    table_high, table_low = table_ref[:, :size], table_ref[:, size:]
    table = jnp.concatenate([table_high, table_high, table_low], axis=1)
    products = jnp.dot(table, jnp.concatenate([high, low, high], axis=0), preferred_element_type=F32)
    half = values.shape[1] // 2
    cosine, sine = products[:size], products[size:]
    real = cosine[:, :half] - sign * sine[:, half:]
    imag = cosine[:, half:] + sign * sine[:, :half]
    columns = half // 2
    return [[part[:, p * columns : (p + 1) * columns] for p in range(2)] for part in (real, imag)]


def dft_columns(field, table_ref, sign):
    values = by_columns(field)
    high, low = split(values)
    size = table_ref.shape[0]
    cosine_high, cosine_low, sine_high, sine_low = [table_ref[:, i * size : (i + 1) * size] for i in range(4)]

    def block(cosine, sine):
        plus, minus = (sine, -sine) if sign > 0 else (-sine, sine)
        return jnp.concatenate(
            [jnp.concatenate([cosine, plus], axis=1), jnp.concatenate([minus, cosine], axis=1)], axis=0
        )

    table_high = block(cosine_high, sine_high)
    table = jnp.concatenate([table_high, table_high, block(cosine_low, sine_low)], axis=0)
    return from_columns(jnp.dot(jnp.concatenate([high, low, high], axis=1), table, preferred_element_type=F32))


def by_columns(field):
    planes = range(len(field[0]))
    return jnp.concatenate([jnp.concatenate([field[0][p], field[1][p]], axis=1) for p in planes], axis=0)


def from_columns(values):
    rows, columns = values.shape[0] // 2, values.shape[1] // 2
    return [[values[p * rows : (p + 1) * rows, a * columns : (a + 1) * columns] for p in range(2)] for a in range(2)]


def load_image(blocks_ref):
    count, _, columns = blocks_ref.shape
    rows = 16

    def one(a, p):
        start = (2 * a + p) * rows
        return blocks_ref[:, start : start + rows, :].reshape(count * rows, columns)

    return [[one(a, p) for p in range(2)] for a in range(2)]


def store_image(blocks_ref, image):
    count, _, columns = blocks_ref.shape
    rows = 16
    for a in range(2):
        for p in range(2):
            start = (2 * a + p) * rows
            blocks_ref[:, start : start + rows, :] = image[a][p].reshape(count, rows, columns)


def coil_field(maps_ref, image):
    real = [maps_ref[0, p] * image[0][p] - maps_ref[1, p] * image[1][p] for p in range(2)]
    imag = [maps_ref[0, p] * image[1][p] + maps_ref[1, p] * image[0][p] for p in range(2)]
    return [real, imag]


def coil_term(maps_ref, field):
    real = [maps_ref[0, p] * field[0][p] + maps_ref[1, p] * field[1][p] for p in range(2)]
    imag = [maps_ref[0, p] * field[1][p] - maps_ref[1, p] * field[0][p] for p in range(2)]
    return [real, imag]


def masked(field, mask_ref):
    masks = [mask_ref[p].astype(F32) for p in range(2)]
    return [[field[a][p] * masks[p] for p in range(2)] for a in range(2)]


def inner(first, second):
    return sum(row_sum(first[a][p] * second[a][p]) for a in range(2) for p in range(2))


def row_sum(values):
    folded = jnp.sum(values.reshape(-1, 8, values.shape[-1]), axis=0)
    folded = jnp.sum(folded, axis=0, keepdims=True)
    return folded


def tile_of(rows):
    blank = jnp.zeros((1, 128), F32)
    return jnp.concatenate(list(rows) + [blank] * (8 - len(rows)), axis=0)


def store_near(near_ref, blocks_ref, at):
    count = blocks_ref.shape[0]
    for a in range(2):
        for p in range(2):
            start = (2 * a + p) * 16
            near_ref[p, a, 8:24, :] = blocks_ref[at, start : start + 16, :]
            before = blocks_ref[jnp.maximum(at - 1, 0), start + 8 : start + 16, :]
            after = blocks_ref[jnp.minimum(at + 1, count - 1), start : start + 8, :]
            near_ref[p, a, 0:8, :] = jnp.where(at > 0, before, 0.0)
            near_ref[p, a, 24:32, :] = jnp.where(at < count - 1, after, 0.0)


def adjoint_kernel(
    mask_hbm, kspace_hbm, rows_hbm, columns_hbm, maps_hbm, out_ref, mask_ref, kspace_ref, rows_ref, columns_ref, maps_ref, sems
):
    sources = (mask_hbm, kspace_hbm, rows_hbm, columns_hbm, maps_hbm)
    targets = (mask_ref, kspace_ref, rows_ref, columns_ref, maps_ref)
    copies = [pltpu.make_async_copy(src, dst, sems.at[i]) for i, (src, dst) in enumerate(zip(sources, targets))]
    for copy in copies:
        copy.start()
    for copy in copies[:3]:
        copy.wait()
    field = masked([[kspace_ref[a, p] for p in range(2)] for a in range(2)], mask_ref)
    field = dft_rows(field, rows_ref, 1.0)
    copies[3].wait()
    field = dft_columns(field, columns_ref, 1.0)
    copies[4].wait()
    store_image(out_ref, coil_term(maps_ref, field))


def adjoint(mask, kspace, rows, columns, maps, coils):
    args = (mask, kspace, rows, columns, maps)
    return pl.pallas_call(
        adjoint_kernel,
        out_shape=struct((coils, 64, 128)),
        in_specs=[pl.BlockSpec(memory_space=pl.ANY)] * len(args),
        out_specs=pl.BlockSpec(memory_space=pltpu.VMEM),
        scratch_shapes=[pltpu.VMEM(arg.shape, arg.dtype) for arg in args] + [pltpu.SemaphoreType.DMA((len(args),))],
        compiler_params=pltpu.CompilerParams(vmem_limit_bytes=60 * 1024 * 1024),
    )(*args)


def rows_kernel(blocks_ref, prior_ref, rows_ref, copies_ref):
    count = blocks_ref.shape[0]
    total = jnp.sum(blocks_ref[...], axis=0)
    prior = jnp.concatenate([prior_ref[a, p] for a in range(2) for p in range(2)], axis=0)
    total = total + LAMBDA * prior
    rows_ref[...] = total
    for k in range(count):
        copies_ref[k] = total


def normal_kernel(
    at_ref, blocks_ref, mask_ref, maps_ref, rows_ref, columns_ref, out_ref, spectrum_ref, tile_ref, near_ref
):
    store_near(near_ref, blocks_ref, at_ref[0])
    image = load_image(blocks_ref)
    field = dft_columns(coil_field(maps_ref, image), columns_ref, -1.0)
    spectrum = masked(dft_rows(field, rows_ref, -1.0), mask_ref)
    for a in range(2):
        for p in range(2):
            spectrum_ref[a, p] = spectrum[a][p]
    field = dft_columns(dft_rows(spectrum, rows_ref, 1.0), columns_ref, 1.0)
    store_image(out_ref, coil_term(maps_ref, field))
    tile_ref[...] = tile_of([inner(image, image)])
    energies = tile_of([inner(spectrum, spectrum)])
    for k in range(blocks_ref.shape[0]):
        out_ref[k, 64:72, :] = energies


def image_kernel(blocks_ref, rhs_rows_ref, norms_ref, copies_ref, sums_ref):
    total = jnp.sum(blocks_ref[...], axis=0)
    rows = total[:64] + LAMBDA * rhs_rows_ref[...]
    for k in range(blocks_ref.shape[0]):
        copies_ref[k] = rows
    sums_ref[...] = tile_of([norms_ref[0:1, :], total[64:65]])


def lane_sum(values):
    return jnp.sum(values, axis=-1, keepdims=True)


def slab_step(norm, energy):
    curved = energy + LAMBDA * norm
    return jnp.where(curved > 0.0, norm / jnp.where(curved > 0.0, curved, 1.0), 1.0)


def last_kernel(
    at_ref, sums_ref, blocks_ref, rhs_ref, spectrum_ref, mask_ref, maps_ref, rows_ref, columns_ref, out_ref, near_ref
):
    store_near(near_ref, blocks_ref, at_ref[0])
    norm, energy = sums_ref[0:1, :], sums_ref[1:2, :]
    step = slab_step(lane_sum(norm), lane_sum(energy))
    image = load_image(blocks_ref)
    rhs = load_image(rhs_ref)
    field = dft_columns(coil_field(maps_ref, image), columns_ref, -1.0)
    spectrum = masked(dft_rows(field, rows_ref, -1.0), mask_ref)
    before = [[spectrum_ref[a, p] for p in range(2)] for a in range(2)]
    residual = [[rhs[a][p] - step * image[a][p] for p in range(2)] for a in range(2)]
    spectrum = [[before[a][p] - step * spectrum[a][p] for p in range(2)] for a in range(2)]
    share = 1.0 / out_ref.shape[0]
    local = [inner(residual, residual), inner(residual, rhs), norm, energy]
    tile = tile_of([inner(spectrum, spectrum), inner(spectrum, before)] + [share * value for value in local])
    for k in range(out_ref.shape[0]):
        out_ref[k] = tile


def spread_kernel(tiles_ref, out_ref):
    total = jnp.sum(tiles_ref[...], axis=0)
    for k in range(out_ref.shape[0]):
        out_ref[k] = total


def final_scales(tiles_ref):
    curve, curve_cross, norm, cross, norm_first, energy_first = [
        lane_sum(tiles_ref[:, i, :]) for i in range(6)
    ]

    def over_slabs(values):
        return jnp.sum(values, axis=0, keepdims=True)

    all_norm, all_energy = over_slabs(norm_first), over_slabs(energy_first)
    step_first = all_norm / (all_energy + LAMBDA * all_norm)
    here = step_first / slab_step(norm_first, energy_first)
    rest = 1.0 - here
    curve = over_slabs(here * here * curve + rest * (2.0 * here * curve_cross + rest * energy_first))
    curve_cross = over_slabs(here * curve_cross + rest * energy_first)
    norm = over_slabs(here * here * norm + rest * (2.0 * here * cross + rest * norm_first))
    cross = over_slabs(here * cross + rest * norm_first)
    ratio = norm / all_norm
    curvature = curve + ratio * (2.0 * curve_cross + ratio * all_energy)
    curvature = curvature + LAMBDA * (norm + ratio * (2.0 * cross + ratio * all_norm))
    return step_first, norm / curvature, ratio


def starts_of(rows):
    starts = list(range(0, rows - GROUP + 1, GROUP))
    if starts[-1] + GROUP < rows:
        starts.append(rows - GROUP)
    return starts


def shifted_sum(parts):
    before, here, after = parts
    lane = lax.broadcasted_iota(jnp.int32, before.shape[:1] + (128,), 1)
    outs = []
    for h in range(2):
        cut = slice(128 * h, 128 * (h + 1))
        low = jnp.where(lane > 0, pltpu.roll(before[:, cut], 1, 1), 0.0)
        high = jnp.where(lane < 127, pltpu.roll(after[:, cut], 127, 1), 0.0)
        outs.append(here[:, cut] + low + high)
    return jnp.concatenate(outs, axis=1)


def denoise_kernel(coil_count, slab_count, *refs):
    at_ref, last_ref = refs[:2]
    rhs_refs = refs[2:9]
    image_refs = refs[9:16]
    w_first_ref, w_middle_ref, w_last_ref, solution_ref, refined_ref = refs[16:21]
    features_ref = refs[21]
    hidden_refs = refs[22:]
    coil_at = at_ref[0]
    slab_at = at_ref[1]

    step_first, step_last, ratio = final_scales(last_ref)
    scale_rhs = step_first + step_last * ratio

    lane = lax.broadcasted_iota(jnp.int32, (48, 128), 1)
    plane = 0
    brick = None
    for rhs_ref, image_ref in zip(rhs_refs, image_refs):
        for p in range(rhs_ref.shape[0]):
            full = []
            for a in range(2):
                rhs = rhs_ref[p, a]
                full.append(scale_rhs * rhs + step_last * (rhs - step_first * image_ref[p, a]))
            if 5 <= plane < 7:
                for a in range(2):
                    solution_ref[a, plane - 5] = full[a][8:24]
            for h in range(2):
                window = jnp.concatenate([f[8 * h : 8 * h + 24] for f in full], axis=0)
                cut = slice(128 * h, 128 * (h + 1))
                low = jnp.where(lane > 0, pltpu.roll(window, 1, 1), 0.0)
                high = jnp.where(lane < 127, pltpu.roll(window, 127, 1), 0.0)
                features_ref[plane, 0:48, cut] = low.astype(BF16)
                features_ref[plane, 48:96, cut] = window.astype(BF16)
                features_ref[plane, 96:144, cut] = high.astype(BF16)
            plane += 1

    def outside(out_ref, depth):
        planes, cells, _ = out_ref.shape
        extra = 4 - depth
        first = 2 * slab_at - extra

        last_plane = 2 * slab_at + 1 + extra
        edge = (coil_at == 0) | (coil_at == coil_count - 1) | (first < 0) | (last_plane >= 2 * slab_count)

        @pl.when(edge)
        def _():
            blank = jnp.zeros((planes, extra * 32, 128), BF16)

            @pl.when(coil_at == 0)
            def _():
                out_ref[:, 0 : extra * 32, 0:128] = blank

            @pl.when(coil_at == coil_count - 1)
            def _():
                out_ref[:, cells - extra * 32 : cells, 128:256] = blank

            for p in list(range(extra)) + list(range(planes - extra, planes)):

                @pl.when((first + p < 0) | (first + p >= 2 * slab_count))
                def _():
                    out_ref[p] = jnp.zeros(out_ref.shape[1:], BF16)

    first_out = hidden_refs[0]

    for p in range(first_out.shape[0]):
        taps = jnp.concatenate([features_ref[p + u] for u in range(3)], axis=0)
        values = jnp.dot(w_first_ref[:, :432], taps, preferred_element_type=F32)
        first_out[p] = jnp.maximum(values, 0.0).astype(BF16)
    outside(first_out, 0)

    for m in range(len(hidden_refs) - 1):
        in_ref, out_ref = hidden_refs[m], hidden_refs[m + 1]
        starts = starts_of(out_ref.shape[1] // 32)

        cells = GROUP * 32
        for p in range(out_ref.shape[0]):
            for start in starts:
                rows = slice(start * 32, (start + GROUP + 2) * 32)
                taps = jnp.concatenate([in_ref[p + u, rows] for u in range(3)], axis=0)
                sums = jnp.dot(w_middle_ref[m, :, : (GROUP + 2) * 96], taps, preferred_element_type=F32)
                values = shifted_sum([sums[t * cells : (t + 1) * cells] for t in range(3)])
                out_ref[p, start * 32 : start * 32 + cells] = jnp.maximum(values, 0.0).astype(BF16)
        outside(out_ref, m + 1)

    in_ref = hidden_refs[-1]
    for p in range(2):
        taps = jnp.concatenate([in_ref[p + u] for u in range(3)], axis=0)
        sums = jnp.dot(w_last_ref[:, :960], taps, preferred_element_type=F32)
        lane = lax.broadcasted_iota(jnp.int32, (64, 128), 1)
        for h in range(2):
            part = sums[:, 128 * h : 128 * (h + 1)]
            low = jnp.where(lane > 0, pltpu.roll(part, 1, 1), 0.0)
            high = jnp.where(lane < 127, pltpu.roll(part, 127, 1), 0.0)
            for a in range(2):
                rows = []
                for r in range(8):
                    at = 8 * r + a
                    rows.append(low[at : at + 1] + part[at + 2 : at + 3] + high[at + 4 : at + 5])
                piece = jnp.concatenate(rows, axis=0)
                refined_ref[a, p, 8 * h : 8 * h + 8] = solution_ref[a, p, 8 * h : 8 * h + 8] + piece


def tables_kernel(first_ref, middle_ref, last_ref, w_first_ref, w_middle_ref, w_last_ref):
    def spots(size, target, count=512):
        column = lax.broadcasted_iota(jnp.int32, (size, count), 1)
        return jnp.where(column == target(lax.broadcasted_iota(jnp.int32, (size, count), 0)), 1.0, 0.0).astype(BF16)

    def first_target(source):
        channel, u, v, t = source // 27, source // 9 % 3, source // 3 % 3, source % 3
        return ((u * 3 + t) * 2 + channel) * 24 + SIDE - HALO + v

    base = jnp.dot(first_ref[...], spots(54, first_target), preferred_element_type=F32)
    for r in range(16):
        w_first_ref[32 * r : 32 * r + 32] = (pltpu.roll(base, r, 1) if r else base).astype(BF16)
    for m in range(middle_ref.shape[0]):
        base = jnp.zeros((96, 512), F32)
        for u in range(3):
            for v in range(3):
                place = spots(32, lambda source: source + (u * (GROUP + 2) + v) * 32)
                taps = jnp.concatenate([middle_ref[m, u, v, t] for t in range(3)], axis=0)
                base = base + jnp.dot(taps, place, preferred_element_type=F32)
        for r in range(GROUP):
            band = (pltpu.roll(base, 32 * r, 1) if r else base).astype(BF16)
            for t in range(3):
                start = (t * GROUP + r) * 32
                w_middle_ref[m, start : start + 32] = band[32 * t : 32 * t + 32]
    bands = []
    for r in range(8):
        bands.append(pltpu.roll(last_ref[...], 32 * r, 1) if r else last_ref[...])
    w_last_ref[...] = jnp.concatenate(bands, axis=0).astype(BF16)


def tables(w_first, w_middle, w_last):
    first = w_first.reshape(w_first.shape[0], 54)
    middle = jnp.transpose(w_middle, (0, 3, 4, 5, 1, 2))
    last = jnp.pad(jnp.transpose(w_last, (4, 0, 2, 3, 1)), ((0, 0), (0, 0), (0, 0), (0, 7), (0, 0)))
    last = jnp.pad(last.reshape(6, 960), ((0, 2), (0, 64))).astype(F32)
    return call(
        tables_kernel,
        (struct((512, 512), BF16), struct((3, 96 * GROUP, 512), BF16), struct((64, 1024), BF16)),
        (first, middle, last),
    )


def swap(blocks, axis):
    return lax.all_to_all(blocks, axis, 0, 0, tiled=True)


def near_planes(near):
    count = lax.axis_size("slab")

    def shifted(part, step):
        pairs = [(i, i + step) for i in range(count) if 0 <= i + step < count]
        return lax.ppermute(part, "slab", pairs)

    below = [shifted(near[1:], 3), shifted(near, 2), shifted(near, 1)]
    above = [shifted(near, -1), shifted(near, -2), shifted(near[:1], -3)]
    return below + [near] + above


def body(sensitivity, kspace, sampling, prior_image, w_first, w_middle, w_last):
    maps = sensitivity[0]
    len_y, len_z = maps.shape[2:]
    coils, slabs = lax.axis_size("coil"), lax.axis_size("slab")
    at = jnp.stack([lax.axis_index("coil"), lax.axis_index("slab")]).astype(jnp.int32)
    rows, columns = left_table(len_y), right_table(len_z)
    weights = tables(w_first, w_middle, w_last)

    term = adjoint(sampling, kspace[0], rows, columns, maps, coils)
    rhs_rows, copies = call(
        rows_kernel,
        (struct((64, 128)), struct((coils, 64, 128))),
        (swap(term, "coil"), prior_image),
        after=(),
    )
    rhs = swap(copies, "coil")
    near_shape = struct((2, 2, 32, 128))
    term, spectrum, norms, rhs_near = call(
        normal_kernel,
        (struct((coils, 72, 128)), struct((2, 2, len_y, len_z)), struct((8, 128)), near_shape),
        (at, rhs, sampling, maps, rows, columns),
        in_smem=(0,),
    )
    rhs_parts = near_planes(rhs_near)
    copies, sums = call(
        image_kernel,
        (struct((coils, 64, 128)), struct((8, 128))),
        (swap(term, "coil"), rhs_rows, norms),
        after=rhs_parts,
    )
    image = swap(copies, "coil")
    tiles, image_near = call(
        last_kernel,
        (struct((coils, 8, 128)), near_shape),
        (at, sums, image, rhs, spectrum, sampling, maps, rows, columns),
        in_smem=(0,),
    )
    image_parts = near_planes(image_near)
    tiles = call(spread_kernel, struct((slabs, 8, 128)), (swap(tiles, "coil"),), after=image_parts[:4])
    last = swap(tiles, "slab")
    scratch = [pltpu.VMEM((12, 144, 256), BF16)]
    scratch += [pltpu.VMEM((10 - 2 * m, (16 - 2 * m) * 32, 256), BF16) for m in range(4)]
    return call(
        functools.partial(denoise_kernel, coils, slabs),
        (struct(prior_image.shape), struct(prior_image.shape)),
        (at, last, *rhs_parts, *image_parts, *weights),
        scratch=scratch,
        in_smem=(0,),
    )


def solution(mesh):
    placed = (
        P("coil", None, "slab", None, None),
        P("coil", None, "slab", None, None),
        P("slab", None, None),
        P(None, "slab", "coil", None),
        P(),
        P(),
        P(),
    )
    return jax.shard_map(
        body,
        mesh=mesh,
        in_specs=placed,
        out_specs=(P(None, "slab", "coil", None), P(None, "slab", "coil", None)),
        check_vma=False,
    )
```

```python
import functools
import math

import jax
import jax.numpy as jnp
import numpy as np
from jax import lax
from jax.experimental import pallas as pl
from jax.experimental.pallas import tpu as pltpu
from jax.sharding import PartitionSpec as P

LAMBDA = 0.5
HALO = 5
SIDE = 8
GROUP = 2
AHEAD = 3
F32 = jnp.float32
BF16 = jnp.bfloat16
VMEM_BYTES = 20 * 1024 * 1024


def call(kernel, out_shape, args, scratch=(), in_smem=(), after=()):
    specs = [
        pl.BlockSpec(memory_space=pltpu.SMEM if i in in_smem else pltpu.VMEM) for i in range(len(args))
    ]
    specs += [pl.BlockSpec(memory_space=pl.ANY)] * len(after)
    if after:
        inner_kernel, count = kernel, len(args)

        def kernel(*refs):
            inner_kernel(*refs[:count], *refs[count + len(after) :])

    outs = jax.tree.map(lambda _: pl.BlockSpec(memory_space=pltpu.VMEM), out_shape)
    return pl.pallas_call(
        kernel,
        out_shape=out_shape,
        in_specs=specs,
        out_specs=outs,
        scratch_shapes=list(scratch),
        compiler_params=pltpu.CompilerParams(vmem_limit_bytes=VMEM_BYTES),
    )(*args, *after)


def struct(shape, dtype=F32):
    return jax.ShapeDtypeStruct(shape, dtype)


def halves(table):
    high = table.astype(np.float32).astype(jnp.bfloat16)
    low = (table.astype(np.float32) - high.astype(np.float32)).astype(jnp.bfloat16)
    return high, low


def dft_pair(length):
    positions = np.arange(length)
    angles = 2.0 * math.pi / length * (positions[:, None] * positions[None, :] % length)
    scaling = 1.0 / math.sqrt(length)
    return np.cos(angles) * scaling, scaling * np.sin(angles)


def left_table(length):
    cosine, sine = dft_pair(length)
    parts = [np.concatenate(halves(part), axis=1) for part in (cosine, sine)]
    return np.concatenate(parts, axis=0)


def right_table(length):
    cosine, sine = dft_pair(length)
    return np.concatenate(halves(cosine) + halves(sine), axis=1)


def split(values):
    high = values.astype(BF16)
    low = (values - high.astype(F32)).astype(BF16)
    return high, low


def dft_rows(field, table_ref, sign):
    values = jnp.concatenate(field[0] + field[1], axis=1)
    high, low = split(values)
    size = values.shape[0]
    table_high, table_low = table_ref[:, :size], table_ref[:, size:]
    table = jnp.concatenate([table_high, table_high, table_low], axis=1)
    products = jnp.dot(table, jnp.concatenate([high, low, high], axis=0), preferred_element_type=F32)
    half = values.shape[1] // 2
    cosine, sine = products[:size], products[size:]
    real = cosine[:, :half] - sign * sine[:, half:]
    imag = cosine[:, half:] + sign * sine[:, :half]
    columns = half // 2
    return [[part[:, p * columns : (p + 1) * columns] for p in range(2)] for part in (real, imag)]


def dft_columns(field, table_ref, sign):
    values = by_columns(field)
    high, low = split(values)
    size = table_ref.shape[0]
    cosine_high, cosine_low, sine_high, sine_low = [table_ref[:, i * size : (i + 1) * size] for i in range(4)]

    def block(cosine, sine):
        plus, minus = (sine, -sine) if sign > 0 else (-sine, sine)
        return jnp.concatenate(
            [jnp.concatenate([cosine, plus], axis=1), jnp.concatenate([minus, cosine], axis=1)], axis=0
        )

    table_high = block(cosine_high, sine_high)
    table = jnp.concatenate([table_high, table_high, block(cosine_low, sine_low)], axis=0)
    return from_columns(jnp.dot(jnp.concatenate([high, low, high], axis=1), table, preferred_element_type=F32))


def by_columns(field):
    planes = range(len(field[0]))
    return jnp.concatenate([jnp.concatenate([field[0][p], field[1][p]], axis=1) for p in planes], axis=0)


def from_columns(values):
    rows, columns = values.shape[0] // 2, values.shape[1] // 2
    return [[values[p * rows : (p + 1) * rows, a * columns : (a + 1) * columns] for p in range(2)] for a in range(2)]


def load_image(blocks_ref):
    count, _, columns = blocks_ref.shape
    rows = 16

    def one(a, p):
        start = (2 * a + p) * rows
        return blocks_ref[:, start : start + rows, :].astype(F32).reshape(count * rows, columns)

    return [[one(a, p) for p in range(2)] for a in range(2)]


def store_image(blocks_ref, image):
    count, _, columns = blocks_ref.shape
    rows = 16
    for a in range(2):
        for p in range(2):
            start = (2 * a + p) * rows
            blocks_ref[:, start : start + rows, :] = image[a][p].reshape(count, rows, columns)


def coil_field(maps_ref, image):
    real = [maps_ref[0, p] * image[0][p] - maps_ref[1, p] * image[1][p] for p in range(2)]
    imag = [maps_ref[0, p] * image[1][p] + maps_ref[1, p] * image[0][p] for p in range(2)]
    return [real, imag]


def coil_term(maps_ref, field):
    real = [maps_ref[0, p] * field[0][p] + maps_ref[1, p] * field[1][p] for p in range(2)]
    imag = [maps_ref[0, p] * field[1][p] - maps_ref[1, p] * field[0][p] for p in range(2)]
    return [real, imag]


def masked(field, mask_ref):
    masks = [mask_ref[p].astype(F32) for p in range(2)]
    return [[field[a][p] * masks[p] for p in range(2)] for a in range(2)]


def inner(first, second):
    return sum(row_sum(first[a][p] * second[a][p]) for a in range(2) for p in range(2))


def row_sum(values):
    folded = jnp.sum(values.reshape(-1, 8, values.shape[-1]), axis=0)
    folded = jnp.sum(folded, axis=0, keepdims=True)
    return folded


def tile_of(rows):
    blank = jnp.zeros((1, 128), F32)
    return jnp.concatenate(list(rows) + [blank] * (8 - len(rows)), axis=0)


def store_near(near_ref, blocks_ref, at):
    count = blocks_ref.shape[0]
    for a in range(2):
        for p in range(2):
            start = (2 * a + p) * 16
            near_ref[p, a, 8:24, :] = blocks_ref[at, start : start + 16, :]
            before = blocks_ref[jnp.maximum(at - 1, 0), start + 8 : start + 16, :]
            after = blocks_ref[jnp.minimum(at + 1, count - 1), start : start + 8, :]
            near_ref[p, a, 0:8, :] = jnp.where(at > 0, before, 0.0)
            near_ref[p, a, 24:32, :] = jnp.where(at < count - 1, after, 0.0)


def adjoint_kernel(
    mask_hbm, kspace_hbm, rows_hbm, columns_hbm, maps_hbm, out_ref, mask_ref, kspace_ref, rows_ref, columns_ref, maps_ref, sems
):
    sources = (mask_hbm, kspace_hbm, rows_hbm, columns_hbm, maps_hbm)
    targets = (mask_ref, kspace_ref, rows_ref, columns_ref, maps_ref)
    copies = [pltpu.make_async_copy(src, dst, sems.at[i]) for i, (src, dst) in enumerate(zip(sources, targets))]
    for copy in copies:
        copy.start()
    for copy in copies[:3]:
        copy.wait()
    field = masked([[kspace_ref[a, p] for p in range(2)] for a in range(2)], mask_ref)
    field = dft_rows(field, rows_ref, 1.0)
    copies[3].wait()
    field = dft_columns(field, columns_ref, 1.0)
    copies[4].wait()
    store_image(out_ref, coil_term(maps_ref, field))


def adjoint(mask, kspace, rows, columns, maps, coils):
    args = (mask, kspace, rows, columns, maps)
    return pl.pallas_call(
        adjoint_kernel,
        out_shape=struct((coils, 64, 128)),
        in_specs=[pl.BlockSpec(memory_space=pl.ANY)] * len(args),
        out_specs=pl.BlockSpec(memory_space=pltpu.VMEM),
        scratch_shapes=[pltpu.VMEM(arg.shape, arg.dtype) for arg in args] + [pltpu.SemaphoreType.DMA((len(args),))],
        compiler_params=pltpu.CompilerParams(vmem_limit_bytes=60 * 1024 * 1024),
    )(*args)


def rows_kernel(blocks_ref, prior_ref, rows_ref, copies_ref):
    count = blocks_ref.shape[0]
    total = jnp.sum(blocks_ref[...], axis=0)
    prior = jnp.concatenate([prior_ref[a, p] for a in range(2) for p in range(2)], axis=0)
    total = total + LAMBDA * prior
    rows_ref[...] = total
    for k in range(count):
        copies_ref[k] = total


def normal_kernel(
    at_ref, blocks_ref, mask_ref, maps_ref, rows_ref, columns_ref, out_ref, spectrum_ref, tile_ref, near_ref
):
    store_near(near_ref, blocks_ref, at_ref[0])
    image = load_image(blocks_ref)
    field = dft_columns(coil_field(maps_ref, image), columns_ref, -1.0)
    spectrum = masked(dft_rows(field, rows_ref, -1.0), mask_ref)
    for a in range(2):
        for p in range(2):
            spectrum_ref[a, p] = spectrum[a][p]
    field = dft_columns(dft_rows(spectrum, rows_ref, 1.0), columns_ref, 1.0)
    store_image(out_ref, coil_term(maps_ref, field))
    tile_ref[...] = tile_of([inner(image, image)])
    energies = tile_of([inner(spectrum, spectrum)])
    for k in range(blocks_ref.shape[0]):
        out_ref[k, 64:72, :] = energies


def lane_sum(values):
    return jnp.sum(values, axis=-1, keepdims=True)


def slab_step(norm, energy):
    curved = energy + LAMBDA * norm
    return jnp.where(curved > 0.0, norm / jnp.where(curved > 0.0, curved, 1.0), 1.0)


def image_kernel(blocks_ref, rhs_rows_ref, norms_ref, copies_ref, rows_ref, sums_ref):
    total = jnp.sum(blocks_ref[...], axis=0)
    rhs = rhs_rows_ref[...]
    image = total[:64] + LAMBDA * rhs
    norm, energy = norms_ref[0:1, :], total[64:65]
    residual = rhs - slab_step(lane_sum(norm), lane_sum(energy)) * image
    for a in range(2):
        for p in range(2):
            rows_ref[p, a] = image[(2 * a + p) * 16 : (2 * a + p + 1) * 16]
    rounded = residual.astype(BF16)
    for k in range(blocks_ref.shape[0]):
        copies_ref[k] = rounded
    share = 1.0 / blocks_ref.shape[0]
    sums_ref[...] = tile_of([row_sum(residual * residual), row_sum(residual * rhs), share * norm, share * energy])


def last_kernel(sums_ref, blocks_ref, spectrum_ref, mask_ref, maps_ref, rows_ref, columns_ref, out_ref):
    field = dft_columns(coil_field(maps_ref, load_image(blocks_ref)), columns_ref, -1.0)
    spectrum = masked(dft_rows(field, rows_ref, -1.0), mask_ref)
    before = [[spectrum_ref[a, p] for p in range(2)] for a in range(2)]
    tile = tile_of([inner(spectrum, spectrum), inner(spectrum, before)] + [sums_ref[i : i + 1, :] for i in range(4)])
    for k in range(out_ref.shape[0]):
        out_ref[k] = tile


def spread_kernel(tiles_ref, out_ref):
    total = jnp.sum(tiles_ref[...], axis=0)
    for k in range(out_ref.shape[0]):
        out_ref[k] = total


def final_scales(tiles_ref):
    curve, curve_cross, norm, cross, norm_first, energy_first = [
        lane_sum(tiles_ref[:, i, :]) for i in range(6)
    ]

    def over_slabs(values):
        return jnp.sum(values, axis=0, keepdims=True)

    all_norm, all_energy = over_slabs(norm_first), over_slabs(energy_first)
    step_first = all_norm / (all_energy + LAMBDA * all_norm)
    here = step_first / slab_step(norm_first, energy_first)
    rest = 1.0 - here
    curve = over_slabs(here * here * curve + rest * (2.0 * here * curve_cross + rest * energy_first))
    curve_cross = over_slabs(here * curve_cross + rest * energy_first)
    norm = over_slabs(here * here * norm + rest * (2.0 * here * cross + rest * norm_first))
    cross = over_slabs(here * cross + rest * norm_first)
    ratio = norm / all_norm
    curvature = curve + ratio * (2.0 * curve_cross + ratio * all_energy)
    curvature = curvature + LAMBDA * (norm + ratio * (2.0 * cross + ratio * all_norm))
    return step_first, norm / curvature, ratio


def starts_of(rows):
    starts = list(range(0, rows - GROUP + 1, GROUP))
    if starts[-1] + GROUP < rows:
        starts.append(rows - GROUP)
    return starts


def shifted_sum(parts):
    before, here, after = parts
    lane = lax.broadcasted_iota(jnp.int32, before.shape[:1] + (128,), 1)
    outs = []
    for h in range(2):
        cut = slice(128 * h, 128 * (h + 1))
        low = jnp.where(lane > 0, pltpu.roll(before[:, cut], 1, 1), 0.0)
        high = jnp.where(lane < 127, pltpu.roll(after[:, cut], 127, 1), 0.0)
        outs.append(here[:, cut] + low + high)
    return jnp.concatenate(outs, axis=1)


def denoise_kernel(coil_count, slab_count, *refs):
    at_ref, last_ref = refs[:2]
    rhs_refs = refs[2:9]
    image_refs = refs[9:16]
    w_first_ref, w_middle_ref, w_last_ref, solution_ref, refined_ref = refs[16:21]
    features_ref = refs[21]
    hidden_refs = refs[22:]
    coil_at = at_ref[0]
    slab_at = at_ref[1]

    step_first, step_last, ratio = final_scales(last_ref)
    scale_rhs = step_first + step_last * ratio

    lane = lax.broadcasted_iota(jnp.int32, (48, 128), 1)
    plane = 0
    brick = None
    for rhs_ref, image_ref in zip(rhs_refs, image_refs):
        for p in range(rhs_ref.shape[0]):
            full = []
            for a in range(2):
                rhs = rhs_ref[p, a]
                full.append(scale_rhs * rhs + step_last * (rhs - step_first * image_ref[p, a]))
            if 5 <= plane < 7:
                for a in range(2):
                    solution_ref[a, plane - 5] = full[a][8:24]
            for h in range(2):
                window = jnp.concatenate([f[8 * h : 8 * h + 24] for f in full], axis=0)
                cut = slice(128 * h, 128 * (h + 1))
                low = jnp.where(lane > 0, pltpu.roll(window, 1, 1), 0.0)
                high = jnp.where(lane < 127, pltpu.roll(window, 127, 1), 0.0)
                features_ref[plane, 0:48, cut] = low.astype(BF16)
                features_ref[plane, 48:96, cut] = window.astype(BF16)
                features_ref[plane, 96:144, cut] = high.astype(BF16)
            plane += 1

    def outside(out_ref, depth):
        planes, cells, _ = out_ref.shape
        extra = 4 - depth
        first = 2 * slab_at - extra

        last_plane = 2 * slab_at + 1 + extra
        edge = (coil_at == 0) | (coil_at == coil_count - 1) | (first < 0) | (last_plane >= 2 * slab_count)

        @pl.when(edge)
        def _():
            blank = jnp.zeros((planes, extra * 32, 128), BF16)

            @pl.when(coil_at == 0)
            def _():
                out_ref[:, 0 : extra * 32, 0:128] = blank

            @pl.when(coil_at == coil_count - 1)
            def _():
                out_ref[:, cells - extra * 32 : cells, 128:256] = blank

            for p in list(range(extra)) + list(range(planes - extra, planes)):

                @pl.when((first + p < 0) | (first + p >= 2 * slab_count))
                def _():
                    out_ref[p] = jnp.zeros(out_ref.shape[1:], BF16)

    first_out = hidden_refs[0]

    for p in range(first_out.shape[0]):
        taps = jnp.concatenate([features_ref[p + u] for u in range(3)], axis=0)
        values = jnp.dot(w_first_ref[:, :432], taps, preferred_element_type=F32)
        first_out[p] = jnp.maximum(values, 0.0).astype(BF16)
    outside(first_out, 0)

    for m in range(len(hidden_refs) - 1):
        in_ref, out_ref = hidden_refs[m], hidden_refs[m + 1]
        starts = starts_of(out_ref.shape[1] // 32)

        cells = GROUP * 32
        for p in range(out_ref.shape[0]):
            for start in starts:
                rows = slice(start * 32, (start + GROUP + 2) * 32)
                taps = jnp.concatenate([in_ref[p + u, rows] for u in range(3)], axis=0)
                sums = jnp.dot(w_middle_ref[m, :, : (GROUP + 2) * 96], taps, preferred_element_type=F32)
                values = shifted_sum([sums[t * cells : (t + 1) * cells] for t in range(3)])
                out_ref[p, start * 32 : start * 32 + cells] = jnp.maximum(values, 0.0).astype(BF16)
        outside(out_ref, m + 1)

    in_ref = hidden_refs[-1]
    for p in range(2):
        taps = jnp.concatenate([in_ref[p + u] for u in range(3)], axis=0)
        sums = jnp.dot(w_last_ref[:, :960], taps, preferred_element_type=F32)
        lane = lax.broadcasted_iota(jnp.int32, (64, 128), 1)
        for h in range(2):
            part = sums[:, 128 * h : 128 * (h + 1)]
            low = jnp.where(lane > 0, pltpu.roll(part, 1, 1), 0.0)
            high = jnp.where(lane < 127, pltpu.roll(part, 127, 1), 0.0)
            for a in range(2):
                rows = []
                for r in range(8):
                    at = 8 * r + a
                    rows.append(low[at : at + 1] + part[at + 2 : at + 3] + high[at + 4 : at + 5])
                piece = jnp.concatenate(rows, axis=0)
                refined_ref[a, p, 8 * h : 8 * h + 8] = solution_ref[a, p, 8 * h : 8 * h + 8] + piece


def tables_kernel(first_ref, middle_ref, last_ref, w_first_ref, w_middle_ref, w_last_ref):
    def spots(size, target, count=512):
        column = lax.broadcasted_iota(jnp.int32, (size, count), 1)
        return jnp.where(column == target(lax.broadcasted_iota(jnp.int32, (size, count), 0)), 1.0, 0.0).astype(BF16)

    def first_target(source):
        channel, u, v, t = source // 27, source // 9 % 3, source // 3 % 3, source % 3
        return ((u * 3 + t) * 2 + channel) * 24 + SIDE - HALO + v

    base = jnp.dot(first_ref[...], spots(54, first_target), preferred_element_type=F32)
    for r in range(16):
        w_first_ref[32 * r : 32 * r + 32] = (pltpu.roll(base, r, 1) if r else base).astype(BF16)
    for m in range(middle_ref.shape[0]):
        base = jnp.zeros((96, 512), F32)
        for u in range(3):
            for v in range(3):
                place = spots(32, lambda source: source + (u * (GROUP + 2) + v) * 32)
                taps = jnp.concatenate([middle_ref[m, u, v, t] for t in range(3)], axis=0)
                base = base + jnp.dot(taps, place, preferred_element_type=F32)
        for r in range(GROUP):
            band = (pltpu.roll(base, 32 * r, 1) if r else base).astype(BF16)
            for t in range(3):
                start = (t * GROUP + r) * 32
                w_middle_ref[m, start : start + 32] = band[32 * t : 32 * t + 32]
    bands = []
    for r in range(8):
        bands.append(pltpu.roll(last_ref[...], 32 * r, 1) if r else last_ref[...])
    w_last_ref[...] = jnp.concatenate(bands, axis=0).astype(BF16)


def tables(w_first, w_middle, w_last):
    first = w_first.reshape(w_first.shape[0], 54)
    middle = jnp.transpose(w_middle, (0, 3, 4, 5, 1, 2))
    last = jnp.pad(jnp.transpose(w_last, (4, 0, 2, 3, 1)), ((0, 0), (0, 0), (0, 0), (0, 7), (0, 0)))
    last = jnp.pad(last.reshape(6, 960), ((0, 2), (0, 64))).astype(F32)
    return call(
        tables_kernel,
        (struct((512, 512), BF16), struct((3, 96 * GROUP, 512), BF16), struct((64, 1024), BF16)),
        (first, middle, last),
    )


def swap(blocks, axis):
    return lax.all_to_all(blocks, axis, 0, 0, tiled=True)


def near_rows(rows):
    count = lax.axis_size("coil")
    before = lax.ppermute(rows[:, :, SIDE:], "coil", [(i, i + 1) for i in range(count - 1)])
    after = lax.ppermute(rows[:, :, :SIDE], "coil", [(i + 1, i) for i in range(count - 1)])
    return jnp.concatenate([before, rows, after], axis=2)


def near_planes(near):
    count = lax.axis_size("slab")

    def shifted(part, step):
        pairs = [(i, i + step) for i in range(count) if 0 <= i + step < count]
        return lax.ppermute(part, "slab", pairs)

    below = [shifted(near[1:], 3), shifted(near, 2), shifted(near, 1)]
    above = [shifted(near, -1), shifted(near, -2), shifted(near[:1], -3)]
    return below + [near] + above


def body(sensitivity, kspace, sampling, prior_image, w_first, w_middle, w_last):
    maps = sensitivity[0]
    len_y, len_z = maps.shape[2:]
    coils, slabs = lax.axis_size("coil"), lax.axis_size("slab")
    at = jnp.stack([lax.axis_index("coil"), lax.axis_index("slab")]).astype(jnp.int32)
    rows, columns = left_table(len_y), right_table(len_z)
    weights = tables(w_first, w_middle, w_last)

    term = adjoint(sampling, kspace[0], rows, columns, maps, coils)
    rhs_rows, copies = call(
        rows_kernel,
        (struct((64, 128)), struct((coils, 64, 128))),
        (swap(term, "coil"), prior_image),
        after=(),
    )
    rhs = swap(copies, "coil")
    near_shape = struct((2, 2, 32, 128))
    term, spectrum, norms, rhs_near = call(
        normal_kernel,
        (struct((coils, 72, 128)), struct((2, 2, len_y, len_z)), struct((8, 128)), near_shape),
        (at, rhs, sampling, maps, rows, columns),
        in_smem=(0,),
    )
    rhs_parts = near_planes(rhs_near)
    copies, image_rows, sums = call(
        image_kernel,
        (struct((coils, 64, 128), BF16), struct((2, 2, 16, 128)), struct((8, 128))),
        (swap(term, "coil"), rhs_rows, norms),
        after=rhs_parts,
    )
    image_parts = near_planes(near_rows(image_rows))
    tiles = call(
        last_kernel,
        struct((coils, 8, 128)),
        (sums, swap(copies, "coil"), spectrum, sampling, maps, rows, columns),
        after=image_parts[:AHEAD],
    )
    tiles = call(spread_kernel, struct((slabs, 8, 128)), (swap(tiles, "coil"),), after=image_parts[AHEAD:])
    last = swap(tiles, "slab")
    scratch = [pltpu.VMEM((12, 144, 256), BF16)]
    scratch += [pltpu.VMEM((10 - 2 * m, (16 - 2 * m) * 32, 256), BF16) for m in range(4)]
    return call(
        functools.partial(denoise_kernel, coils, slabs),
        (struct(prior_image.shape), struct(prior_image.shape)),
        (at, last, *rhs_parts, *image_parts, *weights),
        scratch=scratch,
        in_smem=(0,),
    )


def solution(mesh):
    placed = (
        P("coil", None, "slab", None, None),
        P("coil", None, "slab", None, None),
        P("slab", None, None),
        P(None, "slab", "coil", None),
        P(),
        P(),
        P(),
    )
    return jax.shard_map(
        body,
        mesh=mesh,
        in_specs=placed,
        out_specs=(P(None, "slab", "coil", None), P(None, "slab", "coil", None)),
        check_vma=False,
    )
```

```python
import functools
import math

import jax
import jax.numpy as jnp
import numpy as np
from jax import lax
from jax.experimental import pallas as pl
from jax.experimental.pallas import tpu as pltpu
from jax.sharding import PartitionSpec as P

LAMBDA = 0.5
HALO = 5
SIDE = 8
GROUP = 2
F32 = jnp.float32
BF16 = jnp.bfloat16
VMEM_BYTES = 20 * 1024 * 1024


def call(kernel, out_shape, args, scratch=(), in_smem=(), after=()):
    specs = [
        pl.BlockSpec(memory_space=pltpu.SMEM if i in in_smem else pltpu.VMEM) for i in range(len(args))
    ]
    specs += [pl.BlockSpec(memory_space=pl.ANY)] * len(after)
    if after:
        inner_kernel, count = kernel, len(args)

        def kernel(*refs):
            inner_kernel(*refs[:count], *refs[count + len(after) :])

    outs = jax.tree.map(lambda _: pl.BlockSpec(memory_space=pltpu.VMEM), out_shape)
    return pl.pallas_call(
        kernel,
        out_shape=out_shape,
        in_specs=specs,
        out_specs=outs,
        scratch_shapes=list(scratch),
        compiler_params=pltpu.CompilerParams(vmem_limit_bytes=VMEM_BYTES),
    )(*args, *after)


def struct(shape, dtype=F32):
    return jax.ShapeDtypeStruct(shape, dtype)


def halves(table):
    high = table.astype(np.float32).astype(jnp.bfloat16)
    low = (table.astype(np.float32) - high.astype(np.float32)).astype(jnp.bfloat16)
    return high, low


def dft_pair(length):
    positions = np.arange(length)
    angles = 2.0 * math.pi / length * (positions[:, None] * positions[None, :] % length)
    scaling = 1.0 / math.sqrt(length)
    return np.cos(angles) * scaling, scaling * np.sin(angles)


def left_table(length):
    cosine, sine = dft_pair(length)
    parts = [np.concatenate(halves(part), axis=1) for part in (cosine, sine)]
    return np.concatenate(parts, axis=0)


def right_table(length):
    cosine, sine = dft_pair(length)
    return np.concatenate(halves(cosine) + halves(sine), axis=1)


def split(values):
    high = values.astype(BF16)
    low = (values - high.astype(F32)).astype(BF16)
    return high, low


def dft_rows(field, table_ref, sign):
    values = jnp.concatenate(field[0] + field[1], axis=1)
    high, low = split(values)
    size = values.shape[0]
    table_high, table_low = table_ref[:, :size], table_ref[:, size:]
    table = jnp.concatenate([table_high, table_high, table_low], axis=1)
    products = jnp.dot(table, jnp.concatenate([high, low, high], axis=0), preferred_element_type=F32)
    half = values.shape[1] // 2
    cosine, sine = products[:size], products[size:]
    real = cosine[:, :half] - sign * sine[:, half:]
    imag = cosine[:, half:] + sign * sine[:, :half]
    columns = half // 2
    return [[part[:, p * columns : (p + 1) * columns] for p in range(2)] for part in (real, imag)]


def dft_columns(field, table_ref, sign):
    values = by_columns(field)
    high, low = split(values)
    size = table_ref.shape[0]
    cosine_high, cosine_low, sine_high, sine_low = [table_ref[:, i * size : (i + 1) * size] for i in range(4)]

    def block(cosine, sine):
        plus, minus = (sine, -sine) if sign > 0 else (-sine, sine)
        return jnp.concatenate(
            [jnp.concatenate([cosine, plus], axis=1), jnp.concatenate([minus, cosine], axis=1)], axis=0
        )

    table_high = block(cosine_high, sine_high)
    table = jnp.concatenate([table_high, table_high, block(cosine_low, sine_low)], axis=0)
    return from_columns(jnp.dot(jnp.concatenate([high, low, high], axis=1), table, preferred_element_type=F32))


def by_columns(field):
    planes = range(len(field[0]))
    return jnp.concatenate([jnp.concatenate([field[0][p], field[1][p]], axis=1) for p in planes], axis=0)


def from_columns(values):
    rows, columns = values.shape[0] // 2, values.shape[1] // 2
    return [[values[p * rows : (p + 1) * rows, a * columns : (a + 1) * columns] for p in range(2)] for a in range(2)]


def load_image(blocks_ref):
    count, _, columns = blocks_ref.shape
    rows = 16

    def one(a, p):
        start = (2 * a + p) * rows
        return blocks_ref[:, start : start + rows, :].reshape(count * rows, columns)

    return [[one(a, p) for p in range(2)] for a in range(2)]


def store_image(blocks_ref, image):
    count, _, columns = blocks_ref.shape
    rows = 16
    for a in range(2):
        for p in range(2):
            start = (2 * a + p) * rows
            blocks_ref[:, start : start + rows, :] = image[a][p].reshape(count, rows, columns)


def coil_field(maps_ref, image):
    real = [maps_ref[0, p] * image[0][p] - maps_ref[1, p] * image[1][p] for p in range(2)]
    imag = [maps_ref[0, p] * image[1][p] + maps_ref[1, p] * image[0][p] for p in range(2)]
    return [real, imag]


def coil_term(maps_ref, field):
    real = [maps_ref[0, p] * field[0][p] + maps_ref[1, p] * field[1][p] for p in range(2)]
    imag = [maps_ref[0, p] * field[1][p] - maps_ref[1, p] * field[0][p] for p in range(2)]
    return [real, imag]


def masked(field, mask_ref):
    masks = [mask_ref[p].astype(F32) for p in range(2)]
    return [[field[a][p] * masks[p] for p in range(2)] for a in range(2)]


def inner(first, second):
    return sum(row_sum(first[a][p] * second[a][p]) for a in range(2) for p in range(2))


def row_sum(values):
    folded = jnp.sum(values.reshape(-1, 8, values.shape[-1]), axis=0)
    folded = jnp.sum(folded, axis=0, keepdims=True)
    return folded


def tile_of(rows):
    blank = jnp.zeros((1, 128), F32)
    return jnp.concatenate(list(rows) + [blank] * (8 - len(rows)), axis=0)


def store_near(near_ref, blocks_ref, at):
    count = blocks_ref.shape[0]
    for a in range(2):
        for p in range(2):
            start = (2 * a + p) * 16
            near_ref[p, a, 8:24, :] = blocks_ref[at, start : start + 16, :]
            before = blocks_ref[jnp.maximum(at - 1, 0), start + 8 : start + 16, :]
            after = blocks_ref[jnp.minimum(at + 1, count - 1), start : start + 8, :]
            near_ref[p, a, 0:8, :] = jnp.where(at > 0, before, 0.0)
            near_ref[p, a, 24:32, :] = jnp.where(at < count - 1, after, 0.0)


def adjoint_kernel(
    mask_hbm, kspace_hbm, rows_hbm, columns_hbm, maps_hbm, out_ref, mask_ref, kspace_ref, rows_ref, columns_ref, maps_ref, sems
):
    sources = (mask_hbm, kspace_hbm, rows_hbm, columns_hbm, maps_hbm)
    targets = (mask_ref, kspace_ref, rows_ref, columns_ref, maps_ref)
    copies = [pltpu.make_async_copy(src, dst, sems.at[i]) for i, (src, dst) in enumerate(zip(sources, targets))]
    for copy in copies:
        copy.start()
    for copy in copies[:3]:
        copy.wait()
    field = masked([[kspace_ref[a, p] for p in range(2)] for a in range(2)], mask_ref)
    field = dft_rows(field, rows_ref, 1.0)
    copies[3].wait()
    field = dft_columns(field, columns_ref, 1.0)
    copies[4].wait()
    store_image(out_ref, coil_term(maps_ref, field))


def adjoint(mask, kspace, rows, columns, maps, coils):
    args = (mask, kspace, rows, columns, maps)
    return pl.pallas_call(
        adjoint_kernel,
        out_shape=struct((coils, 64, 128)),
        in_specs=[pl.BlockSpec(memory_space=pl.ANY)] * len(args),
        out_specs=pl.BlockSpec(memory_space=pltpu.VMEM),
        scratch_shapes=[pltpu.VMEM(arg.shape, arg.dtype) for arg in args] + [pltpu.SemaphoreType.DMA((len(args),))],
        compiler_params=pltpu.CompilerParams(vmem_limit_bytes=60 * 1024 * 1024),
    )(*args)


def rows_kernel(blocks_ref, prior_ref, rows_ref, copies_ref):
    count = blocks_ref.shape[0]
    total = jnp.sum(blocks_ref[...], axis=0)
    prior = jnp.concatenate([prior_ref[a, p] for a in range(2) for p in range(2)], axis=0)
    total = total + LAMBDA * prior
    rows_ref[...] = total
    for k in range(count):
        copies_ref[k] = total


def normal_kernel(
    at_ref, blocks_ref, mask_ref, maps_ref, rows_ref, columns_ref, out_ref, spectrum_ref, tile_ref, near_ref
):
    store_near(near_ref, blocks_ref, at_ref[0])
    image = load_image(blocks_ref)
    field = dft_columns(coil_field(maps_ref, image), columns_ref, -1.0)
    spectrum = masked(dft_rows(field, rows_ref, -1.0), mask_ref)
    for a in range(2):
        for p in range(2):
            spectrum_ref[a, p] = spectrum[a][p]
    field = dft_columns(dft_rows(spectrum, rows_ref, 1.0), columns_ref, 1.0)
    store_image(out_ref, coil_term(maps_ref, field))
    tile_ref[...] = tile_of([inner(image, image)])
    energies = tile_of([inner(spectrum, spectrum)])
    for k in range(blocks_ref.shape[0]):
        out_ref[k, 64:72, :] = energies


def lane_sum(values):
    return jnp.sum(values, axis=-1, keepdims=True)


def slab_step(norm, energy):
    curved = energy + LAMBDA * norm
    return jnp.where(curved > 0.0, norm / jnp.where(curved > 0.0, curved, 1.0), 1.0)


def image_kernel(blocks_ref, rhs_rows_ref, norms_ref, copies_ref, sums_ref):
    total = jnp.sum(blocks_ref[...], axis=0)
    rhs = rhs_rows_ref[...]
    image = total[:64] + LAMBDA * rhs
    for k in range(blocks_ref.shape[0]):
        copies_ref[k] = image
    norm, energy = norms_ref[0:1, :], total[64:65]
    residual = rhs - slab_step(lane_sum(norm), lane_sum(energy)) * image
    share = 1.0 / blocks_ref.shape[0]
    sums_ref[...] = tile_of([row_sum(residual * residual), row_sum(residual * rhs), share * norm, share * energy])


def last_kernel(sums_ref, blocks_ref, spectrum_ref, mask_ref, maps_ref, rows_ref, columns_ref, out_ref):
    step = slab_step(lane_sum(sums_ref[2:3, :]), lane_sum(sums_ref[3:4, :]))
    field = dft_columns(coil_field(maps_ref, load_image(blocks_ref)), columns_ref, -1.0)
    spectrum = masked(dft_rows(field, rows_ref, -1.0), mask_ref)
    before = [[spectrum_ref[a, p] for p in range(2)] for a in range(2)]
    spectrum = [[before[a][p] - step * spectrum[a][p] for p in range(2)] for a in range(2)]
    tile = tile_of([inner(spectrum, spectrum), inner(spectrum, before)] + [sums_ref[i : i + 1, :] for i in range(4)])
    for k in range(out_ref.shape[0]):
        out_ref[k, 0:8] = tile
        out_ref[k, 8:] = jnp.zeros((out_ref.shape[1] - 8, 128), F32)


def near_kernel(at_ref, blocks_ref, near_ref):
    store_near(near_ref, blocks_ref, at_ref[0])


def spread_kernel(tiles_ref, out_ref):
    total = jnp.sum(tiles_ref[:, 0:8, :], axis=0)
    for k in range(out_ref.shape[0]):
        out_ref[k] = total


def final_scales(tiles_ref):
    curve, curve_cross, norm, cross, norm_first, energy_first = [
        lane_sum(tiles_ref[:, i, :]) for i in range(6)
    ]

    def over_slabs(values):
        return jnp.sum(values, axis=0, keepdims=True)

    all_norm, all_energy = over_slabs(norm_first), over_slabs(energy_first)
    step_first = all_norm / (all_energy + LAMBDA * all_norm)
    here = step_first / slab_step(norm_first, energy_first)
    rest = 1.0 - here
    curve = over_slabs(here * here * curve + rest * (2.0 * here * curve_cross + rest * energy_first))
    curve_cross = over_slabs(here * curve_cross + rest * energy_first)
    norm = over_slabs(here * here * norm + rest * (2.0 * here * cross + rest * norm_first))
    cross = over_slabs(here * cross + rest * norm_first)
    ratio = norm / all_norm
    curvature = curve + ratio * (2.0 * curve_cross + ratio * all_energy)
    curvature = curvature + LAMBDA * (norm + ratio * (2.0 * cross + ratio * all_norm))
    return step_first, norm / curvature, ratio


def starts_of(rows):
    starts = list(range(0, rows - GROUP + 1, GROUP))
    if starts[-1] + GROUP < rows:
        starts.append(rows - GROUP)
    return starts


def shifted_sum(parts):
    before, here, after = parts
    lane = lax.broadcasted_iota(jnp.int32, before.shape[:1] + (128,), 1)
    outs = []
    for h in range(2):
        cut = slice(128 * h, 128 * (h + 1))
        low = jnp.where(lane > 0, pltpu.roll(before[:, cut], 1, 1), 0.0)
        high = jnp.where(lane < 127, pltpu.roll(after[:, cut], 127, 1), 0.0)
        outs.append(here[:, cut] + low + high)
    return jnp.concatenate(outs, axis=1)


def denoise_kernel(coil_count, slab_count, *refs):
    at_ref, last_ref = refs[:2]
    rhs_refs = refs[2:7]
    image_refs = refs[7:12]
    w_first_ref, w_middle_ref, w_last_ref, solution_ref, refined_ref = refs[12:17]
    features_ref = refs[17]
    hidden_refs = refs[18:]
    coil_at = at_ref[0]
    slab_at = at_ref[1]

    step_first, step_last, ratio = final_scales(last_ref)
    scale_rhs = step_first + step_last * ratio

    lane = lax.broadcasted_iota(jnp.int32, (48, 128), 1)
    plane = 0
    brick = None
    for rhs_ref, image_ref in zip(rhs_refs, image_refs):
        for p in range(rhs_ref.shape[0]):
            full = []
            for a in range(2):
                rhs = rhs_ref[p, a]
                full.append(scale_rhs * rhs + step_last * (rhs - step_first * image_ref[p, a]))
            if 5 <= plane < 7:
                for a in range(2):
                    solution_ref[a, plane - 5] = full[a][8:24]
            for h in range(2):
                window = jnp.concatenate([f[8 * h : 8 * h + 24] for f in full], axis=0)
                cut = slice(128 * h, 128 * (h + 1))
                low = jnp.where(lane > 0, pltpu.roll(window, 1, 1), 0.0)
                high = jnp.where(lane < 127, pltpu.roll(window, 127, 1), 0.0)
                features_ref[plane, 0:48, cut] = low.astype(BF16)
                features_ref[plane, 48:96, cut] = window.astype(BF16)
                features_ref[plane, 96:144, cut] = high.astype(BF16)
            plane += 1

    def outside(out_ref, depth):
        planes, cells, _ = out_ref.shape
        extra = 4 - depth
        first = 2 * slab_at - extra

        last_plane = 2 * slab_at + 1 + extra
        edge = (coil_at == 0) | (coil_at == coil_count - 1) | (first < 0) | (last_plane >= 2 * slab_count)

        @pl.when(edge)
        def _():
            blank = jnp.zeros((planes, extra * 32, 128), BF16)

            @pl.when(coil_at == 0)
            def _():
                out_ref[:, 0 : extra * 32, 0:128] = blank

            @pl.when(coil_at == coil_count - 1)
            def _():
                out_ref[:, cells - extra * 32 : cells, 128:256] = blank

            for p in list(range(extra)) + list(range(planes - extra, planes)):

                @pl.when((first + p < 0) | (first + p >= 2 * slab_count))
                def _():
                    out_ref[p] = jnp.zeros(out_ref.shape[1:], BF16)

    first_out = hidden_refs[0]

    for p in range(first_out.shape[0]):
        taps = jnp.concatenate([features_ref[p + u] for u in range(3)], axis=0)
        values = jnp.dot(w_first_ref[:, :432], taps, preferred_element_type=F32)
        first_out[p] = jnp.maximum(values, 0.0).astype(BF16)
    outside(first_out, 0)

    for m in range(len(hidden_refs) - 1):
        in_ref, out_ref = hidden_refs[m], hidden_refs[m + 1]
        starts = starts_of(out_ref.shape[1] // 32)

        cells = GROUP * 32
        for p in range(out_ref.shape[0]):
            for start in starts:
                rows = slice(start * 32, (start + GROUP + 2) * 32)
                taps = jnp.concatenate([in_ref[p + u, rows] for u in range(3)], axis=0)
                sums = jnp.dot(w_middle_ref[m, :, : (GROUP + 2) * 96], taps, preferred_element_type=F32)
                values = shifted_sum([sums[t * cells : (t + 1) * cells] for t in range(3)])
                out_ref[p, start * 32 : start * 32 + cells] = jnp.maximum(values, 0.0).astype(BF16)
        outside(out_ref, m + 1)

    in_ref = hidden_refs[-1]
    for p in range(2):
        taps = jnp.concatenate([in_ref[p + u] for u in range(3)], axis=0)
        sums = jnp.dot(w_last_ref[:, :960], taps, preferred_element_type=F32)
        lane = lax.broadcasted_iota(jnp.int32, (64, 128), 1)
        for h in range(2):
            part = sums[:, 128 * h : 128 * (h + 1)]
            low = jnp.where(lane > 0, pltpu.roll(part, 1, 1), 0.0)
            high = jnp.where(lane < 127, pltpu.roll(part, 127, 1), 0.0)
            for a in range(2):
                rows = []
                for r in range(8):
                    at = 8 * r + a
                    rows.append(low[at : at + 1] + part[at + 2 : at + 3] + high[at + 4 : at + 5])
                piece = jnp.concatenate(rows, axis=0)
                refined_ref[a, p, 8 * h : 8 * h + 8] = solution_ref[a, p, 8 * h : 8 * h + 8] + piece


def tables_kernel(first_ref, middle_ref, w_first_ref, w_middle_ref):
    def spots(size, target, count=512):
        column = lax.broadcasted_iota(jnp.int32, (size, count), 1)
        return jnp.where(column == target(lax.broadcasted_iota(jnp.int32, (size, count), 0)), 1.0, 0.0).astype(BF16)

    def first_target(source):
        channel, u, v, t = source // 27, source // 9 % 3, source // 3 % 3, source % 3
        return ((u * 3 + t) * 2 + channel) * 24 + SIDE - HALO + v

    base = jnp.dot(first_ref[...], spots(54, first_target), preferred_element_type=F32)
    for r in range(16):
        w_first_ref[32 * r : 32 * r + 32] = (pltpu.roll(base, r, 1) if r else base).astype(BF16)
    for m in range(middle_ref.shape[0]):
        base = jnp.zeros((96, 512), F32)
        for u in range(3):
            for v in range(3):
                place = spots(32, lambda source: source + (u * (GROUP + 2) + v) * 32)
                taps = jnp.concatenate([middle_ref[m, u, v, t] for t in range(3)], axis=0)
                base = base + jnp.dot(taps, place, preferred_element_type=F32)
        for r in range(GROUP):
            band = (pltpu.roll(base, 32 * r, 1) if r else base).astype(BF16)
            for t in range(3):
                start = (t * GROUP + r) * 32
                w_middle_ref[m, start : start + 32] = band[32 * t : 32 * t + 32]


def last_table_kernel(last_ref, w_last_ref):
    bands = []
    for r in range(8):
        bands.append(pltpu.roll(last_ref[...], 32 * r, 1) if r else last_ref[...])
    w_last_ref[...] = jnp.concatenate(bands, axis=0).astype(BF16)


def tables(w_first, w_middle, w_last):
    first = w_first.reshape(w_first.shape[0], 54)
    middle = jnp.transpose(w_middle, (0, 3, 4, 5, 1, 2))
    last = jnp.pad(jnp.transpose(w_last, (4, 0, 2, 3, 1)), ((0, 0), (0, 0), (0, 0), (0, 7), (0, 0)))
    last = jnp.pad(last.reshape(6, 960), ((0, 2), (0, 64))).astype(F32)
    pair = call(
        tables_kernel,
        (struct((512, 512), BF16), struct((3, 96 * GROUP, 512), BF16)),
        (first, middle),
    )
    return (*pair, call(last_table_kernel, struct((64, 1024), BF16), (last,))), (first, last)


def swap(blocks, axis):
    return lax.all_to_all(blocks, axis, 0, 0, tiled=True)


def near_planes(near):
    count = lax.axis_size("slab")

    def shifted(part, step):
        pairs = [(i, i + step) for i in range(count) if 0 <= i + step < count]
        return lax.ppermute(part, "slab", pairs)

    below, above = shifted(near, 1), shifted(near, -1)
    below_far = shifted(jnp.concatenate([below[1:], near]), 2)
    above_far = shifted(jnp.concatenate([near, above[:1]]), -2)
    return [below_far, below, near, above, above_far]


def body(sensitivity, kspace, sampling, prior_image, w_first, w_middle, w_last):
    maps = sensitivity[0]
    len_y, len_z = maps.shape[2:]
    coils, slabs = lax.axis_size("coil"), lax.axis_size("slab")
    at = jnp.stack([lax.axis_index("coil"), lax.axis_index("slab")]).astype(jnp.int32)
    rows, columns = left_table(len_y), right_table(len_z)
    weights, prepared = tables(w_first, w_middle, w_last)

    term = adjoint(sampling, kspace[0], rows, columns, maps, coils)
    rhs_rows, copies = call(
        rows_kernel,
        (struct((64, 128)), struct((coils, 64, 128))),
        (swap(term, "coil"), prior_image),
        after=prepared,
    )
    rhs = swap(copies, "coil")
    near_shape = struct((2, 2, 32, 128))
    term, spectrum, norms, rhs_near = call(
        normal_kernel,
        (struct((coils, 72, 128)), struct((2, 2, len_y, len_z)), struct((8, 128)), near_shape),
        (at, rhs, sampling, maps, rows, columns),
        in_smem=(0,),
    )
    rhs_parts = near_planes(rhs_near)
    copies, sums = call(
        image_kernel,
        (struct((coils, 64, 128)), struct((8, 128))),
        (swap(term, "coil"), rhs_rows, norms),
        after=rhs_parts,
    )
    image = swap(copies, "coil")
    tiles = call(
        last_kernel,
        struct((coils, 16, 128)),
        (sums, image, spectrum, sampling, maps, rows, columns),
        after=weights[2:],
    )
    image_parts = near_planes(call(near_kernel, near_shape, (at, image), in_smem=(0,), after=(tiles,)))
    tiles = call(spread_kernel, struct((slabs, 8, 128)), (swap(tiles, "coil"),), after=(image_parts[1], image_parts[3]))
    last = swap(tiles, "slab")
    scratch = [pltpu.VMEM((12, 144, 256), BF16)]
    scratch += [pltpu.VMEM((10 - 2 * m, (16 - 2 * m) * 32, 256), BF16) for m in range(4)]
    return call(
        functools.partial(denoise_kernel, coils, slabs),
        (struct(prior_image.shape), struct(prior_image.shape)),
        (at, last, *rhs_parts, *image_parts, *weights),
        scratch=scratch,
        in_smem=(0,),
    )


def solution(mesh):
    placed = (
        P("coil", None, "slab", None, None),
        P("coil", None, "slab", None, None),
        P("slab", None, None),
        P(None, "slab", "coil", None),
        P(),
        P(),
        P(),
    )
    return jax.shard_map(
        body,
        mesh=mesh,
        in_specs=placed,
        out_specs=(P(None, "slab", "coil", None), P(None, "slab", "coil", None)),
        check_vma=False,
    )
```

```python
import functools
import math

import jax
import jax.numpy as jnp
import numpy as np
from jax import lax
from jax.experimental import pallas as pl
from jax.experimental.pallas import tpu as pltpu
from jax.sharding import PartitionSpec as P

LAMBDA = 0.5
HALO = 5
SIDE = 8
GROUP = 2
F32 = jnp.float32
BF16 = jnp.bfloat16
VMEM_BYTES = 20 * 1024 * 1024


def call(kernel, out_shape, args, scratch=(), in_smem=(), after=()):
    specs = [
        pl.BlockSpec(memory_space=pltpu.SMEM if i in in_smem else pltpu.VMEM) for i in range(len(args))
    ]
    specs += [pl.BlockSpec(memory_space=pl.ANY)] * len(after)
    if after:
        inner_kernel, count = kernel, len(args)

        def kernel(*refs):
            inner_kernel(*refs[:count], *refs[count + len(after) :])

    outs = jax.tree.map(lambda _: pl.BlockSpec(memory_space=pltpu.VMEM), out_shape)
    return pl.pallas_call(
        kernel,
        out_shape=out_shape,
        in_specs=specs,
        out_specs=outs,
        scratch_shapes=list(scratch),
        compiler_params=pltpu.CompilerParams(vmem_limit_bytes=VMEM_BYTES),
    )(*args, *after)


def struct(shape, dtype=F32):
    return jax.ShapeDtypeStruct(shape, dtype)


def halves(table):
    high = table.astype(np.float32).astype(jnp.bfloat16)
    low = (table.astype(np.float32) - high.astype(np.float32)).astype(jnp.bfloat16)
    return high, low


def dft_pair(length):
    positions = np.arange(length)
    angles = 2.0 * math.pi / length * (positions[:, None] * positions[None, :] % length)
    scaling = 1.0 / math.sqrt(length)
    return np.cos(angles) * scaling, scaling * np.sin(angles)


def left_table(length):
    cosine, sine = dft_pair(length)
    parts = [np.concatenate(halves(part), axis=1) for part in (cosine, sine)]
    return np.concatenate(parts, axis=0)


def right_table(length):
    cosine, sine = dft_pair(length)
    return np.concatenate(halves(cosine) + halves(sine), axis=1)


def split(values):
    high = values.astype(BF16)
    low = (values - high.astype(F32)).astype(BF16)
    return high, low


def dft_rows(field, table_ref, sign):
    values = jnp.concatenate(field[0] + field[1], axis=1)
    high, low = split(values)
    size = values.shape[0]
    table_high, table_low = table_ref[:, :size], table_ref[:, size:]
    table = jnp.concatenate([table_high, table_high, table_low], axis=1)
    products = jnp.dot(table, jnp.concatenate([high, low, high], axis=0), preferred_element_type=F32)
    half = values.shape[1] // 2
    cosine, sine = products[:size], products[size:]
    real = cosine[:, :half] - sign * sine[:, half:]
    imag = cosine[:, half:] + sign * sine[:, :half]
    columns = half // 2
    return [[part[:, p * columns : (p + 1) * columns] for p in range(2)] for part in (real, imag)]


def dft_columns(field, table_ref, sign):
    values = by_columns(field)
    high, low = split(values)
    size = table_ref.shape[0]
    cosine_high, cosine_low, sine_high, sine_low = [table_ref[:, i * size : (i + 1) * size] for i in range(4)]

    def block(cosine, sine):
        plus, minus = (sine, -sine) if sign > 0 else (-sine, sine)
        return jnp.concatenate(
            [jnp.concatenate([cosine, plus], axis=1), jnp.concatenate([minus, cosine], axis=1)], axis=0
        )

    table_high = block(cosine_high, sine_high)
    table = jnp.concatenate([table_high, table_high, block(cosine_low, sine_low)], axis=0)
    return from_columns(jnp.dot(jnp.concatenate([high, low, high], axis=1), table, preferred_element_type=F32))


def by_columns(field):
    planes = range(len(field[0]))
    return jnp.concatenate([jnp.concatenate([field[0][p], field[1][p]], axis=1) for p in planes], axis=0)


def from_columns(values):
    rows, columns = values.shape[0] // 2, values.shape[1] // 2
    return [[values[p * rows : (p + 1) * rows, a * columns : (a + 1) * columns] for p in range(2)] for a in range(2)]


def load_image(blocks_ref):
    count, _, columns = blocks_ref.shape
    rows = 16

    def one(a, p):
        start = (2 * a + p) * rows
        return blocks_ref[:, start : start + rows, :].astype(F32).reshape(count * rows, columns)

    return [[one(a, p) for p in range(2)] for a in range(2)]


def store_image(blocks_ref, image):
    count, _, columns = blocks_ref.shape
    rows = 16
    for a in range(2):
        for p in range(2):
            start = (2 * a + p) * rows
            blocks_ref[:, start : start + rows, :] = image[a][p].reshape(count, rows, columns)


def coil_field(maps_ref, image):
    real = [maps_ref[0, p] * image[0][p] - maps_ref[1, p] * image[1][p] for p in range(2)]
    imag = [maps_ref[0, p] * image[1][p] + maps_ref[1, p] * image[0][p] for p in range(2)]
    return [real, imag]


def coil_term(maps_ref, field):
    real = [maps_ref[0, p] * field[0][p] + maps_ref[1, p] * field[1][p] for p in range(2)]
    imag = [maps_ref[0, p] * field[1][p] - maps_ref[1, p] * field[0][p] for p in range(2)]
    return [real, imag]


def masked(field, mask_ref):
    masks = [mask_ref[p].astype(F32) for p in range(2)]
    return [[field[a][p] * masks[p] for p in range(2)] for a in range(2)]


def inner(first, second):
    return sum(row_sum(first[a][p] * second[a][p]) for a in range(2) for p in range(2))


def row_sum(values):
    folded = jnp.sum(values.reshape(-1, 8, values.shape[-1]), axis=0)
    folded = jnp.sum(folded, axis=0, keepdims=True)
    return folded


def tile_of(rows):
    blank = jnp.zeros((1, 128), F32)
    return jnp.concatenate(list(rows) + [blank] * (8 - len(rows)), axis=0)


def store_near(near_ref, blocks_ref, at):
    count = blocks_ref.shape[0]
    for a in range(2):
        for p in range(2):
            start = (2 * a + p) * 16
            near_ref[p, a, 8:24, :] = blocks_ref[at, start : start + 16, :]
            before = blocks_ref[jnp.maximum(at - 1, 0), start + 8 : start + 16, :]
            after = blocks_ref[jnp.minimum(at + 1, count - 1), start : start + 8, :]
            near_ref[p, a, 0:8, :] = jnp.where(at > 0, before, 0.0)
            near_ref[p, a, 24:32, :] = jnp.where(at < count - 1, after, 0.0)


def adjoint_kernel(
    mask_hbm, kspace_hbm, rows_hbm, columns_hbm, maps_hbm, out_ref, mask_ref, kspace_ref, rows_ref, columns_ref, maps_ref, sems
):
    sources = (mask_hbm, kspace_hbm, rows_hbm, columns_hbm, maps_hbm)
    targets = (mask_ref, kspace_ref, rows_ref, columns_ref, maps_ref)
    copies = [pltpu.make_async_copy(src, dst, sems.at[i]) for i, (src, dst) in enumerate(zip(sources, targets))]
    for copy in copies:
        copy.start()
    for copy in copies[:3]:
        copy.wait()
    field = masked([[kspace_ref[a, p] for p in range(2)] for a in range(2)], mask_ref)
    field = dft_rows(field, rows_ref, 1.0)
    copies[3].wait()
    field = dft_columns(field, columns_ref, 1.0)
    copies[4].wait()
    store_image(out_ref, coil_term(maps_ref, field))


def adjoint(mask, kspace, rows, columns, maps, coils):
    args = (mask, kspace, rows, columns, maps)
    return pl.pallas_call(
        adjoint_kernel,
        out_shape=struct((coils, 64, 128)),
        in_specs=[pl.BlockSpec(memory_space=pl.ANY)] * len(args),
        out_specs=pl.BlockSpec(memory_space=pltpu.VMEM),
        scratch_shapes=[pltpu.VMEM(arg.shape, arg.dtype) for arg in args] + [pltpu.SemaphoreType.DMA((len(args),))],
        compiler_params=pltpu.CompilerParams(vmem_limit_bytes=60 * 1024 * 1024),
    )(*args)


def rows_kernel(blocks_ref, prior_ref, rows_ref, copies_ref):
    count = blocks_ref.shape[0]
    total = jnp.sum(blocks_ref[...], axis=0)
    prior = jnp.concatenate([prior_ref[a, p] for a in range(2) for p in range(2)], axis=0)
    total = total + LAMBDA * prior
    rows_ref[...] = total
    for k in range(count):
        copies_ref[k] = total


def normal_kernel(
    at_ref, blocks_ref, mask_ref, maps_ref, rows_ref, columns_ref, out_ref, spectrum_ref, tile_ref, near_ref
):
    store_near(near_ref, blocks_ref, at_ref[0])
    image = load_image(blocks_ref)
    field = dft_columns(coil_field(maps_ref, image), columns_ref, -1.0)
    spectrum = masked(dft_rows(field, rows_ref, -1.0), mask_ref)
    for a in range(2):
        for p in range(2):
            spectrum_ref[a, p] = spectrum[a][p]
    field = dft_columns(dft_rows(spectrum, rows_ref, 1.0), columns_ref, 1.0)
    store_image(out_ref, coil_term(maps_ref, field))
    tile_ref[...] = tile_of([inner(image, image)])
    energies = tile_of([inner(spectrum, spectrum)])
    for k in range(blocks_ref.shape[0]):
        out_ref[k, 64:72, :] = energies


def lane_sum(values):
    return jnp.sum(values, axis=-1, keepdims=True)


def slab_step(norm, energy):
    curved = energy + LAMBDA * norm
    return jnp.where(curved > 0.0, norm / jnp.where(curved > 0.0, curved, 1.0), 1.0)


def lane_sum(values):
    return jnp.sum(values, axis=-1, keepdims=True)


def slab_step(norm, energy):
    curved = energy + LAMBDA * norm
    return jnp.where(curved > 0.0, norm / jnp.where(curved > 0.0, curved, 1.0), 1.0)


def image_kernel(blocks_ref, rhs_rows_ref, norms_ref, copies_ref, sums_ref):
    total = jnp.sum(blocks_ref[...], axis=0)
    rhs = rhs_rows_ref[...]
    image = total[:64] + LAMBDA * rhs
    for k in range(blocks_ref.shape[0]):
        copies_ref[k] = image
    norm, energy = norms_ref[0:1, :], total[64:65]
    residual = rhs - slab_step(lane_sum(norm), lane_sum(energy)) * image
    share = 1.0 / blocks_ref.shape[0]
    sums_ref[...] = tile_of([row_sum(residual * residual), row_sum(residual * rhs), share * norm, share * energy])


def image_kernel(blocks_ref, rhs_rows_ref, norms_ref, copies_ref, rows_ref, head_ref, tail_ref, sums_ref):
    total = jnp.sum(blocks_ref[...], axis=0)
    rhs = rhs_rows_ref[...]
    image = total[:64] + LAMBDA * rhs
    norm, energy = norms_ref[0:1, :], total[64:65]
    residual = rhs - slab_step(lane_sum(norm), lane_sum(energy)) * image
    rounded = residual.astype(BF16)
    for k in range(blocks_ref.shape[0]):
        copies_ref[k] = rounded
    for a in range(2):
        for p in range(2):
            rows = image[(2 * a + p) * 16 : (2 * a + p + 1) * 16]
            rows_ref[p, a] = rows
            head_ref[p, a] = rows[:SIDE]
            tail_ref[p, a] = rows[SIDE:]
    share = 1.0 / blocks_ref.shape[0]
    sums_ref[...] = tile_of([row_sum(residual * residual), row_sum(residual * rhs), share * norm, share * energy])


def last_kernel(sums_ref, blocks_ref, spectrum_ref, mask_ref, maps_ref, rows_ref, columns_ref, out_ref):
    field = dft_columns(coil_field(maps_ref, load_image(blocks_ref)), columns_ref, -1.0)
    spectrum = masked(dft_rows(field, rows_ref, -1.0), mask_ref)
    before = [[spectrum_ref[a, p] for p in range(2)] for a in range(2)]
    tile = tile_of([inner(spectrum, spectrum), inner(spectrum, before)] + [sums_ref[i : i + 1, :] for i in range(4)])
    for k in range(out_ref.shape[0]):
        out_ref[k, 0:8] = tile
        out_ref[k, 8:] = jnp.zeros((out_ref.shape[1] - 8, 128), F32)


def join_kernel(before_ref, rows_ref, after_ref, near_ref):
    near_ref[:, :, 0:8, :] = before_ref[...]
    near_ref[:, :, 8:24, :] = rows_ref[...]
    near_ref[:, :, 24:32, :] = after_ref[...]


def pack_kernel(below_ref, near_ref, above_ref, low_ref, high_ref):
    low_ref[0] = below_ref[1]
    low_ref[1:3] = near_ref[...]
    high_ref[0:2] = near_ref[...]
    high_ref[2] = above_ref[0]


def spread_kernel(tiles_ref, out_ref):
    total = jnp.sum(tiles_ref[:, 0:8, :], axis=0)
    for k in range(out_ref.shape[0]):
        out_ref[k] = total


def final_scales(tiles_ref):
    curve, curve_cross, norm, cross, norm_first, energy_first = [
        lane_sum(tiles_ref[:, i, :]) for i in range(6)
    ]

    def over_slabs(values):
        return jnp.sum(values, axis=0, keepdims=True)

    all_norm, all_energy = over_slabs(norm_first), over_slabs(energy_first)
    step_first = all_norm / (all_energy + LAMBDA * all_norm)
    here = step_first / slab_step(norm_first, energy_first)
    rest = 1.0 - here
    curve = over_slabs(here * here * curve + rest * (2.0 * here * curve_cross + rest * energy_first))
    curve_cross = over_slabs(here * curve_cross + rest * energy_first)
    norm = over_slabs(here * here * norm + rest * (2.0 * here * cross + rest * norm_first))
    cross = over_slabs(here * cross + rest * norm_first)
    ratio = norm / all_norm
    curvature = curve + ratio * (2.0 * curve_cross + ratio * all_energy)
    curvature = curvature + LAMBDA * (norm + ratio * (2.0 * cross + ratio * all_norm))
    return step_first, norm / curvature, ratio


def starts_of(rows):
    starts = list(range(0, rows - GROUP + 1, GROUP))
    if starts[-1] + GROUP < rows:
        starts.append(rows - GROUP)
    return starts


def shifted_sum(parts):
    before, here, after = parts
    lane = lax.broadcasted_iota(jnp.int32, before.shape[:1] + (128,), 1)
    outs = []
    for h in range(2):
        cut = slice(128 * h, 128 * (h + 1))
        low = jnp.where(lane > 0, pltpu.roll(before[:, cut], 1, 1), 0.0)
        high = jnp.where(lane < 127, pltpu.roll(after[:, cut], 127, 1), 0.0)
        outs.append(here[:, cut] + low + high)
    return jnp.concatenate(outs, axis=1)


def denoise_kernel(coil_count, slab_count, *refs):
    at_ref, last_ref = refs[:2]
    rhs_refs = refs[2:7]
    image_refs = refs[7:12]
    w_first_ref, w_middle_ref, w_last_ref, solution_ref, refined_ref = refs[12:17]
    features_ref = refs[17]
    hidden_refs = refs[18:]
    coil_at = at_ref[0]
    slab_at = at_ref[1]

    step_first, step_last, ratio = final_scales(last_ref)
    scale_rhs = step_first + step_last * ratio

    lane = lax.broadcasted_iota(jnp.int32, (48, 128), 1)
    plane = 0
    brick = None
    for rhs_ref, image_ref in zip(rhs_refs, image_refs):
        for p in range(rhs_ref.shape[0]):
            full = []
            for a in range(2):
                rhs = rhs_ref[p, a]
                full.append(scale_rhs * rhs + step_last * (rhs - step_first * image_ref[p, a]))
            if 5 <= plane < 7:
                for a in range(2):
                    solution_ref[a, plane - 5] = full[a][8:24]
            for h in range(2):
                window = jnp.concatenate([f[8 * h : 8 * h + 24] for f in full], axis=0)
                cut = slice(128 * h, 128 * (h + 1))
                low = jnp.where(lane > 0, pltpu.roll(window, 1, 1), 0.0)
                high = jnp.where(lane < 127, pltpu.roll(window, 127, 1), 0.0)
                features_ref[plane, 0:48, cut] = low.astype(BF16)
                features_ref[plane, 48:96, cut] = window.astype(BF16)
                features_ref[plane, 96:144, cut] = high.astype(BF16)
            plane += 1

    def outside(out_ref, depth):
        planes, cells, _ = out_ref.shape
        extra = 4 - depth
        first = 2 * slab_at - extra

        last_plane = 2 * slab_at + 1 + extra
        edge = (coil_at == 0) | (coil_at == coil_count - 1) | (first < 0) | (last_plane >= 2 * slab_count)

        @pl.when(edge)
        def _():
            blank = jnp.zeros((planes, extra * 32, 128), BF16)

            @pl.when(coil_at == 0)
            def _():
                out_ref[:, 0 : extra * 32, 0:128] = blank

            @pl.when(coil_at == coil_count - 1)
            def _():
                out_ref[:, cells - extra * 32 : cells, 128:256] = blank

            for p in list(range(extra)) + list(range(planes - extra, planes)):

                @pl.when((first + p < 0) | (first + p >= 2 * slab_count))
                def _():
                    out_ref[p] = jnp.zeros(out_ref.shape[1:], BF16)

    first_out = hidden_refs[0]

    for p in range(first_out.shape[0]):
        taps = jnp.concatenate([features_ref[p + u] for u in range(3)], axis=0)
        values = jnp.dot(w_first_ref[:, :432], taps, preferred_element_type=F32)
        first_out[p] = jnp.maximum(values, 0.0).astype(BF16)
    outside(first_out, 0)

    for m in range(len(hidden_refs) - 1):
        in_ref, out_ref = hidden_refs[m], hidden_refs[m + 1]
        starts = starts_of(out_ref.shape[1] // 32)

        cells = GROUP * 32
        for p in range(out_ref.shape[0]):
            for start in starts:
                rows = slice(start * 32, (start + GROUP + 2) * 32)
                taps = jnp.concatenate([in_ref[p + u, rows] for u in range(3)], axis=0)
                sums = jnp.dot(w_middle_ref[m, :, : (GROUP + 2) * 96], taps, preferred_element_type=F32)
                values = shifted_sum([sums[t * cells : (t + 1) * cells] for t in range(3)])
                out_ref[p, start * 32 : start * 32 + cells] = jnp.maximum(values, 0.0).astype(BF16)
        outside(out_ref, m + 1)

    in_ref = hidden_refs[-1]
    for p in range(2):
        taps = jnp.concatenate([in_ref[p + u] for u in range(3)], axis=0)
        sums = jnp.dot(w_last_ref[:, :960], taps, preferred_element_type=F32)
        lane = lax.broadcasted_iota(jnp.int32, (64, 128), 1)
        for h in range(2):
            part = sums[:, 128 * h : 128 * (h + 1)]
            low = jnp.where(lane > 0, pltpu.roll(part, 1, 1), 0.0)
            high = jnp.where(lane < 127, pltpu.roll(part, 127, 1), 0.0)
            for a in range(2):
                rows = []
                for r in range(8):
                    at = 8 * r + a
                    rows.append(low[at : at + 1] + part[at + 2 : at + 3] + high[at + 4 : at + 5])
                piece = jnp.concatenate(rows, axis=0)
                refined_ref[a, p, 8 * h : 8 * h + 8] = solution_ref[a, p, 8 * h : 8 * h + 8] + piece


def tables_kernel(first_ref, middle_ref, w_first_ref, w_middle_ref):
    def spots(size, target, count=512):
        column = lax.broadcasted_iota(jnp.int32, (size, count), 1)
        return jnp.where(column == target(lax.broadcasted_iota(jnp.int32, (size, count), 0)), 1.0, 0.0).astype(BF16)

    def first_target(source):
        channel, u, v, t = source // 27, source // 9 % 3, source // 3 % 3, source % 3
        return ((u * 3 + t) * 2 + channel) * 24 + SIDE - HALO + v

    base = jnp.dot(first_ref[...], spots(54, first_target), preferred_element_type=F32)
    for r in range(16):
        w_first_ref[32 * r : 32 * r + 32] = (pltpu.roll(base, r, 1) if r else base).astype(BF16)
    for m in range(middle_ref.shape[0]):
        base = jnp.zeros((96, 512), F32)
        for u in range(3):
            for v in range(3):
                place = spots(32, lambda source: source + (u * (GROUP + 2) + v) * 32)
                taps = jnp.concatenate([middle_ref[m, u, v, t] for t in range(3)], axis=0)
                base = base + jnp.dot(taps, place, preferred_element_type=F32)
        for r in range(GROUP):
            band = (pltpu.roll(base, 32 * r, 1) if r else base).astype(BF16)
            for t in range(3):
                start = (t * GROUP + r) * 32
                w_middle_ref[m, start : start + 32] = band[32 * t : 32 * t + 32]


def last_table_kernel(last_ref, w_last_ref):
    bands = []
    for r in range(8):
        bands.append(pltpu.roll(last_ref[...], 32 * r, 1) if r else last_ref[...])
    w_last_ref[...] = jnp.concatenate(bands, axis=0).astype(BF16)


def tables(w_first, w_middle, w_last):
    first = w_first.reshape(w_first.shape[0], 54)
    middle = jnp.transpose(w_middle, (0, 3, 4, 5, 1, 2))
    last = jnp.pad(jnp.transpose(w_last, (4, 0, 2, 3, 1)), ((0, 0), (0, 0), (0, 0), (0, 7), (0, 0)))
    last = jnp.pad(last.reshape(6, 960), ((0, 2), (0, 64))).astype(F32)
    pair = call(
        tables_kernel,
        (struct((512, 512), BF16), struct((3, 96 * GROUP, 512), BF16)),
        (first, middle),
    )
    return (*pair, call(last_table_kernel, struct((64, 1024), BF16), (last,))), (first, last)


def swap(blocks, axis):
    return lax.all_to_all(blocks, axis, 0, 0, tiled=True)


def shifted(part, axis, step):
    count = lax.axis_size(axis)
    return lax.ppermute(part, axis, [(i, i + step) for i in range(count) if 0 <= i + step < count])


def nearest(near):
    return shifted(near, "slab", 1), near, shifted(near, "slab", -1)


def near_planes(parts, after=()):
    low, high = call(pack_kernel, (struct((3, 2, 32, 128)),) * 2, parts, after=after)
    return [shifted(low, "slab", 2), *parts, shifted(high, "slab", -2)]


def body(sensitivity, kspace, sampling, prior_image, w_first, w_middle, w_last):
    maps = sensitivity[0]
    len_y, len_z = maps.shape[2:]
    coils, slabs = lax.axis_size("coil"), lax.axis_size("slab")
    at = jnp.stack([lax.axis_index("coil"), lax.axis_index("slab")]).astype(jnp.int32)
    rows, columns = left_table(len_y), right_table(len_z)
    weights, prepared = tables(w_first, w_middle, w_last)

    term = adjoint(sampling, kspace[0], rows, columns, maps, coils)
    rhs_rows, copies = call(
        rows_kernel,
        (struct((64, 128)), struct((coils, 64, 128))),
        (swap(term, "coil"), prior_image),
        after=prepared,
    )
    rhs = swap(copies, "coil")
    near_shape = struct((2, 2, 32, 128))
    term, spectrum, norms, rhs_near = call(
        normal_kernel,
        (struct((coils, 72, 128)), struct((2, 2, len_y, len_z)), struct((8, 128)), near_shape),
        (at, rhs, sampling, maps, rows, columns),
        in_smem=(0,),
    )
    rhs_near = nearest(rhs_near)
    edge_shape = struct((2, 2, SIDE, 128))
    copies, image_rows, head, tail, sums = call(
        image_kernel,
        (struct((coils, 64, 128), BF16), struct((2, 2, 16, 128)), edge_shape, edge_shape, struct((8, 128))),
        (swap(term, "coil"), rhs_rows, norms),
        after=rhs_near,
    )
    before, after = shifted(tail, "coil", 1), shifted(head, "coil", -1)
    rhs_parts = near_planes(rhs_near)
    tiles = call(
        last_kernel,
        struct((coils, 16, 128)),
        (sums, swap(copies, "coil"), spectrum, sampling, maps, rows, columns),
        after=(before, after, rhs_parts[0], rhs_parts[-1]),
    )
    image_near = nearest(call(join_kernel, near_shape, (before, image_rows, after), after=(tiles,)))
    tiles = call(spread_kernel, struct((slabs, 8, 128)), (swap(tiles, "coil"),), after=image_near)
    image_parts = near_planes(image_near)
    last = swap(tiles, "slab")
    scratch = [pltpu.VMEM((12, 144, 256), BF16)]
    scratch += [pltpu.VMEM((10 - 2 * m, (16 - 2 * m) * 32, 256), BF16) for m in range(4)]
    return call(
        functools.partial(denoise_kernel, coils, slabs),
        (struct(prior_image.shape), struct(prior_image.shape)),
        (at, last, *rhs_parts, *image_parts, *weights),
        scratch=scratch,
        in_smem=(0,),
    )


def solution(mesh):
    placed = (
        P("coil", None, "slab", None, None),
        P("coil", None, "slab", None, None),
        P("slab", None, None),
        P(None, "slab", "coil", None),
        P(),
        P(),
        P(),
    )
    return jax.shard_map(
        body,
        mesh=mesh,
        in_specs=placed,
        out_specs=(P(None, "slab", "coil", None), P(None, "slab", "coil", None)),
        check_vma=False,
    )
```

```python
import functools
import math

import jax
import jax.numpy as jnp
import numpy as np
from jax import lax
from jax.experimental import pallas as pl
from jax.experimental.pallas import tpu as pltpu
from jax.sharding import PartitionSpec as P

LAMBDA = 0.5
HALO = 5
STEPS = 32000.0
SIDE = 8
GROUP = 2
F32 = jnp.float32
BF16 = jnp.bfloat16
VMEM_BYTES = 20 * 1024 * 1024


def call(kernel, out_shape, args, scratch=(), in_smem=(), after=()):
    specs = [
        pl.BlockSpec(memory_space=pltpu.SMEM if i in in_smem else pltpu.VMEM) for i in range(len(args))
    ]
    specs += [pl.BlockSpec(memory_space=pl.ANY)] * len(after)
    if after:
        inner_kernel, count = kernel, len(args)

        def kernel(*refs):
            inner_kernel(*refs[:count], *refs[count + len(after) :])

    outs = jax.tree.map(lambda _: pl.BlockSpec(memory_space=pltpu.VMEM), out_shape)
    return pl.pallas_call(
        kernel,
        out_shape=out_shape,
        in_specs=specs,
        out_specs=outs,
        scratch_shapes=list(scratch),
        compiler_params=pltpu.CompilerParams(vmem_limit_bytes=VMEM_BYTES),
    )(*args, *after)


def struct(shape, dtype=F32):
    return jax.ShapeDtypeStruct(shape, dtype)


def halves(table):
    high = table.astype(np.float32).astype(jnp.bfloat16)
    low = (table.astype(np.float32) - high.astype(np.float32)).astype(jnp.bfloat16)
    return high, low


def dft_pair(length):
    positions = np.arange(length)
    angles = 2.0 * math.pi / length * (positions[:, None] * positions[None, :] % length)
    scaling = 1.0 / math.sqrt(length)
    return np.cos(angles) * scaling, scaling * np.sin(angles)


def left_table(length):
    cosine, sine = dft_pair(length)
    parts = [np.concatenate(halves(part), axis=1) for part in (cosine, sine)]
    return np.concatenate(parts, axis=0)


def right_table(length):
    cosine, sine = dft_pair(length)
    return np.concatenate(halves(cosine) + halves(sine), axis=1)


def split(values):
    high = values.astype(BF16)
    low = (values - high.astype(F32)).astype(BF16)
    return high, low


def dft_rows(field, table_ref, sign):
    values = jnp.concatenate(field[0] + field[1], axis=1)
    high, low = split(values)
    size = values.shape[0]
    table_high, table_low = table_ref[:, :size], table_ref[:, size:]
    table = jnp.concatenate([table_high, table_high, table_low], axis=1)
    products = jnp.dot(table, jnp.concatenate([high, low, high], axis=0), preferred_element_type=F32)
    half = values.shape[1] // 2
    cosine, sine = products[:size], products[size:]
    real = cosine[:, :half] - sign * sine[:, half:]
    imag = cosine[:, half:] + sign * sine[:, :half]
    columns = half // 2
    return [[part[:, p * columns : (p + 1) * columns] for p in range(2)] for part in (real, imag)]


def dft_columns(field, table_ref, sign):
    values = by_columns(field)
    high, low = split(values)
    size = table_ref.shape[0]
    cosine_high, cosine_low, sine_high, sine_low = [table_ref[:, i * size : (i + 1) * size] for i in range(4)]

    def block(cosine, sine):
        plus, minus = (sine, -sine) if sign > 0 else (-sine, sine)
        return jnp.concatenate(
            [jnp.concatenate([cosine, plus], axis=1), jnp.concatenate([minus, cosine], axis=1)], axis=0
        )

    table_high = block(cosine_high, sine_high)
    table = jnp.concatenate([table_high, table_high, block(cosine_low, sine_low)], axis=0)
    return from_columns(jnp.dot(jnp.concatenate([high, low, high], axis=1), table, preferred_element_type=F32))


def by_columns(field):
    planes = range(len(field[0]))
    return jnp.concatenate([jnp.concatenate([field[0][p], field[1][p]], axis=1) for p in planes], axis=0)


def from_columns(values):
    rows, columns = values.shape[0] // 2, values.shape[1] // 2
    return [[values[p * rows : (p + 1) * rows, a * columns : (a + 1) * columns] for p in range(2)] for a in range(2)]


def to_float(values):
    return values.astype(jnp.int32).astype(F32)


def to_short(values):
    return jnp.floor(values + 0.5).astype(jnp.int32).astype(jnp.int16)


def exponent_of(largest):
    return jnp.ceil(jnp.log2(jnp.maximum(largest, 1e-30)))


def scales_of(blocks_ref):
    return jnp.exp2(to_float(blocks_ref[:, 64:80, :])[:, 0:1, :]) * (1.0 / STEPS)


def load_image(blocks_ref):
    count, _, columns = blocks_ref.shape
    scales = scales_of(blocks_ref)

    def one(a, p):
        start = (2 * a + p) * 16
        return (to_float(blocks_ref[:, start : start + 16, :]) * scales).reshape(count * 16, columns)

    return [[one(a, p) for p in range(2)] for a in range(2)]


def store_image(blocks_ref, image, extra):
    count, _, columns = blocks_ref.shape
    blocks = [image[a][p].reshape(count, 16, columns) for a in range(2) for p in range(2)]
    largest = jnp.maximum(
        jnp.maximum(jnp.abs(blocks[0]), jnp.abs(blocks[1])), jnp.maximum(jnp.abs(blocks[2]), jnp.abs(blocks[3]))
    )
    largest = jnp.max(jnp.max(largest, axis=1, keepdims=True), axis=2, keepdims=True)
    exponents = exponent_of(largest)
    factors = jnp.exp2(-exponents) * STEPS
    for i in range(4):
        blocks_ref[:, 16 * i : 16 * i + 16, :] = to_short(blocks[i] * factors)
    row = lax.broadcasted_iota(jnp.int32, (count, 16, columns), 1)
    last = jnp.where(row == 0, exponents, extra)
    blocks_ref[:, 64:80, :] = to_short(last)


def store_copies(blocks_ref, rows):
    exponent = exponent_of(jnp.max(jnp.max(jnp.abs(rows), axis=0, keepdims=True), axis=1, keepdims=True))
    shorts = to_short(rows * (jnp.exp2(-exponent) * STEPS))
    tail = to_short(jnp.broadcast_to(exponent, (16, 128)))
    for k in range(blocks_ref.shape[0]):
        blocks_ref[k, 0:64, :] = shorts
        blocks_ref[k, 64:80, :] = tail
    return to_float(shorts) * (jnp.exp2(exponent) * (1.0 / STEPS))


def sum_blocks(blocks_ref):
    scales = scales_of(blocks_ref)
    total = to_float(blocks_ref[0, 0:64, :]) * scales[0]
    for k in range(1, blocks_ref.shape[0]):
        total = total + to_float(blocks_ref[k, 0:64, :]) * scales[k]
    return total


def coil_field(maps_ref, image):
    real = [maps_ref[0, p] * image[0][p] - maps_ref[1, p] * image[1][p] for p in range(2)]
    imag = [maps_ref[0, p] * image[1][p] + maps_ref[1, p] * image[0][p] for p in range(2)]
    return [real, imag]


def coil_term(maps_ref, field):
    real = [maps_ref[0, p] * field[0][p] + maps_ref[1, p] * field[1][p] for p in range(2)]
    imag = [maps_ref[0, p] * field[1][p] - maps_ref[1, p] * field[0][p] for p in range(2)]
    return [real, imag]


def masked(field, mask_ref):
    masks = [mask_ref[p].astype(F32) for p in range(2)]
    return [[field[a][p] * masks[p] for p in range(2)] for a in range(2)]


def inner(first, second):
    return sum(row_sum(first[a][p] * second[a][p]) for a in range(2) for p in range(2))


def row_sum(values):
    folded = jnp.sum(values.reshape(-1, 8, values.shape[-1]), axis=0)
    folded = jnp.sum(folded, axis=0, keepdims=True)
    return folded


def tile_of(rows):
    blank = jnp.zeros((1, 128), F32)
    return jnp.concatenate(list(rows) + [blank] * (8 - len(rows)), axis=0)


def store_near(near_ref, blocks_ref, at):
    count = blocks_ref.shape[0]

    def one(at, start):
        scale = jnp.exp2(to_float(blocks_ref[at, 64:80, :])[0:1]) * (1.0 / STEPS)
        return to_float(blocks_ref[at, start : start + 16, :]) * scale

    for a in range(2):
        for p in range(2):
            start = (2 * a + p) * 16
            near_ref[p, a, 8:24, :] = one(at, start)
            before = one(jnp.maximum(at - 1, 0), start)[8:16]
            after = one(jnp.minimum(at + 1, count - 1), start)[0:8]
            near_ref[p, a, 0:8, :] = jnp.where(at > 0, before, 0.0)
            near_ref[p, a, 24:32, :] = jnp.where(at < count - 1, after, 0.0)


def adjoint_kernel(
    mask_hbm, kspace_hbm, rows_hbm, columns_hbm, maps_hbm, out_ref, mask_ref, kspace_ref, rows_ref, columns_ref, maps_ref, sems
):
    sources = (mask_hbm, kspace_hbm, rows_hbm, columns_hbm, maps_hbm)
    targets = (mask_ref, kspace_ref, rows_ref, columns_ref, maps_ref)
    copies = [pltpu.make_async_copy(src, dst, sems.at[i]) for i, (src, dst) in enumerate(zip(sources, targets))]
    for copy in copies:
        copy.start()
    for copy in copies[:3]:
        copy.wait()
    field = masked([[kspace_ref[a, p] for p in range(2)] for a in range(2)], mask_ref)
    field = dft_rows(field, rows_ref, 1.0)
    copies[3].wait()
    field = dft_columns(field, columns_ref, 1.0)
    copies[4].wait()
    store_image(out_ref, coil_term(maps_ref, field), 0.0)


def adjoint(mask, kspace, rows, columns, maps, coils):
    args = (mask, kspace, rows, columns, maps)
    return pl.pallas_call(
        adjoint_kernel,
        out_shape=struct((coils, 80, 128), jnp.int16),
        in_specs=[pl.BlockSpec(memory_space=pl.ANY)] * len(args),
        out_specs=pl.BlockSpec(memory_space=pltpu.VMEM),
        scratch_shapes=[pltpu.VMEM(arg.shape, arg.dtype) for arg in args] + [pltpu.SemaphoreType.DMA((len(args),))],
        compiler_params=pltpu.CompilerParams(vmem_limit_bytes=60 * 1024 * 1024),
    )(*args)


def rows_kernel(blocks_ref, prior_ref, rows_ref, copies_ref):
    prior = jnp.concatenate([prior_ref[a, p] for a in range(2) for p in range(2)], axis=0)
    rows_ref[...] = store_copies(copies_ref, sum_blocks(blocks_ref) + LAMBDA * prior)


def normal_kernel(
    at_ref, blocks_ref, mask_ref, maps_ref, rows_ref, columns_ref, out_ref, spectrum_ref, tile_ref, near_ref
):
    store_near(near_ref, blocks_ref, at_ref[0])
    image = load_image(blocks_ref)
    field = dft_columns(coil_field(maps_ref, image), columns_ref, -1.0)
    spectrum = masked(dft_rows(field, rows_ref, -1.0), mask_ref)
    for a in range(2):
        for p in range(2):
            spectrum_ref[a, p] = spectrum[a][p]
    field = dft_columns(dft_rows(spectrum, rows_ref, 1.0), columns_ref, 1.0)
    energy = inner(spectrum, spectrum)
    tile_ref[...] = tile_of([inner(image, image), energy])
    coarse = lane_sum(energy)
    level = exponent_of(coarse)
    row = lax.broadcasted_iota(jnp.int32, (1, 16, 128), 1)
    extra = jnp.where(row == 1, level, jnp.exp2(-level) * STEPS * coarse)
    store_image(out_ref, coil_term(maps_ref, field), extra)


def image_kernel(blocks_ref, rhs_rows_ref, tile_ref, copies_ref, sums_ref):
    rhs = rhs_rows_ref[...]
    image = store_copies(copies_ref, sum_blocks(blocks_ref) + LAMBDA * rhs)
    extra = to_float(blocks_ref[:, 64:80, :])
    coarse = jnp.sum(jnp.exp2(extra[:, 1:2, :]) * extra[:, 2:3, :], axis=0) * (1.0 / STEPS)
    norm, energy = tile_ref[0:1, :], tile_ref[1:2, :]
    step = slab_step(lane_sum(norm), coarse)
    residual = rhs - step * image
    share = 1.0 / blocks_ref.shape[0]
    rows = [row_sum(residual * residual), row_sum(residual * rhs), share * norm, energy, share * step]
    sums_ref[...] = tile_of(rows)


def lane_sum(values):
    return jnp.sum(values, axis=-1, keepdims=True)


def slab_step(norm, energy):
    curved = energy + LAMBDA * norm
    return jnp.where(curved > 0.0, norm / jnp.where(curved > 0.0, curved, 1.0), 1.0)


def last_kernel(sums_ref, blocks_ref, spectrum_ref, mask_ref, maps_ref, rows_ref, columns_ref, out_ref):
    step = sums_ref[4:5, :] * float(blocks_ref.shape[0])
    field = dft_columns(coil_field(maps_ref, load_image(blocks_ref)), columns_ref, -1.0)
    spectrum = masked(dft_rows(field, rows_ref, -1.0), mask_ref)
    before = [[spectrum_ref[a, p] for p in range(2)] for a in range(2)]
    spectrum = [[before[a][p] - step * spectrum[a][p] for p in range(2)] for a in range(2)]
    tile = tile_of([inner(spectrum, spectrum), inner(spectrum, before)] + [sums_ref[i : i + 1, :] for i in range(5)])
    for k in range(out_ref.shape[0]):
        out_ref[k, 0:8] = tile
        out_ref[k, 8:] = jnp.zeros((out_ref.shape[1] - 8, 128), F32)


def near_kernel(at_ref, blocks_ref, near_ref):
    store_near(near_ref, blocks_ref, at_ref[0])


def pack_kernel(below_ref, near_ref, above_ref, low_ref, high_ref):
    low_ref[0] = below_ref[1]
    low_ref[1:3] = near_ref[...]
    high_ref[0:2] = near_ref[...]
    high_ref[2] = above_ref[0]


def spread_kernel(tiles_ref, out_ref):
    total = jnp.sum(tiles_ref[:, 0:8, :], axis=0)
    for k in range(out_ref.shape[0]):
        out_ref[k] = total


def final_scales(tiles_ref):
    curve, curve_cross, norm, cross, norm_first, energy_first = [
        lane_sum(tiles_ref[:, i, :]) for i in range(6)
    ]
    step_here = tiles_ref[:, 6, 0:1]

    def over_slabs(values):
        return jnp.sum(values, axis=0, keepdims=True)

    all_norm, all_energy = over_slabs(norm_first), over_slabs(energy_first)
    step_first = all_norm / (all_energy + LAMBDA * all_norm)
    here = step_first / step_here
    rest = 1.0 - here
    curve = over_slabs(here * here * curve + rest * (2.0 * here * curve_cross + rest * energy_first))
    curve_cross = over_slabs(here * curve_cross + rest * energy_first)
    norm = over_slabs(here * here * norm + rest * (2.0 * here * cross + rest * norm_first))
    cross = over_slabs(here * cross + rest * norm_first)
    ratio = norm / all_norm
    curvature = curve + ratio * (2.0 * curve_cross + ratio * all_energy)
    curvature = curvature + LAMBDA * (norm + ratio * (2.0 * cross + ratio * all_norm))
    return step_first, norm / curvature, ratio


def starts_of(rows):
    starts = list(range(0, rows - GROUP + 1, GROUP))
    if starts[-1] + GROUP < rows:
        starts.append(rows - GROUP)
    return starts


def shifted_sum(parts):
    before, here, after = parts
    lane = lax.broadcasted_iota(jnp.int32, before.shape[:1] + (128,), 1)
    outs = []
    for h in range(2):
        cut = slice(128 * h, 128 * (h + 1))
        low = jnp.where(lane > 0, pltpu.roll(before[:, cut], 1, 1), 0.0)
        high = jnp.where(lane < 127, pltpu.roll(after[:, cut], 127, 1), 0.0)
        outs.append(here[:, cut] + low + high)
    return jnp.concatenate(outs, axis=1)


def denoise_kernel(coil_count, slab_count, *refs):
    at_ref, last_ref = refs[:2]
    rhs_refs = refs[2:7]
    image_refs = refs[7:12]
    w_first_ref, w_middle_ref, w_last_ref, solution_ref, refined_ref = refs[12:17]
    features_ref = refs[17]
    hidden_refs = refs[18:]
    coil_at = at_ref[0]
    slab_at = at_ref[1]

    step_first, step_last, ratio = final_scales(last_ref)
    scale_rhs = step_first + step_last * ratio

    lane = lax.broadcasted_iota(jnp.int32, (48, 128), 1)
    plane = 0
    brick = None
    for rhs_ref, image_ref in zip(rhs_refs, image_refs):
        for p in range(rhs_ref.shape[0]):
            full = []
            for a in range(2):
                rhs = rhs_ref[p, a]
                full.append(scale_rhs * rhs + step_last * (rhs - step_first * image_ref[p, a]))
            if 5 <= plane < 7:
                for a in range(2):
                    solution_ref[a, plane - 5] = full[a][8:24]
            for h in range(2):
                window = jnp.concatenate([f[8 * h : 8 * h + 24] for f in full], axis=0)
                cut = slice(128 * h, 128 * (h + 1))
                low = jnp.where(lane > 0, pltpu.roll(window, 1, 1), 0.0)
                high = jnp.where(lane < 127, pltpu.roll(window, 127, 1), 0.0)
                features_ref[plane, 0:48, cut] = low.astype(BF16)
                features_ref[plane, 48:96, cut] = window.astype(BF16)
                features_ref[plane, 96:144, cut] = high.astype(BF16)
            plane += 1

    def outside(out_ref, depth):
        planes, cells, _ = out_ref.shape
        extra = 4 - depth
        first = 2 * slab_at - extra

        last_plane = 2 * slab_at + 1 + extra
        edge = (coil_at == 0) | (coil_at == coil_count - 1) | (first < 0) | (last_plane >= 2 * slab_count)

        @pl.when(edge)
        def _():
            blank = jnp.zeros((planes, extra * 32, 128), BF16)

            @pl.when(coil_at == 0)
            def _():
                out_ref[:, 0 : extra * 32, 0:128] = blank

            @pl.when(coil_at == coil_count - 1)
            def _():
                out_ref[:, cells - extra * 32 : cells, 128:256] = blank

            for p in list(range(extra)) + list(range(planes - extra, planes)):

                @pl.when((first + p < 0) | (first + p >= 2 * slab_count))
                def _():
                    out_ref[p] = jnp.zeros(out_ref.shape[1:], BF16)

    first_out = hidden_refs[0]

    for p in range(first_out.shape[0]):
        taps = jnp.concatenate([features_ref[p + u] for u in range(3)], axis=0)
        values = jnp.dot(w_first_ref[:, :432], taps, preferred_element_type=F32)
        first_out[p] = jnp.maximum(values, 0.0).astype(BF16)
    outside(first_out, 0)

    for m in range(len(hidden_refs) - 1):
        in_ref, out_ref = hidden_refs[m], hidden_refs[m + 1]
        starts = starts_of(out_ref.shape[1] // 32)

        cells = GROUP * 32
        for p in range(out_ref.shape[0]):
            for start in starts:
                rows = slice(start * 32, (start + GROUP + 2) * 32)
                taps = jnp.concatenate([in_ref[p + u, rows] for u in range(3)], axis=0)
                sums = jnp.dot(w_middle_ref[m, :, : (GROUP + 2) * 96], taps, preferred_element_type=F32)
                values = shifted_sum([sums[t * cells : (t + 1) * cells] for t in range(3)])
                out_ref[p, start * 32 : start * 32 + cells] = jnp.maximum(values, 0.0).astype(BF16)
        outside(out_ref, m + 1)

    in_ref = hidden_refs[-1]
    for p in range(2):
        taps = jnp.concatenate([in_ref[p + u] for u in range(3)], axis=0)
        sums = jnp.dot(w_last_ref[:, :960], taps, preferred_element_type=F32)
        lane = lax.broadcasted_iota(jnp.int32, (64, 128), 1)
        for h in range(2):
            part = sums[:, 128 * h : 128 * (h + 1)]
            low = jnp.where(lane > 0, pltpu.roll(part, 1, 1), 0.0)
            high = jnp.where(lane < 127, pltpu.roll(part, 127, 1), 0.0)
            for a in range(2):
                rows = []
                for r in range(8):
                    at = 8 * r + a
                    rows.append(low[at : at + 1] + part[at + 2 : at + 3] + high[at + 4 : at + 5])
                piece = jnp.concatenate(rows, axis=0)
                refined_ref[a, p, 8 * h : 8 * h + 8] = solution_ref[a, p, 8 * h : 8 * h + 8] + piece


def tables_kernel(first_ref, middle_ref, w_first_ref, w_middle_ref):
    def spots(size, target, count=512):
        column = lax.broadcasted_iota(jnp.int32, (size, count), 1)
        return jnp.where(column == target(lax.broadcasted_iota(jnp.int32, (size, count), 0)), 1.0, 0.0).astype(BF16)

    def first_target(source):
        channel, u, v, t = source // 27, source // 9 % 3, source // 3 % 3, source % 3
        return ((u * 3 + t) * 2 + channel) * 24 + SIDE - HALO + v

    base = jnp.dot(first_ref[...], spots(54, first_target), preferred_element_type=F32)
    for r in range(16):
        w_first_ref[32 * r : 32 * r + 32] = (pltpu.roll(base, r, 1) if r else base).astype(BF16)
    for m in range(middle_ref.shape[0]):
        base = jnp.zeros((96, 512), F32)
        for u in range(3):
            for v in range(3):
                place = spots(32, lambda source: source + (u * (GROUP + 2) + v) * 32)
                taps = jnp.concatenate([middle_ref[m, u, v, t] for t in range(3)], axis=0)
                base = base + jnp.dot(taps, place, preferred_element_type=F32)
        for r in range(GROUP):
            band = (pltpu.roll(base, 32 * r, 1) if r else base).astype(BF16)
            for t in range(3):
                start = (t * GROUP + r) * 32
                w_middle_ref[m, start : start + 32] = band[32 * t : 32 * t + 32]


def last_table_kernel(last_ref, w_last_ref):
    bands = []
    for r in range(8):
        bands.append(pltpu.roll(last_ref[...], 32 * r, 1) if r else last_ref[...])
    w_last_ref[...] = jnp.concatenate(bands, axis=0).astype(BF16)


def tables(w_first, w_middle, w_last):
    first = w_first.reshape(w_first.shape[0], 54)
    middle = jnp.transpose(w_middle, (0, 3, 4, 5, 1, 2))
    last = jnp.pad(jnp.transpose(w_last, (4, 0, 2, 3, 1)), ((0, 0), (0, 0), (0, 0), (0, 7), (0, 0)))
    last = jnp.pad(last.reshape(6, 960), ((0, 2), (0, 64))).astype(F32)
    pair = call(
        tables_kernel,
        (struct((512, 512), BF16), struct((3, 96 * GROUP, 512), BF16)),
        (first, middle),
    )
    return (*pair, call(last_table_kernel, struct((64, 1024), BF16), (last,))), (first, last)


def swap(blocks, axis):
    return lax.all_to_all(blocks, axis, 0, 0, tiled=True)


def shifted(part, axis, step):
    count = lax.axis_size(axis)
    return lax.ppermute(part, axis, [(i, i + step) for i in range(count) if 0 <= i + step < count])


def near_planes(near):
    below, above = shifted(near, "slab", 1), shifted(near, "slab", -1)
    low, high = call(pack_kernel, (struct((3, 2, 32, 128)),) * 2, (below, near, above))
    return [shifted(low, "slab", 2), below, near, above, shifted(high, "slab", -2)]


def body(sensitivity, kspace, sampling, prior_image, w_first, w_middle, w_last):
    maps = sensitivity[0]
    len_y, len_z = maps.shape[2:]
    coils, slabs = lax.axis_size("coil"), lax.axis_size("slab")
    at = jnp.stack([lax.axis_index("coil"), lax.axis_index("slab")]).astype(jnp.int32)
    rows, columns = left_table(len_y), right_table(len_z)
    weights, prepared = tables(w_first, w_middle, w_last)

    term = adjoint(sampling, kspace[0], rows, columns, maps, coils)
    rhs_rows, copies = call(
        rows_kernel,
        (struct((64, 128)), struct((coils, 80, 128), jnp.int16)),
        (swap(term, "coil"), prior_image),
        after=prepared,
    )
    rhs = swap(copies, "coil")
    near_shape = struct((2, 2, 32, 128))
    term, spectrum, norms, rhs_near = call(
        normal_kernel,
        (
            struct((coils, 80, 128), jnp.int16),
            struct((2, 2, len_y, len_z)),
            struct((8, 128)),
            near_shape,
        ),
        (at, rhs, sampling, maps, rows, columns),
        in_smem=(0,),
    )
    rhs_parts = near_planes(rhs_near)
    copies, sums = call(
        image_kernel,
        (struct((coils, 80, 128), jnp.int16), struct((8, 128))),
        (swap(term, "coil"), rhs_rows, norms),
        after=rhs_parts,
    )
    image = swap(copies, "coil")
    tiles = call(
        last_kernel,
        struct((coils, 16, 128)),
        (sums, image, spectrum, sampling, maps, rows, columns),
        after=weights[2:],
    )
    image_parts = near_planes(call(near_kernel, near_shape, (at, image), in_smem=(0,), after=(tiles,)))
    tiles = call(spread_kernel, struct((slabs, 8, 128)), (swap(tiles, "coil"),), after=(image_parts[1], image_parts[3]))
    last = swap(tiles, "slab")
    scratch = [pltpu.VMEM((12, 144, 256), BF16)]
    scratch += [pltpu.VMEM((10 - 2 * m, (16 - 2 * m) * 32, 256), BF16) for m in range(4)]
    return call(
        functools.partial(denoise_kernel, coils, slabs),
        (struct(prior_image.shape), struct(prior_image.shape)),
        (at, last, *rhs_parts, *image_parts, *weights),
        scratch=scratch,
        in_smem=(0,),
    )


def solution(mesh):
    placed = (
        P("coil", None, "slab", None, None),
        P("coil", None, "slab", None, None),
        P("slab", None, None),
        P(None, "slab", "coil", None),
        P(),
        P(),
        P(),
    )
    return jax.shard_map(
        body,
        mesh=mesh,
        in_specs=placed,
        out_specs=(P(None, "slab", "coil", None), P(None, "slab", "coil", None)),
        check_vma=False,
    )
```

```python
import functools
import math

import jax
import jax.numpy as jnp
import numpy as np
from jax import lax
from jax.experimental import pallas as pl
from jax.experimental.pallas import tpu as pltpu
from jax.sharding import PartitionSpec as P

LAMBDA = 0.5
HALO = 5
STEPS = 32000.0
FINE = 256.0
SIDE = 8
GROUP = 2
F32 = jnp.float32
BF16 = jnp.bfloat16
VMEM_BYTES = 20 * 1024 * 1024


def call(kernel, out_shape, args, scratch=(), in_smem=(), after=()):
    specs = [
        pl.BlockSpec(memory_space=pltpu.SMEM if i in in_smem else pltpu.VMEM) for i in range(len(args))
    ]
    specs += [pl.BlockSpec(memory_space=pl.ANY)] * len(after)
    if after:
        inner_kernel, count = kernel, len(args)

        def kernel(*refs):
            inner_kernel(*refs[:count], *refs[count + len(after) :])

    outs = jax.tree.map(lambda _: pl.BlockSpec(memory_space=pltpu.VMEM), out_shape)
    return pl.pallas_call(
        kernel,
        out_shape=out_shape,
        in_specs=specs,
        out_specs=outs,
        scratch_shapes=list(scratch),
        compiler_params=pltpu.CompilerParams(vmem_limit_bytes=VMEM_BYTES),
    )(*args, *after)


def struct(shape, dtype=F32):
    return jax.ShapeDtypeStruct(shape, dtype)


def halves(table):
    high = table.astype(np.float32).astype(jnp.bfloat16)
    low = (table.astype(np.float32) - high.astype(np.float32)).astype(jnp.bfloat16)
    return high, low


def dft_pair(length):
    positions = np.arange(length)
    angles = 2.0 * math.pi / length * (positions[:, None] * positions[None, :] % length)
    scaling = 1.0 / math.sqrt(length)
    return np.cos(angles) * scaling, scaling * np.sin(angles)


def left_table(length):
    cosine, sine = dft_pair(length)
    parts = [np.concatenate(halves(part), axis=1) for part in (cosine, sine)]
    return np.concatenate(parts, axis=0)


def right_table(length):
    cosine, sine = dft_pair(length)
    return np.concatenate(halves(cosine) + halves(sine), axis=1)


def split(values):
    high = values.astype(BF16)
    low = (values - high.astype(F32)).astype(BF16)
    return high, low


def dft_rows(field, table_ref, sign):
    values = jnp.concatenate(field[0] + field[1], axis=1)
    high, low = split(values)
    size = values.shape[0]
    table_high, table_low = table_ref[:, :size], table_ref[:, size:]
    table = jnp.concatenate([table_high, table_high, table_low], axis=1)
    products = jnp.dot(table, jnp.concatenate([high, low, high], axis=0), preferred_element_type=F32)
    half = values.shape[1] // 2
    cosine, sine = products[:size], products[size:]
    real = cosine[:, :half] - sign * sine[:, half:]
    imag = cosine[:, half:] + sign * sine[:, :half]
    columns = half // 2
    return [[part[:, p * columns : (p + 1) * columns] for p in range(2)] for part in (real, imag)]


def dft_columns(field, table_ref, sign):
    values = by_columns(field)
    high, low = split(values)
    size = table_ref.shape[0]
    cosine_high, cosine_low, sine_high, sine_low = [table_ref[:, i * size : (i + 1) * size] for i in range(4)]

    def block(cosine, sine):
        plus, minus = (sine, -sine) if sign > 0 else (-sine, sine)
        return jnp.concatenate(
            [jnp.concatenate([cosine, plus], axis=1), jnp.concatenate([minus, cosine], axis=1)], axis=0
        )

    table_high = block(cosine_high, sine_high)
    table = jnp.concatenate([table_high, table_high, block(cosine_low, sine_low)], axis=0)
    return from_columns(jnp.dot(jnp.concatenate([high, low, high], axis=1), table, preferred_element_type=F32))


def by_columns(field):
    planes = range(len(field[0]))
    return jnp.concatenate([jnp.concatenate([field[0][p], field[1][p]], axis=1) for p in planes], axis=0)


def from_columns(values):
    rows, columns = values.shape[0] // 2, values.shape[1] // 2
    return [[values[p * rows : (p + 1) * rows, a * columns : (a + 1) * columns] for p in range(2)] for a in range(2)]


def to_float(values):
    return values.astype(jnp.int32).astype(F32)


def to_short(values):
    return jnp.floor(values + 0.5).astype(jnp.int32).astype(jnp.int16)


def exponent_of(largest):
    return jnp.ceil(jnp.log2(jnp.maximum(largest, 1e-30)) * FINE) * (1.0 / FINE)


def scales_of(blocks_ref):
    return jnp.exp2(to_float(blocks_ref[:, 64:80, :])[:, 0:1, :] * (1.0 / FINE)) * (1.0 / STEPS)


def load_image(blocks_ref):
    count, _, columns = blocks_ref.shape
    scales = scales_of(blocks_ref)

    def one(a, p):
        start = (2 * a + p) * 16
        return (to_float(blocks_ref[:, start : start + 16, :]) * scales).reshape(count * 16, columns)

    return [[one(a, p) for p in range(2)] for a in range(2)]


def store_image(blocks_ref, image, extra):
    count, _, columns = blocks_ref.shape
    blocks = [image[a][p].reshape(count, 16, columns) for a in range(2) for p in range(2)]
    largest = jnp.maximum(
        jnp.maximum(jnp.abs(blocks[0]), jnp.abs(blocks[1])), jnp.maximum(jnp.abs(blocks[2]), jnp.abs(blocks[3]))
    )
    largest = jnp.max(jnp.max(largest, axis=1, keepdims=True), axis=2, keepdims=True)
    exponents = exponent_of(largest)
    factors = jnp.exp2(-exponents) * STEPS
    for i in range(4):
        blocks_ref[:, 16 * i : 16 * i + 16, :] = to_short(blocks[i] * factors)
    row = lax.broadcasted_iota(jnp.int32, (count, 16, columns), 1)
    last = jnp.where(row == 0, exponents * FINE, extra)
    blocks_ref[:, 64:80, :] = to_short(last)


def store_copies(blocks_ref, rows):
    exponent = exponent_of(jnp.max(jnp.max(jnp.abs(rows), axis=0, keepdims=True), axis=1, keepdims=True))
    shorts = to_short(rows * (jnp.exp2(-exponent) * STEPS))
    tail = to_short(jnp.broadcast_to(exponent * FINE, (16, 128)))
    for k in range(blocks_ref.shape[0]):
        blocks_ref[k, 0:64, :] = shorts
        blocks_ref[k, 64:80, :] = tail
    return to_float(shorts) * (jnp.exp2(exponent) * (1.0 / STEPS))


def sum_blocks(blocks_ref):
    scales = scales_of(blocks_ref)
    total = to_float(blocks_ref[0, 0:64, :]) * scales[0]
    for k in range(1, blocks_ref.shape[0]):
        total = total + to_float(blocks_ref[k, 0:64, :]) * scales[k]
    return total


def coil_field(maps_ref, image):
    real = [maps_ref[0, p] * image[0][p] - maps_ref[1, p] * image[1][p] for p in range(2)]
    imag = [maps_ref[0, p] * image[1][p] + maps_ref[1, p] * image[0][p] for p in range(2)]
    return [real, imag]


def coil_term(maps_ref, field):
    real = [maps_ref[0, p] * field[0][p] + maps_ref[1, p] * field[1][p] for p in range(2)]
    imag = [maps_ref[0, p] * field[1][p] - maps_ref[1, p] * field[0][p] for p in range(2)]
    return [real, imag]


def masked(field, mask_ref):
    masks = [mask_ref[p].astype(F32) for p in range(2)]
    return [[field[a][p] * masks[p] for p in range(2)] for a in range(2)]


def inner(first, second):
    return sum(row_sum(first[a][p] * second[a][p]) for a in range(2) for p in range(2))


def row_sum(values):
    folded = jnp.sum(values.reshape(-1, 8, values.shape[-1]), axis=0)
    folded = jnp.sum(folded, axis=0, keepdims=True)
    return folded


def tile_of(rows):
    blank = jnp.zeros((1, 128), F32)
    return jnp.concatenate(list(rows) + [blank] * (8 - len(rows)), axis=0)


def store_near(near_ref, blocks_ref, at):
    count = blocks_ref.shape[0]

    def one(at, start):
        scale = jnp.exp2(to_float(blocks_ref[at, 64:80, :])[0:1] * (1.0 / FINE)) * (1.0 / STEPS)
        return to_float(blocks_ref[at, start : start + 16, :]) * scale

    for a in range(2):
        for p in range(2):
            start = (2 * a + p) * 16
            near_ref[p, a, 8:24, :] = one(at, start)
            before = one(jnp.maximum(at - 1, 0), start)[8:16]
            after = one(jnp.minimum(at + 1, count - 1), start)[0:8]
            near_ref[p, a, 0:8, :] = jnp.where(at > 0, before, 0.0)
            near_ref[p, a, 24:32, :] = jnp.where(at < count - 1, after, 0.0)


def adjoint_kernel(
    mask_hbm, kspace_hbm, rows_hbm, columns_hbm, maps_hbm, out_ref, mask_ref, kspace_ref, rows_ref, columns_ref, maps_ref, sems
):
    sources = (mask_hbm, kspace_hbm, rows_hbm, columns_hbm, maps_hbm)
    targets = (mask_ref, kspace_ref, rows_ref, columns_ref, maps_ref)
    copies = [pltpu.make_async_copy(src, dst, sems.at[i]) for i, (src, dst) in enumerate(zip(sources, targets))]
    for copy in copies:
        copy.start()
    for copy in copies[:3]:
        copy.wait()
    field = masked([[kspace_ref[a, p] for p in range(2)] for a in range(2)], mask_ref)
    field = dft_rows(field, rows_ref, 1.0)
    copies[3].wait()
    field = dft_columns(field, columns_ref, 1.0)
    copies[4].wait()
    store_image(out_ref, coil_term(maps_ref, field), 0.0)


def adjoint(mask, kspace, rows, columns, maps, coils):
    args = (mask, kspace, rows, columns, maps)
    return pl.pallas_call(
        adjoint_kernel,
        out_shape=struct((coils, 80, 128), jnp.int16),
        in_specs=[pl.BlockSpec(memory_space=pl.ANY)] * len(args),
        out_specs=pl.BlockSpec(memory_space=pltpu.VMEM),
        scratch_shapes=[pltpu.VMEM(arg.shape, arg.dtype) for arg in args] + [pltpu.SemaphoreType.DMA((len(args),))],
        compiler_params=pltpu.CompilerParams(vmem_limit_bytes=60 * 1024 * 1024),
    )(*args)


def rows_kernel(blocks_ref, prior_ref, rows_ref, copies_ref):
    prior = jnp.concatenate([prior_ref[a, p] for a in range(2) for p in range(2)], axis=0)
    rows_ref[...] = store_copies(copies_ref, sum_blocks(blocks_ref) + LAMBDA * prior)


def normal_kernel(
    at_ref, blocks_ref, mask_ref, maps_ref, rows_ref, columns_ref, out_ref, spectrum_ref, tile_ref, near_ref
):
    store_near(near_ref, blocks_ref, at_ref[0])
    image = load_image(blocks_ref)
    field = dft_columns(coil_field(maps_ref, image), columns_ref, -1.0)
    spectrum = masked(dft_rows(field, rows_ref, -1.0), mask_ref)
    for a in range(2):
        for p in range(2):
            spectrum_ref[a, p] = spectrum[a][p]
    field = dft_columns(dft_rows(spectrum, rows_ref, 1.0), columns_ref, 1.0)
    energy = inner(spectrum, spectrum)
    tile_ref[...] = tile_of([inner(image, image), energy])
    coarse = lane_sum(energy)
    level = exponent_of(coarse)
    row = lax.broadcasted_iota(jnp.int32, (1, 16, 128), 1)
    extra = jnp.where(row == 1, level * FINE, jnp.exp2(-level) * STEPS * coarse)
    store_image(out_ref, coil_term(maps_ref, field), extra)


def image_kernel(blocks_ref, rhs_rows_ref, tile_ref, copies_ref, sums_ref):
    rhs = rhs_rows_ref[...]
    image = store_copies(copies_ref, sum_blocks(blocks_ref) + LAMBDA * rhs)
    extra = to_float(blocks_ref[:, 64:80, :])
    coarse = jnp.sum(jnp.exp2(extra[:, 1:2, :] * (1.0 / FINE)) * extra[:, 2:3, :], axis=0) * (1.0 / STEPS)
    norm, energy = tile_ref[0:1, :], tile_ref[1:2, :]
    step = slab_step(lane_sum(norm), coarse)
    residual = rhs - step * image
    share = 1.0 / blocks_ref.shape[0]
    rows = [row_sum(residual * residual), row_sum(residual * rhs), share * norm, energy, share * step]
    sums_ref[...] = tile_of(rows)


def lane_sum(values):
    return jnp.sum(values, axis=-1, keepdims=True)


def slab_step(norm, energy):
    curved = energy + LAMBDA * norm
    return jnp.where(curved > 0.0, norm / jnp.where(curved > 0.0, curved, 1.0), 1.0)


def last_kernel(sums_ref, blocks_ref, spectrum_ref, mask_ref, maps_ref, rows_ref, columns_ref, out_ref):
    step = sums_ref[4:5, :] * float(blocks_ref.shape[0])
    field = dft_columns(coil_field(maps_ref, load_image(blocks_ref)), columns_ref, -1.0)
    spectrum = masked(dft_rows(field, rows_ref, -1.0), mask_ref)
    before = [[spectrum_ref[a, p] for p in range(2)] for a in range(2)]
    spectrum = [[before[a][p] - step * spectrum[a][p] for p in range(2)] for a in range(2)]
    tile = tile_of([inner(spectrum, spectrum), inner(spectrum, before)] + [sums_ref[i : i + 1, :] for i in range(5)])
    for k in range(out_ref.shape[0]):
        out_ref[k, 0:8] = tile
        out_ref[k, 8:] = jnp.zeros((out_ref.shape[1] - 8, 128), F32)


def near_kernel(at_ref, blocks_ref, near_ref):
    store_near(near_ref, blocks_ref, at_ref[0])


def pack_kernel(below_ref, near_ref, above_ref, low_ref, high_ref):
    low_ref[0] = below_ref[1]
    low_ref[1:3] = near_ref[...]
    high_ref[0:2] = near_ref[...]
    high_ref[2] = above_ref[0]


def spread_kernel(tiles_ref, out_ref):
    total = jnp.sum(tiles_ref[:, 0:8, :], axis=0)
    for k in range(out_ref.shape[0]):
        out_ref[k] = total


def final_scales(tiles_ref):
    curve, curve_cross, norm, cross, norm_first, energy_first = [
        lane_sum(tiles_ref[:, i, :]) for i in range(6)
    ]
    step_here = tiles_ref[:, 6, 0:1]

    def over_slabs(values):
        return jnp.sum(values, axis=0, keepdims=True)

    all_norm, all_energy = over_slabs(norm_first), over_slabs(energy_first)
    step_first = all_norm / (all_energy + LAMBDA * all_norm)
    here = step_first / step_here
    rest = 1.0 - here
    curve = over_slabs(here * here * curve + rest * (2.0 * here * curve_cross + rest * energy_first))
    curve_cross = over_slabs(here * curve_cross + rest * energy_first)
    norm = over_slabs(here * here * norm + rest * (2.0 * here * cross + rest * norm_first))
    cross = over_slabs(here * cross + rest * norm_first)
    ratio = norm / all_norm
    curvature = curve + ratio * (2.0 * curve_cross + ratio * all_energy)
    curvature = curvature + LAMBDA * (norm + ratio * (2.0 * cross + ratio * all_norm))
    return step_first, norm / curvature, ratio


def starts_of(rows):
    starts = list(range(0, rows - GROUP + 1, GROUP))
    if starts[-1] + GROUP < rows:
        starts.append(rows - GROUP)
    return starts


def shifted_sum(parts):
    before, here, after = parts
    lane = lax.broadcasted_iota(jnp.int32, before.shape[:1] + (128,), 1)
    outs = []
    for h in range(2):
        cut = slice(128 * h, 128 * (h + 1))
        low = jnp.where(lane > 0, pltpu.roll(before[:, cut], 1, 1), 0.0)
        high = jnp.where(lane < 127, pltpu.roll(after[:, cut], 127, 1), 0.0)
        outs.append(here[:, cut] + low + high)
    return jnp.concatenate(outs, axis=1)


def denoise_kernel(coil_count, slab_count, *refs):
    at_ref, last_ref = refs[:2]
    rhs_refs = refs[2:7]
    image_refs = refs[7:12]
    w_first_ref, w_middle_ref, w_last_ref, solution_ref, refined_ref = refs[12:17]
    features_ref = refs[17]
    hidden_refs = refs[18:]
    coil_at = at_ref[0]
    slab_at = at_ref[1]

    step_first, step_last, ratio = final_scales(last_ref)
    scale_rhs = step_first + step_last * ratio

    lane = lax.broadcasted_iota(jnp.int32, (48, 128), 1)
    plane = 0
    brick = None
    for rhs_ref, image_ref in zip(rhs_refs, image_refs):
        for p in range(rhs_ref.shape[0]):
            full = []
            for a in range(2):
                rhs = rhs_ref[p, a]
                full.append(scale_rhs * rhs + step_last * (rhs - step_first * image_ref[p, a]))
            if 5 <= plane < 7:
                for a in range(2):
                    solution_ref[a, plane - 5] = full[a][8:24]
            for h in range(2):
                window = jnp.concatenate([f[8 * h : 8 * h + 24] for f in full], axis=0)
                cut = slice(128 * h, 128 * (h + 1))
                low = jnp.where(lane > 0, pltpu.roll(window, 1, 1), 0.0)
                high = jnp.where(lane < 127, pltpu.roll(window, 127, 1), 0.0)
                features_ref[plane, 0:48, cut] = low.astype(BF16)
                features_ref[plane, 48:96, cut] = window.astype(BF16)
                features_ref[plane, 96:144, cut] = high.astype(BF16)
            plane += 1

    def outside(out_ref, depth):
        planes, cells, _ = out_ref.shape
        extra = 4 - depth
        first = 2 * slab_at - extra

        last_plane = 2 * slab_at + 1 + extra
        edge = (coil_at == 0) | (coil_at == coil_count - 1) | (first < 0) | (last_plane >= 2 * slab_count)

        @pl.when(edge)
        def _():
            blank = jnp.zeros((planes, extra * 32, 128), BF16)

            @pl.when(coil_at == 0)
            def _():
                out_ref[:, 0 : extra * 32, 0:128] = blank

            @pl.when(coil_at == coil_count - 1)
            def _():
                out_ref[:, cells - extra * 32 : cells, 128:256] = blank

            for p in list(range(extra)) + list(range(planes - extra, planes)):

                @pl.when((first + p < 0) | (first + p >= 2 * slab_count))
                def _():
                    out_ref[p] = jnp.zeros(out_ref.shape[1:], BF16)

    first_out = hidden_refs[0]

    for p in range(first_out.shape[0]):
        taps = jnp.concatenate([features_ref[p + u] for u in range(3)], axis=0)
        values = jnp.dot(w_first_ref[:, :432], taps, preferred_element_type=F32)
        first_out[p] = jnp.maximum(values, 0.0).astype(BF16)
    outside(first_out, 0)

    for m in range(len(hidden_refs) - 1):
        in_ref, out_ref = hidden_refs[m], hidden_refs[m + 1]
        starts = starts_of(out_ref.shape[1] // 32)

        cells = GROUP * 32
        for p in range(out_ref.shape[0]):
            for start in starts:
                rows = slice(start * 32, (start + GROUP + 2) * 32)
                taps = jnp.concatenate([in_ref[p + u, rows] for u in range(3)], axis=0)
                sums = jnp.dot(w_middle_ref[m, :, : (GROUP + 2) * 96], taps, preferred_element_type=F32)
                values = shifted_sum([sums[t * cells : (t + 1) * cells] for t in range(3)])
                out_ref[p, start * 32 : start * 32 + cells] = jnp.maximum(values, 0.0).astype(BF16)
        outside(out_ref, m + 1)

    in_ref = hidden_refs[-1]
    for p in range(2):
        taps = jnp.concatenate([in_ref[p + u] for u in range(3)], axis=0)
        sums = jnp.dot(w_last_ref[:, :960], taps, preferred_element_type=F32)
        lane = lax.broadcasted_iota(jnp.int32, (64, 128), 1)
        for h in range(2):
            part = sums[:, 128 * h : 128 * (h + 1)]
            low = jnp.where(lane > 0, pltpu.roll(part, 1, 1), 0.0)
            high = jnp.where(lane < 127, pltpu.roll(part, 127, 1), 0.0)
            for a in range(2):
                rows = []
                for r in range(8):
                    at = 8 * r + a
                    rows.append(low[at : at + 1] + part[at + 2 : at + 3] + high[at + 4 : at + 5])
                piece = jnp.concatenate(rows, axis=0)
                refined_ref[a, p, 8 * h : 8 * h + 8] = solution_ref[a, p, 8 * h : 8 * h + 8] + piece


def tables_kernel(first_ref, middle_ref, w_first_ref, w_middle_ref):
    def spots(size, target, count=512):
        column = lax.broadcasted_iota(jnp.int32, (size, count), 1)
        return jnp.where(column == target(lax.broadcasted_iota(jnp.int32, (size, count), 0)), 1.0, 0.0).astype(BF16)

    def first_target(source):
        channel, u, v, t = source // 27, source // 9 % 3, source // 3 % 3, source % 3
        return ((u * 3 + t) * 2 + channel) * 24 + SIDE - HALO + v

    base = jnp.dot(first_ref[...], spots(54, first_target), preferred_element_type=F32)
    for r in range(16):
        w_first_ref[32 * r : 32 * r + 32] = (pltpu.roll(base, r, 1) if r else base).astype(BF16)
    for m in range(middle_ref.shape[0]):
        base = jnp.zeros((96, 512), F32)
        for u in range(3):
            for v in range(3):
                place = spots(32, lambda source: source + (u * (GROUP + 2) + v) * 32)
                taps = jnp.concatenate([middle_ref[m, u, v, t] for t in range(3)], axis=0)
                base = base + jnp.dot(taps, place, preferred_element_type=F32)
        for r in range(GROUP):
            band = (pltpu.roll(base, 32 * r, 1) if r else base).astype(BF16)
            for t in range(3):
                start = (t * GROUP + r) * 32
                w_middle_ref[m, start : start + 32] = band[32 * t : 32 * t + 32]


def last_table_kernel(last_ref, w_last_ref):
    bands = []
    for r in range(8):
        bands.append(pltpu.roll(last_ref[...], 32 * r, 1) if r else last_ref[...])
    w_last_ref[...] = jnp.concatenate(bands, axis=0).astype(BF16)


def tables(w_first, w_middle, w_last):
    first = w_first.reshape(w_first.shape[0], 54)
    middle = jnp.transpose(w_middle, (0, 3, 4, 5, 1, 2))
    last = jnp.pad(jnp.transpose(w_last, (4, 0, 2, 3, 1)), ((0, 0), (0, 0), (0, 0), (0, 7), (0, 0)))
    last = jnp.pad(last.reshape(6, 960), ((0, 2), (0, 64))).astype(F32)
    pair = call(
        tables_kernel,
        (struct((512, 512), BF16), struct((3, 96 * GROUP, 512), BF16)),
        (first, middle),
    )
    return (*pair, call(last_table_kernel, struct((64, 1024), BF16), (last,))), (first, last)


def swap(blocks, axis):
    return lax.all_to_all(blocks, axis, 0, 0, tiled=True)


def shifted(part, axis, step):
    count = lax.axis_size(axis)
    return lax.ppermute(part, axis, [(i, i + step) for i in range(count) if 0 <= i + step < count])


def near_planes(near):
    below, above = shifted(near, "slab", 1), shifted(near, "slab", -1)
    low, high = call(pack_kernel, (struct((3, 2, 32, 128)),) * 2, (below, near, above))
    return [shifted(low, "slab", 2), below, near, above, shifted(high, "slab", -2)]


def body(sensitivity, kspace, sampling, prior_image, w_first, w_middle, w_last):
    maps = sensitivity[0]
    len_y, len_z = maps.shape[2:]
    coils, slabs = lax.axis_size("coil"), lax.axis_size("slab")
    at = jnp.stack([lax.axis_index("coil"), lax.axis_index("slab")]).astype(jnp.int32)
    rows, columns = left_table(len_y), right_table(len_z)
    weights, prepared = tables(w_first, w_middle, w_last)

    term = adjoint(sampling, kspace[0], rows, columns, maps, coils)
    rhs_rows, copies = call(
        rows_kernel,
        (struct((64, 128)), struct((coils, 80, 128), jnp.int16)),
        (swap(term, "coil"), prior_image),
        after=prepared,
    )
    rhs = swap(copies, "coil")
    near_shape = struct((2, 2, 32, 128))
    term, spectrum, norms, rhs_near = call(
        normal_kernel,
        (
            struct((coils, 80, 128), jnp.int16),
            struct((2, 2, len_y, len_z)),
            struct((8, 128)),
            near_shape,
        ),
        (at, rhs, sampling, maps, rows, columns),
        in_smem=(0,),
    )
    rhs_parts = near_planes(rhs_near)
    copies, sums = call(
        image_kernel,
        (struct((coils, 80, 128), jnp.int16), struct((8, 128))),
        (swap(term, "coil"), rhs_rows, norms),
        after=(rhs_parts[1], rhs_parts[3]),
    )
    image = swap(copies, "coil")
    tiles = call(
        last_kernel,
        struct((coils, 16, 128)),
        (sums, image, spectrum, sampling, maps, rows, columns),
        after=(*weights[2:], rhs_parts[0], rhs_parts[4]),
    )
    image_parts = near_planes(call(near_kernel, near_shape, (at, image), in_smem=(0,), after=(tiles,)))
    tiles = call(spread_kernel, struct((slabs, 8, 128)), (swap(tiles, "coil"),), after=(image_parts[1], image_parts[3]))
    last = swap(tiles, "slab")
    scratch = [pltpu.VMEM((12, 144, 256), BF16)]
    scratch += [pltpu.VMEM((10 - 2 * m, (16 - 2 * m) * 32, 256), BF16) for m in range(4)]
    return call(
        functools.partial(denoise_kernel, coils, slabs),
        (struct(prior_image.shape), struct(prior_image.shape)),
        (at, last, *rhs_parts, *image_parts, *weights),
        scratch=scratch,
        in_smem=(0,),
    )


def solution(mesh):
    placed = (
        P("coil", None, "slab", None, None),
        P("coil", None, "slab", None, None),
        P("slab", None, None),
        P(None, "slab", "coil", None),
        P(),
        P(),
        P(),
    )
    return jax.shard_map(
        body,
        mesh=mesh,
        in_specs=placed,
        out_specs=(P(None, "slab", "coil", None), P(None, "slab", "coil", None)),
        check_vma=False,
    )
```

```python
import functools
import math

import jax
import jax.numpy as jnp
import numpy as np
from jax import lax
from jax.experimental import pallas as pl
from jax.experimental.pallas import tpu as pltpu
from jax.sharding import PartitionSpec as P

LAMBDA = 0.5
HALO = 5
STEPS = 32000.0
FINE = 256.0
SIDE = 8
GROUP = 2
F32 = jnp.float32
BF16 = jnp.bfloat16
VMEM_BYTES = 20 * 1024 * 1024


def call(kernel, out_shape, args, scratch=(), in_smem=(), after=()):
    specs = [
        pl.BlockSpec(memory_space=pltpu.SMEM if i in in_smem else pltpu.VMEM) for i in range(len(args))
    ]
    specs += [pl.BlockSpec(memory_space=pl.ANY)] * len(after)
    if after:
        inner_kernel, count = kernel, len(args)

        def kernel(*refs):
            inner_kernel(*refs[:count], *refs[count + len(after) :])

    outs = jax.tree.map(lambda _: pl.BlockSpec(memory_space=pltpu.VMEM), out_shape)
    return pl.pallas_call(
        kernel,
        out_shape=out_shape,
        in_specs=specs,
        out_specs=outs,
        scratch_shapes=list(scratch),
        compiler_params=pltpu.CompilerParams(vmem_limit_bytes=VMEM_BYTES),
    )(*args, *after)


def struct(shape, dtype=F32):
    return jax.ShapeDtypeStruct(shape, dtype)


def halves(table):
    high = table.astype(np.float32).astype(jnp.bfloat16)
    low = (table.astype(np.float32) - high.astype(np.float32)).astype(jnp.bfloat16)
    return high, low


def dft_pair(length):
    positions = np.arange(length)
    angles = 2.0 * math.pi / length * (positions[:, None] * positions[None, :] % length)
    scaling = 1.0 / math.sqrt(length)
    return np.cos(angles) * scaling, scaling * np.sin(angles)


def left_table(length):
    cosine, sine = dft_pair(length)
    parts = [np.concatenate(halves(part), axis=1) for part in (cosine, sine)]
    return np.concatenate(parts, axis=0)


def right_table(length):
    cosine, sine = dft_pair(length)
    return np.concatenate(halves(cosine) + halves(sine), axis=1)


def split(values):
    high = values.astype(BF16)
    low = (values - high.astype(F32)).astype(BF16)
    return high, low


def dft_rows(field, table_ref, sign):
    values = jnp.concatenate(field[0] + field[1], axis=1)
    high, low = split(values)
    size = values.shape[0]
    table_high, table_low = table_ref[:, :size], table_ref[:, size:]
    table = jnp.concatenate([table_high, table_high, table_low], axis=1)
    products = jnp.dot(table, jnp.concatenate([high, low, high], axis=0), preferred_element_type=F32)
    half = values.shape[1] // 2
    cosine, sine = products[:size], products[size:]
    real = cosine[:, :half] - sign * sine[:, half:]
    imag = cosine[:, half:] + sign * sine[:, :half]
    columns = half // 2
    return [[part[:, p * columns : (p + 1) * columns] for p in range(2)] for part in (real, imag)]


def dft_columns(field, table_ref, sign):
    values = by_columns(field)
    high, low = split(values)
    size = table_ref.shape[0]
    cosine_high, cosine_low, sine_high, sine_low = [table_ref[:, i * size : (i + 1) * size] for i in range(4)]

    def block(cosine, sine):
        plus, minus = (sine, -sine) if sign > 0 else (-sine, sine)
        return jnp.concatenate(
            [jnp.concatenate([cosine, plus], axis=1), jnp.concatenate([minus, cosine], axis=1)], axis=0
        )

    table_high = block(cosine_high, sine_high)
    table = jnp.concatenate([table_high, table_high, block(cosine_low, sine_low)], axis=0)
    return from_columns(jnp.dot(jnp.concatenate([high, low, high], axis=1), table, preferred_element_type=F32))


def by_columns(field):
    planes = range(len(field[0]))
    return jnp.concatenate([jnp.concatenate([field[0][p], field[1][p]], axis=1) for p in planes], axis=0)


def from_columns(values):
    rows, columns = values.shape[0] // 2, values.shape[1] // 2
    return [[values[p * rows : (p + 1) * rows, a * columns : (a + 1) * columns] for p in range(2)] for a in range(2)]


def to_float(values):
    return values.astype(jnp.int32).astype(F32)


def to_short(values):
    return jnp.floor(values + 0.5).astype(jnp.int32).astype(jnp.int16)


def exponent_of(largest):
    return jnp.ceil(jnp.log2(jnp.maximum(largest, 1e-30)) * FINE) * (1.0 / FINE)


def scales_of(blocks_ref):
    return jnp.exp2(to_float(blocks_ref[:, 64:80, :])[:, 0:1, :] * (1.0 / FINE)) * (1.0 / STEPS)


def load_image(blocks_ref):
    count, _, columns = blocks_ref.shape
    scales = scales_of(blocks_ref)

    def one(a, p):
        start = (2 * a + p) * 16
        return (to_float(blocks_ref[:, start : start + 16, :]) * scales).reshape(count * 16, columns)

    return [[one(a, p) for p in range(2)] for a in range(2)]


def store_image(blocks_ref, image, extra):
    count, _, columns = blocks_ref.shape
    blocks = [image[a][p].reshape(count, 16, columns) for a in range(2) for p in range(2)]
    largest = jnp.maximum(
        jnp.maximum(jnp.abs(blocks[0]), jnp.abs(blocks[1])), jnp.maximum(jnp.abs(blocks[2]), jnp.abs(blocks[3]))
    )
    largest = jnp.max(jnp.max(largest, axis=1, keepdims=True), axis=2, keepdims=True)
    exponents = exponent_of(largest)
    factors = jnp.exp2(-exponents) * STEPS
    for i in range(4):
        blocks_ref[:, 16 * i : 16 * i + 16, :] = to_short(blocks[i] * factors)
    row = lax.broadcasted_iota(jnp.int32, (count, 16, columns), 1)
    last = jnp.where(row == 0, exponents * FINE, extra)
    blocks_ref[:, 64:80, :] = to_short(last)


def store_copies(blocks_ref, rows):
    exponent = exponent_of(jnp.max(jnp.max(jnp.abs(rows), axis=0, keepdims=True), axis=1, keepdims=True))
    shorts = to_short(rows * (jnp.exp2(-exponent) * STEPS))
    tail = to_short(jnp.broadcast_to(exponent * FINE, (16, 128)))
    for k in range(blocks_ref.shape[0]):
        blocks_ref[k, 0:64, :] = shorts
        blocks_ref[k, 64:80, :] = tail
    return to_float(shorts) * (jnp.exp2(exponent) * (1.0 / STEPS))


def sum_blocks(blocks_ref):
    scales = scales_of(blocks_ref)
    total = to_float(blocks_ref[0, 0:64, :]) * scales[0]
    for k in range(1, blocks_ref.shape[0]):
        total = total + to_float(blocks_ref[k, 0:64, :]) * scales[k]
    return total


def coil_field(maps_ref, image):
    real = [maps_ref[0, p] * image[0][p] - maps_ref[1, p] * image[1][p] for p in range(2)]
    imag = [maps_ref[0, p] * image[1][p] + maps_ref[1, p] * image[0][p] for p in range(2)]
    return [real, imag]


def coil_term(maps_ref, field):
    real = [maps_ref[0, p] * field[0][p] + maps_ref[1, p] * field[1][p] for p in range(2)]
    imag = [maps_ref[0, p] * field[1][p] - maps_ref[1, p] * field[0][p] for p in range(2)]
    return [real, imag]


def masked(field, mask_ref):
    masks = [mask_ref[p].astype(F32) for p in range(2)]
    return [[field[a][p] * masks[p] for p in range(2)] for a in range(2)]


def inner(first, second):
    return sum(row_sum(first[a][p] * second[a][p]) for a in range(2) for p in range(2))


def row_sum(values):
    folded = jnp.sum(values.reshape(-1, 8, values.shape[-1]), axis=0)
    folded = jnp.sum(folded, axis=0, keepdims=True)
    return folded


def tile_of(rows):
    blank = jnp.zeros((1, 128), F32)
    return jnp.concatenate(list(rows) + [blank] * (8 - len(rows)), axis=0)


def store_near(near_ref, blocks_ref, at):
    count = blocks_ref.shape[0]

    def one(at, start):
        scale = jnp.exp2(to_float(blocks_ref[at, 64:80, :])[0:1] * (1.0 / FINE)) * (1.0 / STEPS)
        return to_float(blocks_ref[at, start : start + 16, :]) * scale

    for a in range(2):
        for p in range(2):
            start = (2 * a + p) * 16
            near_ref[p, a, 8:24, :] = one(at, start)
            before = one(jnp.maximum(at - 1, 0), start)[8:16]
            after = one(jnp.minimum(at + 1, count - 1), start)[0:8]
            near_ref[p, a, 0:8, :] = jnp.where(at > 0, before, 0.0)
            near_ref[p, a, 24:32, :] = jnp.where(at < count - 1, after, 0.0)


def adjoint_kernel(
    mask_hbm, kspace_hbm, rows_hbm, columns_hbm, maps_hbm, out_ref, mask_ref, kspace_ref, rows_ref, columns_ref, maps_ref, sems
):
    sources = (mask_hbm, kspace_hbm, rows_hbm, columns_hbm, maps_hbm)
    targets = (mask_ref, kspace_ref, rows_ref, columns_ref, maps_ref)
    copies = [pltpu.make_async_copy(src, dst, sems.at[i]) for i, (src, dst) in enumerate(zip(sources, targets))]
    for copy in copies[:4]:
        copy.start()
    for copy in copies[:2]:
        copy.wait()
    copies[4].start()
    copies[2].wait()
    field = masked([[kspace_ref[a, p] for p in range(2)] for a in range(2)], mask_ref)
    field = dft_rows(field, rows_ref, 1.0)
    copies[3].wait()
    field = dft_columns(field, columns_ref, 1.0)
    copies[4].wait()
    store_image(out_ref, coil_term(maps_ref, field), 0.0)


def adjoint(mask, kspace, rows, columns, maps, coils):
    args = (mask, kspace, rows, columns, maps)
    return pl.pallas_call(
        adjoint_kernel,
        out_shape=struct((coils, 80, 128), jnp.int16),
        in_specs=[pl.BlockSpec(memory_space=pl.ANY)] * len(args),
        out_specs=pl.BlockSpec(memory_space=pltpu.VMEM),
        scratch_shapes=[pltpu.VMEM(arg.shape, arg.dtype) for arg in args] + [pltpu.SemaphoreType.DMA((len(args),))],
        compiler_params=pltpu.CompilerParams(vmem_limit_bytes=60 * 1024 * 1024),
    )(*args)


def rows_kernel(blocks_ref, prior_ref, rows_ref, copies_ref):
    prior = jnp.concatenate([prior_ref[a, p] for a in range(2) for p in range(2)], axis=0)
    rows_ref[...] = store_copies(copies_ref, sum_blocks(blocks_ref) + LAMBDA * prior)


def normal_kernel(
    at_ref, blocks_ref, mask_ref, maps_ref, rows_ref, columns_ref, out_ref, spectrum_ref, tile_ref, near_ref
):
    store_near(near_ref, blocks_ref, at_ref[0])
    image = load_image(blocks_ref)
    field = dft_columns(coil_field(maps_ref, image), columns_ref, -1.0)
    spectrum = masked(dft_rows(field, rows_ref, -1.0), mask_ref)
    for a in range(2):
        for p in range(2):
            spectrum_ref[a, p] = spectrum[a][p]
    field = dft_columns(dft_rows(spectrum, rows_ref, 1.0), columns_ref, 1.0)
    energy = inner(spectrum, spectrum)
    tile_ref[...] = tile_of([inner(image, image), energy])
    coarse = lane_sum(energy)
    level = exponent_of(coarse)
    row = lax.broadcasted_iota(jnp.int32, (1, 16, 128), 1)
    extra = jnp.where(row == 1, level * FINE, jnp.exp2(-level) * STEPS * coarse)
    store_image(out_ref, coil_term(maps_ref, field), extra)


def image_kernel(blocks_ref, rhs_rows_ref, tile_ref, copies_ref, sums_ref):
    rhs = rhs_rows_ref[...]
    image = store_copies(copies_ref, sum_blocks(blocks_ref) + LAMBDA * rhs)
    extra = to_float(blocks_ref[:, 64:80, :])
    coarse = jnp.sum(jnp.exp2(extra[:, 1:2, :] * (1.0 / FINE)) * extra[:, 2:3, :], axis=0) * (1.0 / STEPS)
    norm, energy = tile_ref[0:1, :], tile_ref[1:2, :]
    step = slab_step(lane_sum(norm), coarse)
    residual = rhs - step * image
    share = 1.0 / blocks_ref.shape[0]
    rows = [row_sum(residual * residual), row_sum(residual * rhs), share * norm, energy, share * step]
    sums_ref[...] = tile_of(rows)


def lane_sum(values):
    return jnp.sum(values, axis=-1, keepdims=True)


def slab_step(norm, energy):
    curved = energy + LAMBDA * norm
    return jnp.where(curved > 0.0, norm / jnp.where(curved > 0.0, curved, 1.0), 1.0)


def last_kernel(sums_ref, blocks_ref, spectrum_ref, mask_ref, maps_ref, rows_ref, columns_ref, out_ref):
    step = sums_ref[4:5, :] * float(blocks_ref.shape[0])
    field = dft_columns(coil_field(maps_ref, load_image(blocks_ref)), columns_ref, -1.0)
    spectrum = masked(dft_rows(field, rows_ref, -1.0), mask_ref)
    before = [[spectrum_ref[a, p] for p in range(2)] for a in range(2)]
    spectrum = [[before[a][p] - step * spectrum[a][p] for p in range(2)] for a in range(2)]
    tile = tile_of([inner(spectrum, spectrum), inner(spectrum, before)] + [sums_ref[i : i + 1, :] for i in range(5)])
    for k in range(out_ref.shape[0]):
        out_ref[k, 0:8] = tile


def near_kernel(at_ref, blocks_ref, near_ref):
    store_near(near_ref, blocks_ref, at_ref[0])


def pack_kernel(below_ref, near_ref, above_ref, low_ref, high_ref):
    low_ref[0] = below_ref[1]
    low_ref[1:3] = near_ref[...]
    high_ref[0:2] = near_ref[...]
    high_ref[2] = above_ref[0]


def spread_kernel(tiles_ref, out_ref):
    total = jnp.sum(tiles_ref[:, 0:8, :], axis=0)
    for k in range(out_ref.shape[0]):
        out_ref[k] = total


def final_scales(tiles_ref):
    curve, curve_cross, norm, cross, norm_first, energy_first = [
        lane_sum(tiles_ref[:, i, :]) for i in range(6)
    ]
    step_here = tiles_ref[:, 6, 0:1]

    def over_slabs(values):
        return jnp.sum(values, axis=0, keepdims=True)

    all_norm, all_energy = over_slabs(norm_first), over_slabs(energy_first)
    step_first = all_norm / (all_energy + LAMBDA * all_norm)
    here = step_first / step_here
    rest = 1.0 - here
    curve = over_slabs(here * here * curve + rest * (2.0 * here * curve_cross + rest * energy_first))
    curve_cross = over_slabs(here * curve_cross + rest * energy_first)
    norm = over_slabs(here * here * norm + rest * (2.0 * here * cross + rest * norm_first))
    cross = over_slabs(here * cross + rest * norm_first)
    ratio = norm / all_norm
    curvature = curve + ratio * (2.0 * curve_cross + ratio * all_energy)
    curvature = curvature + LAMBDA * (norm + ratio * (2.0 * cross + ratio * all_norm))
    return step_first, norm / curvature, ratio


def starts_of(rows):
    starts = list(range(0, rows - GROUP + 1, GROUP))
    if starts[-1] + GROUP < rows:
        starts.append(rows - GROUP)
    return starts


def shifted_sum(parts):
    before, here, after = parts
    lane = lax.broadcasted_iota(jnp.int32, before.shape[:1] + (128,), 1)
    outs = []
    for h in range(2):
        cut = slice(128 * h, 128 * (h + 1))
        low = jnp.where(lane > 0, pltpu.roll(before[:, cut], 1, 1), 0.0)
        high = jnp.where(lane < 127, pltpu.roll(after[:, cut], 127, 1), 0.0)
        outs.append(here[:, cut] + low + high)
    return jnp.concatenate(outs, axis=1)


def denoise_kernel(coil_count, slab_count, *refs):
    at_ref, last_ref = refs[:2]
    rhs_refs = refs[2:7]
    image_refs = refs[7:12]
    w_first_ref, w_middle_ref, w_last_ref, solution_ref, refined_ref = refs[12:17]
    features_ref = refs[17]
    hidden_refs = refs[18:]
    coil_at = at_ref[0]
    slab_at = at_ref[1]

    step_first, step_last, ratio = final_scales(last_ref)
    scale_rhs = step_first + step_last * ratio

    lane = lax.broadcasted_iota(jnp.int32, (48, 128), 1)
    plane = 0
    brick = None
    for rhs_ref, image_ref in zip(rhs_refs, image_refs):
        for p in range(rhs_ref.shape[0]):
            full = []
            for a in range(2):
                rhs = rhs_ref[p, a]
                full.append(scale_rhs * rhs + step_last * (rhs - step_first * image_ref[p, a]))
            if 5 <= plane < 7:
                for a in range(2):
                    solution_ref[a, plane - 5] = full[a][8:24]
            for h in range(2):
                window = jnp.concatenate([f[8 * h : 8 * h + 24] for f in full], axis=0)
                cut = slice(128 * h, 128 * (h + 1))
                low = jnp.where(lane > 0, pltpu.roll(window, 1, 1), 0.0)
                high = jnp.where(lane < 127, pltpu.roll(window, 127, 1), 0.0)
                features_ref[plane, 0:48, cut] = low.astype(BF16)
                features_ref[plane, 48:96, cut] = window.astype(BF16)
                features_ref[plane, 96:144, cut] = high.astype(BF16)
            plane += 1

    def outside(out_ref, depth):
        planes, cells, _ = out_ref.shape
        extra = 4 - depth
        first = 2 * slab_at - extra

        last_plane = 2 * slab_at + 1 + extra
        edge = (coil_at == 0) | (coil_at == coil_count - 1) | (first < 0) | (last_plane >= 2 * slab_count)

        @pl.when(edge)
        def _():
            blank = jnp.zeros((planes, extra * 32, 128), BF16)

            @pl.when(coil_at == 0)
            def _():
                out_ref[:, 0 : extra * 32, 0:128] = blank

            @pl.when(coil_at == coil_count - 1)
            def _():
                out_ref[:, cells - extra * 32 : cells, 128:256] = blank

            for p in list(range(extra)) + list(range(planes - extra, planes)):

                @pl.when((first + p < 0) | (first + p >= 2 * slab_count))
                def _():
                    out_ref[p] = jnp.zeros(out_ref.shape[1:], BF16)

    first_out = hidden_refs[0]

    for p in range(first_out.shape[0]):
        taps = jnp.concatenate([features_ref[p + u] for u in range(3)], axis=0)
        values = jnp.dot(w_first_ref[:, :432], taps, preferred_element_type=F32)
        first_out[p] = jnp.maximum(values, 0.0).astype(BF16)
    outside(first_out, 0)

    for m in range(len(hidden_refs) - 1):
        in_ref, out_ref = hidden_refs[m], hidden_refs[m + 1]
        starts = starts_of(out_ref.shape[1] // 32)

        cells = GROUP * 32
        for p in range(out_ref.shape[0]):
            for start in starts:
                rows = slice(start * 32, (start + GROUP + 2) * 32)
                taps = jnp.concatenate([in_ref[p + u, rows] for u in range(3)], axis=0)
                sums = jnp.dot(w_middle_ref[m, :, : (GROUP + 2) * 96], taps, preferred_element_type=F32)
                values = shifted_sum([sums[t * cells : (t + 1) * cells] for t in range(3)])
                out_ref[p, start * 32 : start * 32 + cells] = jnp.maximum(values, 0.0).astype(BF16)
        outside(out_ref, m + 1)

    in_ref = hidden_refs[-1]
    for p in range(2):
        taps = jnp.concatenate([in_ref[p + u] for u in range(3)], axis=0)
        sums = jnp.dot(w_last_ref[:, :960], taps, preferred_element_type=F32)
        lane = lax.broadcasted_iota(jnp.int32, (64, 128), 1)
        for h in range(2):
            part = sums[:, 128 * h : 128 * (h + 1)]
            low = jnp.where(lane > 0, pltpu.roll(part, 1, 1), 0.0)
            high = jnp.where(lane < 127, pltpu.roll(part, 127, 1), 0.0)
            for a in range(2):
                rows = []
                for r in range(8):
                    at = 8 * r + a
                    rows.append(low[at : at + 1] + part[at + 2 : at + 3] + high[at + 4 : at + 5])
                piece = jnp.concatenate(rows, axis=0)
                refined_ref[a, p, 8 * h : 8 * h + 8] = solution_ref[a, p, 8 * h : 8 * h + 8] + piece


def tables_kernel(first_ref, middle_ref, w_first_ref, w_middle_ref):
    def spots(size, target, count=512):
        column = lax.broadcasted_iota(jnp.int32, (size, count), 1)
        return jnp.where(column == target(lax.broadcasted_iota(jnp.int32, (size, count), 0)), 1.0, 0.0).astype(BF16)

    def first_target(source):
        channel, u, v, t = source // 27, source // 9 % 3, source // 3 % 3, source % 3
        return ((u * 3 + t) * 2 + channel) * 24 + SIDE - HALO + v

    base = jnp.dot(first_ref[...], spots(54, first_target), preferred_element_type=F32)
    for r in range(16):
        w_first_ref[32 * r : 32 * r + 32] = (pltpu.roll(base, r, 1) if r else base).astype(BF16)
    for m in range(middle_ref.shape[0]):
        base = jnp.zeros((96, 512), F32)
        for u in range(3):
            for v in range(3):
                place = spots(32, lambda source: source + (u * (GROUP + 2) + v) * 32)
                taps = jnp.concatenate([middle_ref[m, u, v, t] for t in range(3)], axis=0)
                base = base + jnp.dot(taps, place, preferred_element_type=F32)
        for r in range(GROUP):
            band = (pltpu.roll(base, 32 * r, 1) if r else base).astype(BF16)
            for t in range(3):
                start = (t * GROUP + r) * 32
                w_middle_ref[m, start : start + 32] = band[32 * t : 32 * t + 32]


def last_table_kernel(last_ref, w_last_ref):
    bands = []
    for r in range(8):
        bands.append(pltpu.roll(last_ref[...], 32 * r, 1) if r else last_ref[...])
    w_last_ref[...] = jnp.concatenate(bands, axis=0).astype(BF16)


def tables(w_first, w_middle, w_last):
    first = w_first.reshape(w_first.shape[0], 54)
    middle = jnp.transpose(w_middle, (0, 3, 4, 5, 1, 2))
    last = jnp.pad(jnp.transpose(w_last, (4, 0, 2, 3, 1)), ((0, 0), (0, 0), (0, 0), (0, 7), (0, 0)))
    last = jnp.pad(last.reshape(6, 960), ((0, 2), (0, 64))).astype(F32)
    pair = call(
        tables_kernel,
        (struct((512, 512), BF16), struct((3, 96 * GROUP, 512), BF16)),
        (first, middle),
    )
    return (*pair, call(last_table_kernel, struct((64, 1024), BF16), (last,))), (first, last)


def swap(blocks, axis):
    return lax.all_to_all(blocks, axis, 0, 0, tiled=True)


def shifted(part, axis, step):
    count = lax.axis_size(axis)
    return lax.ppermute(part, axis, [(i, i + step) for i in range(count) if 0 <= i + step < count])


def near_planes(near):
    below, above = shifted(near, "slab", 1), shifted(near, "slab", -1)
    low, high = call(pack_kernel, (struct((3, 2, 32, 128)),) * 2, (below, near, above))
    return [shifted(low, "slab", 2), below, near, above, shifted(high, "slab", -2)]


def body(sensitivity, kspace, sampling, prior_image, w_first, w_middle, w_last):
    maps = sensitivity[0]
    len_y, len_z = maps.shape[2:]
    coils, slabs = lax.axis_size("coil"), lax.axis_size("slab")
    at = jnp.stack([lax.axis_index("coil"), lax.axis_index("slab")]).astype(jnp.int32)
    rows, columns = left_table(len_y), right_table(len_z)
    weights, prepared = tables(w_first, w_middle, w_last)

    term = adjoint(sampling, kspace[0], rows, columns, maps, coils)
    rhs_rows, copies = call(
        rows_kernel,
        (struct((64, 128)), struct((coils, 80, 128), jnp.int16)),
        (swap(term, "coil"), prior_image),
        after=prepared,
    )
    rhs = swap(copies, "coil")
    near_shape = struct((2, 2, 32, 128))
    term, spectrum, norms, rhs_near = call(
        normal_kernel,
        (
            struct((coils, 80, 128), jnp.int16),
            struct((2, 2, len_y, len_z)),
            struct((8, 128)),
            near_shape,
        ),
        (at, rhs, sampling, maps, rows, columns),
        in_smem=(0,),
    )
    rhs_parts = near_planes(rhs_near)
    copies, sums = call(
        image_kernel,
        (struct((coils, 80, 128), jnp.int16), struct((8, 128))),
        (swap(term, "coil"), rhs_rows, norms),
        after=(rhs_parts[1], rhs_parts[3]),
    )
    image = swap(copies, "coil")
    image_near = call(near_kernel, near_shape, (at, image), in_smem=(0,))
    tiles = call(
        last_kernel,
        struct((coils, 8, 128)),
        (sums, image, spectrum, sampling, maps, rows, columns),
        after=(*weights[2:], rhs_parts[0], rhs_parts[4], image_near),
    )
    image_parts = near_planes(image_near)
    tiles = call(spread_kernel, struct((slabs, 8, 128)), (swap(tiles, "coil"),), after=(image_parts[1], image_parts[3]))
    last = swap(tiles, "slab")
    scratch = [pltpu.VMEM((12, 144, 256), BF16)]
    scratch += [pltpu.VMEM((10 - 2 * m, (16 - 2 * m) * 32, 256), BF16) for m in range(4)]
    return call(
        functools.partial(denoise_kernel, coils, slabs),
        (struct(prior_image.shape), struct(prior_image.shape)),
        (at, last, *rhs_parts, *image_parts, *weights),
        scratch=scratch,
        in_smem=(0,),
    )


def solution(mesh):
    placed = (
        P("coil", None, "slab", None, None),
        P("coil", None, "slab", None, None),
        P("slab", None, None),
        P(None, "slab", "coil", None),
        P(),
        P(),
        P(),
    )
    return jax.shard_map(
        body,
        mesh=mesh,
        in_specs=placed,
        out_specs=(P(None, "slab", "coil", None), P(None, "slab", "coil", None)),
        check_vma=False,
    )
```

```python
import functools
import math

import jax
import jax.numpy as jnp
import numpy as np
from jax import lax
from jax.experimental import pallas as pl
from jax.experimental.pallas import tpu as pltpu
from jax.sharding import PartitionSpec as P

LAMBDA = 0.5
HALO = 5
STEPS = 32000.0
FINE = 256.0
SIDE = 8
GROUP = 2
F32 = jnp.float32
BF16 = jnp.bfloat16
VMEM_BYTES = 20 * 1024 * 1024


def call(kernel, out_shape, args, scratch=(), in_smem=(), after=()):
    specs = [
        pl.BlockSpec(memory_space=pltpu.SMEM if i in in_smem else pltpu.VMEM) for i in range(len(args))
    ]
    specs += [pl.BlockSpec(memory_space=pl.ANY)] * len(after)
    if after:
        inner_kernel, count = kernel, len(args)

        def kernel(*refs):
            inner_kernel(*refs[:count], *refs[count + len(after) :])

    outs = jax.tree.map(lambda _: pl.BlockSpec(memory_space=pltpu.VMEM), out_shape)
    return pl.pallas_call(
        kernel,
        out_shape=out_shape,
        in_specs=specs,
        out_specs=outs,
        scratch_shapes=list(scratch),
        compiler_params=pltpu.CompilerParams(vmem_limit_bytes=VMEM_BYTES),
    )(*args, *after)


def struct(shape, dtype=F32):
    return jax.ShapeDtypeStruct(shape, dtype)


def halves(table):
    high = table.astype(np.float32).astype(jnp.bfloat16)
    low = (table.astype(np.float32) - high.astype(np.float32)).astype(jnp.bfloat16)
    return high, low


def dft_pair(length):
    positions = np.arange(length)
    angles = 2.0 * math.pi / length * (positions[:, None] * positions[None, :] % length)
    scaling = 1.0 / math.sqrt(length)
    return np.cos(angles) * scaling, scaling * np.sin(angles)


def left_table(length):
    cosine, sine = dft_pair(length)
    parts = [np.concatenate(halves(part), axis=1) for part in (cosine, sine)]
    return np.concatenate(parts, axis=0)


def right_table(length):
    cosine, sine = dft_pair(length)
    return np.concatenate(halves(cosine) + halves(sine), axis=1)


def split(values):
    high = values.astype(BF16)
    low = (values - high.astype(F32)).astype(BF16)
    return high, low


def dft_rows(field, table_ref, sign):
    values = jnp.concatenate(field[0] + field[1], axis=1)
    high, low = split(values)
    size = values.shape[0]
    table_high, table_low = table_ref[:, :size], table_ref[:, size:]
    table = jnp.concatenate([table_high, table_high, table_low], axis=1)
    products = jnp.dot(table, jnp.concatenate([high, low, high], axis=0), preferred_element_type=F32)
    half = values.shape[1] // 2
    cosine, sine = products[:size], products[size:]
    real = cosine[:, :half] - sign * sine[:, half:]
    imag = cosine[:, half:] + sign * sine[:, :half]
    columns = half // 2
    return [[part[:, p * columns : (p + 1) * columns] for p in range(2)] for part in (real, imag)]


def dft_columns(field, table_ref, sign):
    values = by_columns(field)
    high, low = split(values)
    size = table_ref.shape[0]
    cosine_high, cosine_low, sine_high, sine_low = [table_ref[:, i * size : (i + 1) * size] for i in range(4)]

    def block(cosine, sine):
        plus, minus = (sine, -sine) if sign > 0 else (-sine, sine)
        return jnp.concatenate(
            [jnp.concatenate([cosine, plus], axis=1), jnp.concatenate([minus, cosine], axis=1)], axis=0
        )

    table_high = block(cosine_high, sine_high)
    table = jnp.concatenate([table_high, table_high, block(cosine_low, sine_low)], axis=0)
    return from_columns(jnp.dot(jnp.concatenate([high, low, high], axis=1), table, preferred_element_type=F32))


def by_columns(field):
    planes = range(len(field[0]))
    return jnp.concatenate([jnp.concatenate([field[0][p], field[1][p]], axis=1) for p in planes], axis=0)


def from_columns(values):
    rows, columns = values.shape[0] // 2, values.shape[1] // 2
    return [[values[p * rows : (p + 1) * rows, a * columns : (a + 1) * columns] for p in range(2)] for a in range(2)]


def to_float(values):
    return values.astype(jnp.int32).astype(F32)


def to_short(values):
    return jnp.floor(values + 0.5).astype(jnp.int32).astype(jnp.int16)


def exponent_of(largest):
    return jnp.ceil(jnp.log2(jnp.maximum(largest, 1e-30)) * FINE) * (1.0 / FINE)


def scales_of(blocks_ref):
    return jnp.exp2(to_float(blocks_ref[:, 64:80, :])[:, 0:1, :] * (1.0 / FINE)) * (1.0 / STEPS)


def load_image(blocks_ref):
    count, _, columns = blocks_ref.shape
    scales = scales_of(blocks_ref)

    def one(a, p):
        start = (2 * a + p) * 16
        return (to_float(blocks_ref[:, start : start + 16, :]) * scales).reshape(count * 16, columns)

    return [[one(a, p) for p in range(2)] for a in range(2)]


def store_image(blocks_ref, image, extra):
    count, _, columns = blocks_ref.shape
    blocks = [image[a][p].reshape(count, 16, columns) for a in range(2) for p in range(2)]
    largest = jnp.maximum(
        jnp.maximum(jnp.abs(blocks[0]), jnp.abs(blocks[1])), jnp.maximum(jnp.abs(blocks[2]), jnp.abs(blocks[3]))
    )
    largest = jnp.max(jnp.max(largest, axis=1, keepdims=True), axis=2, keepdims=True)
    exponents = exponent_of(largest)
    factors = jnp.exp2(-exponents) * STEPS
    for i in range(4):
        blocks_ref[:, 16 * i : 16 * i + 16, :] = to_short(blocks[i] * factors)
    row = lax.broadcasted_iota(jnp.int32, (count, 16, columns), 1)
    last = jnp.where(row == 0, exponents * FINE, extra)
    blocks_ref[:, 64:80, :] = to_short(last)


def store_copies(blocks_ref, rows):
    exponent = exponent_of(jnp.max(jnp.max(jnp.abs(rows), axis=0, keepdims=True), axis=1, keepdims=True))
    shorts = to_short(rows * (jnp.exp2(-exponent) * STEPS))
    tail = to_short(jnp.broadcast_to(exponent * FINE, (16, 128)))
    for k in range(blocks_ref.shape[0]):
        blocks_ref[k, 0:64, :] = shorts
        blocks_ref[k, 64:80, :] = tail
    return to_float(shorts) * (jnp.exp2(exponent) * (1.0 / STEPS))


def sum_blocks(blocks_ref):
    scales = scales_of(blocks_ref)
    total = to_float(blocks_ref[0, 0:64, :]) * scales[0]
    for k in range(1, blocks_ref.shape[0]):
        total = total + to_float(blocks_ref[k, 0:64, :]) * scales[k]
    return total


def coil_field(maps_ref, image):
    real = [maps_ref[0, p] * image[0][p] - maps_ref[1, p] * image[1][p] for p in range(2)]
    imag = [maps_ref[0, p] * image[1][p] + maps_ref[1, p] * image[0][p] for p in range(2)]
    return [real, imag]


def coil_term(maps_ref, field):
    real = [maps_ref[0, p] * field[0][p] + maps_ref[1, p] * field[1][p] for p in range(2)]
    imag = [maps_ref[0, p] * field[1][p] - maps_ref[1, p] * field[0][p] for p in range(2)]
    return [real, imag]


def masked(field, mask_ref):
    masks = [mask_ref[p].astype(F32) for p in range(2)]
    return [[field[a][p] * masks[p] for p in range(2)] for a in range(2)]


def inner(first, second):
    return sum(row_sum(first[a][p] * second[a][p]) for a in range(2) for p in range(2))


def row_sum(values):
    folded = jnp.sum(values.reshape(-1, 8, values.shape[-1]), axis=0)
    folded = jnp.sum(folded, axis=0, keepdims=True)
    return folded


def tile_of(rows):
    blank = jnp.zeros((1, 128), F32)
    return jnp.concatenate(list(rows) + [blank] * (8 - len(rows)), axis=0)


def store_near(near_ref, blocks_ref, at):
    count = blocks_ref.shape[0]

    def one(at, start):
        scale = jnp.exp2(to_float(blocks_ref[at, 64:80, :])[0:1] * (1.0 / FINE)) * (1.0 / STEPS)
        return to_float(blocks_ref[at, start : start + 16, :]) * scale

    for a in range(2):
        for p in range(2):
            start = (2 * a + p) * 16
            near_ref[p, a, 8:24, :] = one(at, start)
            before = one(jnp.maximum(at - 1, 0), start)[8:16]
            after = one(jnp.minimum(at + 1, count - 1), start)[0:8]
            near_ref[p, a, 0:8, :] = jnp.where(at > 0, before, 0.0)
            near_ref[p, a, 24:32, :] = jnp.where(at < count - 1, after, 0.0)


def adjoint_kernel(
    mask_hbm, kspace_hbm, rows_hbm, columns_hbm, maps_hbm, out_ref, mask_ref, kspace_ref, rows_ref, columns_ref, maps_ref, sems
):
    sources = (mask_hbm, kspace_hbm, rows_hbm, columns_hbm, maps_hbm)
    targets = (mask_ref, kspace_ref, rows_ref, columns_ref, maps_ref)
    copies = [pltpu.make_async_copy(src, dst, sems.at[i]) for i, (src, dst) in enumerate(zip(sources, targets))]
    for copy in copies[:4]:
        copy.start()
    for copy in copies[:2]:
        copy.wait()
    copies[4].start()
    copies[2].wait()
    field = masked([[kspace_ref[a, p] for p in range(2)] for a in range(2)], mask_ref)
    field = dft_rows(field, rows_ref, 1.0)
    copies[3].wait()
    field = dft_columns(field, columns_ref, 1.0)
    copies[4].wait()
    store_image(out_ref, coil_term(maps_ref, field), 0.0)


def adjoint(mask, kspace, rows, columns, maps, coils):
    args = (mask, kspace, rows, columns, maps)
    return pl.pallas_call(
        adjoint_kernel,
        out_shape=struct((coils, 80, 128), jnp.int16),
        in_specs=[pl.BlockSpec(memory_space=pl.ANY)] * len(args),
        out_specs=pl.BlockSpec(memory_space=pltpu.VMEM),
        scratch_shapes=[pltpu.VMEM(arg.shape, arg.dtype) for arg in args] + [pltpu.SemaphoreType.DMA((len(args),))],
        compiler_params=pltpu.CompilerParams(vmem_limit_bytes=60 * 1024 * 1024),
    )(*args)


def rows_kernel(blocks_ref, prior_ref, rows_ref, copies_ref):
    prior = jnp.concatenate([prior_ref[a, p] for a in range(2) for p in range(2)], axis=0)
    rows_ref[...] = store_copies(copies_ref, sum_blocks(blocks_ref) + LAMBDA * prior)


def normal_kernel(
    at_ref, blocks_ref, mask_ref, maps_ref, rows_ref, columns_ref, out_ref, spectrum_ref, tile_ref, near_ref
):
    store_near(near_ref, blocks_ref, at_ref[0])
    image = load_image(blocks_ref)
    field = dft_columns(coil_field(maps_ref, image), columns_ref, -1.0)
    spectrum = masked(dft_rows(field, rows_ref, -1.0), mask_ref)
    for a in range(2):
        for p in range(2):
            spectrum_ref[a, p] = spectrum[a][p]
    field = dft_columns(dft_rows(spectrum, rows_ref, 1.0), columns_ref, 1.0)
    energy = inner(spectrum, spectrum)
    tile_ref[...] = tile_of([inner(image, image), energy])
    coarse = lane_sum(energy)
    level = exponent_of(coarse)
    row = lax.broadcasted_iota(jnp.int32, (1, 16, 128), 1)
    extra = jnp.where(row == 1, level * FINE, jnp.exp2(-level) * STEPS * coarse)
    store_image(out_ref, coil_term(maps_ref, field), extra)


def image_kernel(blocks_ref, rhs_rows_ref, tile_ref, copies_ref, sums_ref):
    rhs = rhs_rows_ref[...]
    image = store_copies(copies_ref, sum_blocks(blocks_ref) + LAMBDA * rhs)
    extra = to_float(blocks_ref[:, 64:80, :])
    coarse = jnp.sum(jnp.exp2(extra[:, 1:2, :] * (1.0 / FINE)) * extra[:, 2:3, :], axis=0) * (1.0 / STEPS)
    norm, energy = tile_ref[0:1, :], tile_ref[1:2, :]
    step = slab_step(lane_sum(norm), coarse)
    residual = rhs - step * image
    share = 1.0 / blocks_ref.shape[0]
    rows = [row_sum(residual * residual), row_sum(residual * rhs), share * norm, energy, share * step]
    sums_ref[...] = tile_of(rows)


def lane_sum(values):
    return jnp.sum(values, axis=-1, keepdims=True)


def slab_step(norm, energy):
    curved = energy + LAMBDA * norm
    return jnp.where(curved > 0.0, norm / jnp.where(curved > 0.0, curved, 1.0), 1.0)


def last_kernel(sums_ref, blocks_ref, spectrum_ref, mask_ref, maps_ref, rows_ref, columns_ref, out_ref):
    step = sums_ref[4:5, :] * float(blocks_ref.shape[0])
    field = dft_columns(coil_field(maps_ref, load_image(blocks_ref)), columns_ref, -1.0)
    spectrum = masked(dft_rows(field, rows_ref, -1.0), mask_ref)
    before = [[spectrum_ref[a, p] for p in range(2)] for a in range(2)]
    spectrum = [[before[a][p] - step * spectrum[a][p] for p in range(2)] for a in range(2)]
    tile = tile_of([inner(spectrum, spectrum), inner(spectrum, before)] + [sums_ref[i : i + 1, :] for i in range(5)])
    for k in range(out_ref.shape[0]):
        out_ref[k, 0:8] = tile


def near_kernel(at_ref, blocks_ref, near_ref):
    store_near(near_ref, blocks_ref, at_ref[0])


def pack_kernel(below_ref, near_ref, above_ref, low_ref, high_ref):
    low_ref[0] = below_ref[1]
    low_ref[1:3] = near_ref[...]
    high_ref[0:2] = near_ref[...]
    high_ref[2] = above_ref[0]


def spread_kernel(tiles_ref, out_ref):
    total = jnp.sum(tiles_ref[:, 0:8, :], axis=0)
    for k in range(out_ref.shape[0]):
        out_ref[k] = total


def final_scales(tiles_ref):
    curve, curve_cross, norm, cross, norm_first, energy_first = [
        lane_sum(tiles_ref[:, i, :]) for i in range(6)
    ]
    step_here = tiles_ref[:, 6, 0:1]

    def over_slabs(values):
        return jnp.sum(values, axis=0, keepdims=True)

    all_norm, all_energy = over_slabs(norm_first), over_slabs(energy_first)
    step_first = all_norm / (all_energy + LAMBDA * all_norm)
    here = step_first / step_here
    rest = 1.0 - here
    curve = over_slabs(here * here * curve + rest * (2.0 * here * curve_cross + rest * energy_first))
    curve_cross = over_slabs(here * curve_cross + rest * energy_first)
    norm = over_slabs(here * here * norm + rest * (2.0 * here * cross + rest * norm_first))
    cross = over_slabs(here * cross + rest * norm_first)
    ratio = norm / all_norm
    curvature = curve + ratio * (2.0 * curve_cross + ratio * all_energy)
    curvature = curvature + LAMBDA * (norm + ratio * (2.0 * cross + ratio * all_norm))
    return step_first, norm / curvature, ratio


def starts_of(rows):
    starts = list(range(0, rows - GROUP + 1, GROUP))
    if starts[-1] + GROUP < rows:
        starts.append(rows - GROUP)
    return starts


def shifted_sum(parts):
    before, here, after = parts
    lane = lax.broadcasted_iota(jnp.int32, before.shape[:1] + (128,), 1)
    outs = []
    for h in range(2):
        cut = slice(128 * h, 128 * (h + 1))
        low = jnp.where(lane > 0, pltpu.roll(before[:, cut], 1, 1), 0.0)
        high = jnp.where(lane < 127, pltpu.roll(after[:, cut], 127, 1), 0.0)
        outs.append(here[:, cut] + low + high)
    return jnp.concatenate(outs, axis=1)


def denoise_kernel(coil_count, slab_count, *refs):
    at_ref, last_ref = refs[:2]
    rhs_refs = refs[2:7]
    image_refs = refs[7:12]
    w_first_ref, w_middle_ref, w_last_ref, solution_ref, refined_ref = refs[12:17]
    features_ref = refs[17]
    hidden_refs = refs[18:]
    coil_at = at_ref[0]
    slab_at = at_ref[1]

    step_first, step_last, ratio = final_scales(last_ref)
    scale_rhs = step_first + step_last * ratio

    lane = lax.broadcasted_iota(jnp.int32, (48, 128), 1)
    plane = 0
    brick = None
    for rhs_ref, image_ref in zip(rhs_refs, image_refs):
        for p in range(rhs_ref.shape[0]):
            full = []
            for a in range(2):
                rhs = rhs_ref[p, a]
                full.append(scale_rhs * rhs + step_last * (rhs - step_first * image_ref[p, a]))
            if 5 <= plane < 7:
                for a in range(2):
                    solution_ref[a, plane - 5] = full[a][8:24]
            for h in range(2):
                window = jnp.concatenate([f[8 * h : 8 * h + 24] for f in full], axis=0)
                cut = slice(128 * h, 128 * (h + 1))
                low = jnp.where(lane > 0, pltpu.roll(window, 1, 1), 0.0)
                high = jnp.where(lane < 127, pltpu.roll(window, 127, 1), 0.0)
                features_ref[plane, 0:48, cut] = low.astype(BF16)
                features_ref[plane, 48:96, cut] = window.astype(BF16)
                features_ref[plane, 96:144, cut] = high.astype(BF16)
            plane += 1

    def outside(out_ref, depth):
        planes, cells, _ = out_ref.shape
        extra = 4 - depth
        first = 2 * slab_at - extra

        last_plane = 2 * slab_at + 1 + extra
        edge = (coil_at == 0) | (coil_at == coil_count - 1) | (first < 0) | (last_plane >= 2 * slab_count)

        @pl.when(edge)
        def _():
            blank = jnp.zeros((planes, extra * 32, 128), BF16)

            @pl.when(coil_at == 0)
            def _():
                out_ref[:, 0 : extra * 32, 0:128] = blank

            @pl.when(coil_at == coil_count - 1)
            def _():
                out_ref[:, cells - extra * 32 : cells, 128:256] = blank

            for p in list(range(extra)) + list(range(planes - extra, planes)):

                @pl.when((first + p < 0) | (first + p >= 2 * slab_count))
                def _():
                    out_ref[p] = jnp.zeros(out_ref.shape[1:], BF16)

    first_out = hidden_refs[0]

    for p in range(first_out.shape[0]):
        taps = jnp.concatenate([features_ref[p + u] for u in range(3)], axis=0)
        values = jnp.dot(w_first_ref[:, :432], taps, preferred_element_type=F32)
        first_out[p] = jnp.maximum(values, 0.0).astype(BF16)
    outside(first_out, 0)

    for m in range(len(hidden_refs) - 1):
        in_ref, out_ref = hidden_refs[m], hidden_refs[m + 1]
        starts = starts_of(out_ref.shape[1] // 32)

        cells = GROUP * 32
        for p in range(out_ref.shape[0]):
            for start in starts:
                rows = slice(start * 32, (start + GROUP + 2) * 32)
                taps = jnp.concatenate([in_ref[p + u, rows] for u in range(3)], axis=0)
                sums = jnp.dot(w_middle_ref[m, :, : (GROUP + 2) * 96], taps, preferred_element_type=F32)
                values = shifted_sum([sums[t * cells : (t + 1) * cells] for t in range(3)])
                out_ref[p, start * 32 : start * 32 + cells] = jnp.maximum(values, 0.0).astype(BF16)
        outside(out_ref, m + 1)

    in_ref = hidden_refs[-1]
    for p in range(2):
        taps = jnp.concatenate([in_ref[p + u] for u in range(3)], axis=0)
        sums = jnp.dot(w_last_ref[:, :960], taps, preferred_element_type=F32)
        lane = lax.broadcasted_iota(jnp.int32, (64, 128), 1)
        for h in range(2):
            part = sums[:, 128 * h : 128 * (h + 1)]
            low = jnp.where(lane > 0, pltpu.roll(part, 1, 1), 0.0)
            high = jnp.where(lane < 127, pltpu.roll(part, 127, 1), 0.0)
            for a in range(2):
                rows = []
                for r in range(8):
                    at = 8 * r + a
                    rows.append(low[at : at + 1] + part[at + 2 : at + 3] + high[at + 4 : at + 5])
                piece = jnp.concatenate(rows, axis=0)
                refined_ref[a, p, 8 * h : 8 * h + 8] = solution_ref[a, p, 8 * h : 8 * h + 8] + piece


def tables_kernel(first_ref, middle_ref, w_first_ref, w_middle_ref):
    def spots(size, target, count=512):
        column = lax.broadcasted_iota(jnp.int32, (size, count), 1)
        return jnp.where(column == target(lax.broadcasted_iota(jnp.int32, (size, count), 0)), 1.0, 0.0).astype(BF16)

    def first_target(source):
        channel, u, v, t = source // 27, source // 9 % 3, source // 3 % 3, source % 3
        return ((u * 3 + t) * 2 + channel) * 24 + SIDE - HALO + v

    base = jnp.dot(first_ref[...], spots(54, first_target), preferred_element_type=F32)
    for r in range(16):
        w_first_ref[32 * r : 32 * r + 32] = (pltpu.roll(base, r, 1) if r else base).astype(BF16)
    for m in range(middle_ref.shape[0]):
        base = jnp.zeros((96, 512), F32)
        for u in range(3):
            for v in range(3):
                place = spots(32, lambda source: source + (u * (GROUP + 2) + v) * 32)
                taps = jnp.concatenate([middle_ref[m, u, v, t] for t in range(3)], axis=0)
                base = base + jnp.dot(taps, place, preferred_element_type=F32)
        for r in range(GROUP):
            band = (pltpu.roll(base, 32 * r, 1) if r else base).astype(BF16)
            for t in range(3):
                start = (t * GROUP + r) * 32
                w_middle_ref[m, start : start + 32] = band[32 * t : 32 * t + 32]


def last_table_kernel(last_ref, w_last_ref):
    bands = []
    for r in range(8):
        bands.append(pltpu.roll(last_ref[...], 32 * r, 1) if r else last_ref[...])
    w_last_ref[...] = jnp.concatenate(bands, axis=0).astype(BF16)


def tables(w_first, w_middle, w_last):
    first = w_first.reshape(w_first.shape[0], 54)
    middle = jnp.transpose(w_middle, (0, 3, 4, 5, 1, 2))
    last = jnp.pad(jnp.transpose(w_last, (4, 0, 2, 3, 1)), ((0, 0), (0, 0), (0, 0), (0, 7), (0, 0)))
    last = jnp.pad(last.reshape(6, 960), ((0, 2), (0, 64))).astype(F32)
    pair = call(
        tables_kernel,
        (struct((512, 512), BF16), struct((3, 96 * GROUP, 512), BF16)),
        (first, middle),
    )
    return (*pair, call(last_table_kernel, struct((64, 1024), BF16), (last,))), (first, last)


def swap(blocks, axis):
    return lax.all_to_all(blocks, axis, 0, 0, tiled=True)


def shifted(part, axis, step):
    count = lax.axis_size(axis)
    return lax.ppermute(part, axis, [(i, i + step) for i in range(count) if 0 <= i + step < count])


def near_planes(near):
    below, above = shifted(near, "slab", 1), shifted(near, "slab", -1)
    low, high = call(pack_kernel, (struct((3, 2, 32, 128)),) * 2, (below, near, above))
    return [shifted(low, "slab", 2), below, near, above, shifted(high, "slab", -2)]


def body(sensitivity, kspace, sampling, prior_image, w_first, w_middle, w_last):
    maps = sensitivity[0]
    len_y, len_z = maps.shape[2:]
    coils, slabs = lax.axis_size("coil"), lax.axis_size("slab")
    at = jnp.stack([lax.axis_index("coil"), lax.axis_index("slab")]).astype(jnp.int32)
    rows, columns = left_table(len_y), right_table(len_z)
    weights, prepared = tables(w_first, w_middle, w_last)

    term = adjoint(sampling, kspace[0], rows, columns, maps, coils)
    rhs_rows, copies = call(
        rows_kernel,
        (struct((64, 128)), struct((coils, 80, 128), jnp.int16)),
        (swap(term, "coil"), prior_image),
        after=prepared,
    )
    rhs = swap(copies, "coil")
    near_shape = struct((2, 2, 32, 128))
    term, spectrum, norms, rhs_near = call(
        normal_kernel,
        (
            struct((coils, 80, 128), jnp.int16),
            struct((2, 2, len_y, len_z)),
            struct((8, 128)),
            near_shape,
        ),
        (at, rhs, sampling, maps, rows, columns),
        in_smem=(0,),
    )
    rhs_parts = near_planes(rhs_near)
    copies, sums = call(
        image_kernel,
        (struct((coils, 80, 128), jnp.int16), struct((8, 128))),
        (swap(term, "coil"), rhs_rows, norms),
        after=(rhs_parts[1], rhs_parts[3]),
    )
    image = swap(copies, "coil")
    image_near = call(near_kernel, near_shape, (at, image), in_smem=(0,))
    tiles = call(
        last_kernel,
        struct((coils, 8, 128)),
        (sums, image, spectrum, sampling, maps, rows, columns),
        after=(*weights[2:], rhs_parts[0], rhs_parts[4], image_near),
    )
    image_parts = near_planes(image_near)
    tiles = call(spread_kernel, struct((slabs, 8, 128)), (swap(tiles, "coil"),), after=(image_parts[0], image_parts[4]))
    last = swap(tiles, "slab")
    scratch = [pltpu.VMEM((12, 144, 256), BF16)]
    scratch += [pltpu.VMEM((10 - 2 * m, (16 - 2 * m) * 32, 256), BF16) for m in range(4)]
    return call(
        functools.partial(denoise_kernel, coils, slabs),
        (struct(prior_image.shape), struct(prior_image.shape)),
        (at, last, *rhs_parts, *image_parts, *weights),
        scratch=scratch,
        in_smem=(0,),
    )


def solution(mesh):
    placed = (
        P("coil", None, "slab", None, None),
        P("coil", None, "slab", None, None),
        P("slab", None, None),
        P(None, "slab", "coil", None),
        P(),
        P(),
        P(),
    )
    return jax.shard_map(
        body,
        mesh=mesh,
        in_specs=placed,
        out_specs=(P(None, "slab", "coil", None), P(None, "slab", "coil", None)),
        check_vma=False,
    )
```

```python
import functools
import math

import jax
import jax.numpy as jnp
import numpy as np
from jax import lax
from jax.experimental import pallas as pl
from jax.experimental.pallas import tpu as pltpu
from jax.sharding import PartitionSpec as P

LAMBDA = 0.5
HALO = 5
STEPS = 32000.0
FINE = 256.0
SIDE = 8
GROUP = 2
F32 = jnp.float32
BF16 = jnp.bfloat16
VMEM_BYTES = 20 * 1024 * 1024


def call(kernel, out_shape, args, scratch=(), in_smem=(), after=()):
    specs = [
        pl.BlockSpec(memory_space=pltpu.SMEM if i in in_smem else pltpu.VMEM) for i in range(len(args))
    ]
    specs += [pl.BlockSpec(memory_space=pl.ANY)] * len(after)
    if after:
        inner_kernel, count = kernel, len(args)

        def kernel(*refs):
            inner_kernel(*refs[:count], *refs[count + len(after) :])

    outs = jax.tree.map(lambda _: pl.BlockSpec(memory_space=pltpu.VMEM), out_shape)
    return pl.pallas_call(
        kernel,
        out_shape=out_shape,
        in_specs=specs,
        out_specs=outs,
        scratch_shapes=list(scratch),
        compiler_params=pltpu.CompilerParams(vmem_limit_bytes=VMEM_BYTES),
    )(*args, *after)


def struct(shape, dtype=F32):
    return jax.ShapeDtypeStruct(shape, dtype)


def halves(table):
    high = table.astype(np.float32).astype(jnp.bfloat16)
    low = (table.astype(np.float32) - high.astype(np.float32)).astype(jnp.bfloat16)
    return high, low


def dft_pair(length):
    positions = np.arange(length)
    angles = 2.0 * math.pi / length * (positions[:, None] * positions[None, :] % length)
    scaling = 1.0 / math.sqrt(length)
    return np.cos(angles) * scaling, scaling * np.sin(angles)


def left_table(length):
    cosine, sine = dft_pair(length)
    parts = [np.concatenate(halves(part), axis=1) for part in (cosine, sine)]
    return np.concatenate(parts, axis=0)


def right_table(length):
    cosine, sine = dft_pair(length)
    return np.concatenate(halves(cosine) + halves(sine), axis=1)


def split(values):
    high = values.astype(BF16)
    low = (values - high.astype(F32)).astype(BF16)
    return high, low


def dft_rows(field, table_ref, sign):
    values = jnp.concatenate(field[0] + field[1], axis=1)
    high, low = split(values)
    size = values.shape[0]
    table_high, table_low = table_ref[:, :size], table_ref[:, size:]
    table = jnp.concatenate([table_high, table_high, table_low], axis=1)
    products = jnp.dot(table, jnp.concatenate([high, low, high], axis=0), preferred_element_type=F32)
    half = values.shape[1] // 2
    cosine, sine = products[:size], products[size:]
    real = cosine[:, :half] - sign * sine[:, half:]
    imag = cosine[:, half:] + sign * sine[:, :half]
    columns = half // 2
    return [[part[:, p * columns : (p + 1) * columns] for p in range(2)] for part in (real, imag)]


def dft_columns(field, table_ref, sign):
    values = by_columns(field)
    high, low = split(values)
    size = table_ref.shape[0]
    cosine_high, cosine_low, sine_high, sine_low = [table_ref[:, i * size : (i + 1) * size] for i in range(4)]

    def block(cosine, sine):
        plus, minus = (sine, -sine) if sign > 0 else (-sine, sine)
        return jnp.concatenate(
            [jnp.concatenate([cosine, plus], axis=1), jnp.concatenate([minus, cosine], axis=1)], axis=0
        )

    table_high = block(cosine_high, sine_high)
    table = jnp.concatenate([table_high, table_high, block(cosine_low, sine_low)], axis=0)
    return from_columns(jnp.dot(jnp.concatenate([high, low, high], axis=1), table, preferred_element_type=F32))


def by_columns(field):
    planes = range(len(field[0]))
    return jnp.concatenate([jnp.concatenate([field[0][p], field[1][p]], axis=1) for p in planes], axis=0)


def from_columns(values):
    rows, columns = values.shape[0] // 2, values.shape[1] // 2
    return [[values[p * rows : (p + 1) * rows, a * columns : (a + 1) * columns] for p in range(2)] for a in range(2)]


def to_float(values):
    return values.astype(jnp.int32).astype(F32)


def to_short(values):
    return jnp.floor(values + 0.5).astype(jnp.int32).astype(jnp.int16)


def exponent_of(largest):
    return jnp.ceil(jnp.log2(jnp.maximum(largest, 1e-30)) * FINE) * (1.0 / FINE)


def scales_of(blocks_ref):
    return jnp.exp2(to_float(blocks_ref[:, 64:80, :])[:, 0:1, :] * (1.0 / FINE)) * (1.0 / STEPS)


def load_image(blocks_ref):
    count, _, columns = blocks_ref.shape
    scales = scales_of(blocks_ref)

    def one(a, p):
        start = (2 * a + p) * 16
        return (to_float(blocks_ref[:, start : start + 16, :]) * scales).reshape(count * 16, columns)

    return [[one(a, p) for p in range(2)] for a in range(2)]


def store_image(blocks_ref, image, extra):
    count, _, columns = blocks_ref.shape
    blocks = [image[a][p].reshape(count, 16, columns) for a in range(2) for p in range(2)]
    largest = jnp.maximum(
        jnp.maximum(jnp.abs(blocks[0]), jnp.abs(blocks[1])), jnp.maximum(jnp.abs(blocks[2]), jnp.abs(blocks[3]))
    )
    largest = jnp.max(jnp.max(largest, axis=1, keepdims=True), axis=2, keepdims=True)
    exponents = exponent_of(largest)
    factors = jnp.exp2(-exponents) * STEPS
    for i in range(4):
        blocks_ref[:, 16 * i : 16 * i + 16, :] = to_short(blocks[i] * factors)
    row = lax.broadcasted_iota(jnp.int32, (count, 16, columns), 1)
    last = jnp.where(row == 0, exponents * FINE, extra)
    blocks_ref[:, 64:80, :] = to_short(last)


def store_copies(blocks_ref, rows):
    exponent = exponent_of(jnp.max(jnp.max(jnp.abs(rows), axis=0, keepdims=True), axis=1, keepdims=True))
    shorts = to_short(rows * (jnp.exp2(-exponent) * STEPS))
    tail = to_short(jnp.broadcast_to(exponent * FINE, (16, 128)))
    for k in range(blocks_ref.shape[0]):
        blocks_ref[k, 0:64, :] = shorts
        blocks_ref[k, 64:80, :] = tail
    return to_float(shorts) * (jnp.exp2(exponent) * (1.0 / STEPS))


def sum_blocks(blocks_ref):
    scales = scales_of(blocks_ref)
    total = to_float(blocks_ref[0, 0:64, :]) * scales[0]
    for k in range(1, blocks_ref.shape[0]):
        total = total + to_float(blocks_ref[k, 0:64, :]) * scales[k]
    return total


def coil_field(maps_ref, image):
    real = [maps_ref[0, p] * image[0][p] - maps_ref[1, p] * image[1][p] for p in range(2)]
    imag = [maps_ref[0, p] * image[1][p] + maps_ref[1, p] * image[0][p] for p in range(2)]
    return [real, imag]


def coil_term(maps_ref, field):
    real = [maps_ref[0, p] * field[0][p] + maps_ref[1, p] * field[1][p] for p in range(2)]
    imag = [maps_ref[0, p] * field[1][p] - maps_ref[1, p] * field[0][p] for p in range(2)]
    return [real, imag]


def masked(field, mask_ref):
    masks = [mask_ref[p].astype(F32) for p in range(2)]
    return [[field[a][p] * masks[p] for p in range(2)] for a in range(2)]


def inner(first, second):
    return sum(row_sum(first[a][p] * second[a][p]) for a in range(2) for p in range(2))


def row_sum(values):
    folded = jnp.sum(values.reshape(-1, 8, values.shape[-1]), axis=0)
    folded = jnp.sum(folded, axis=0, keepdims=True)
    return folded


def tile_of(rows):
    blank = jnp.zeros((1, 128), F32)
    return jnp.concatenate(list(rows) + [blank] * (8 - len(rows)), axis=0)


def store_near(near_ref, blocks_ref, at):
    count = blocks_ref.shape[0]

    def one(at, start):
        scale = jnp.exp2(to_float(blocks_ref[at, 64:80, :])[0:1] * (1.0 / FINE)) * (1.0 / STEPS)
        return to_float(blocks_ref[at, start : start + 16, :]) * scale

    for a in range(2):
        for p in range(2):
            start = (2 * a + p) * 16
            near_ref[p, a, 8:24, :] = one(at, start)
            before = one(jnp.maximum(at - 1, 0), start)[8:16]
            after = one(jnp.minimum(at + 1, count - 1), start)[0:8]
            near_ref[p, a, 0:8, :] = jnp.where(at > 0, before, 0.0)
            near_ref[p, a, 24:32, :] = jnp.where(at < count - 1, after, 0.0)


def adjoint_kernel(
    mask_hbm, kspace_hbm, rows_hbm, columns_hbm, maps_hbm, out_ref, mask_ref, kspace_ref, rows_ref, columns_ref, maps_ref, sems
):
    sources = (mask_hbm, kspace_hbm, rows_hbm, columns_hbm, maps_hbm)
    targets = (mask_ref, kspace_ref, rows_ref, columns_ref, maps_ref)
    copies = [pltpu.make_async_copy(src, dst, sems.at[i]) for i, (src, dst) in enumerate(zip(sources, targets))]
    for copy in copies[:4]:
        copy.start()
    for copy in copies[:2]:
        copy.wait()
    copies[4].start()
    copies[2].wait()
    field = masked([[kspace_ref[a, p] for p in range(2)] for a in range(2)], mask_ref)
    field = dft_rows(field, rows_ref, 1.0)
    copies[3].wait()
    field = dft_columns(field, columns_ref, 1.0)
    copies[4].wait()
    store_image(out_ref, coil_term(maps_ref, field), 0.0)


def adjoint(mask, kspace, rows, columns, maps, coils):
    args = (mask, kspace, rows, columns, maps)
    return pl.pallas_call(
        adjoint_kernel,
        out_shape=struct((coils, 80, 128), jnp.int16),
        in_specs=[pl.BlockSpec(memory_space=pl.ANY)] * len(args),
        out_specs=pl.BlockSpec(memory_space=pltpu.VMEM),
        scratch_shapes=[pltpu.VMEM(arg.shape, arg.dtype) for arg in args] + [pltpu.SemaphoreType.DMA((len(args),))],
        compiler_params=pltpu.CompilerParams(vmem_limit_bytes=60 * 1024 * 1024),
    )(*args)


def rows_kernel(blocks_ref, prior_ref, rows_ref, copies_ref):
    prior = jnp.concatenate([prior_ref[a, p] for a in range(2) for p in range(2)], axis=0)
    rows_ref[...] = store_copies(copies_ref, sum_blocks(blocks_ref) + LAMBDA * prior)


def normal_kernel(
    at_ref, blocks_ref, mask_ref, maps_ref, rows_ref, columns_ref, out_ref, spectrum_ref, tile_ref, near_ref
):
    store_near(near_ref, blocks_ref, at_ref[0])
    image = load_image(blocks_ref)
    field = dft_columns(coil_field(maps_ref, image), columns_ref, -1.0)
    spectrum = masked(dft_rows(field, rows_ref, -1.0), mask_ref)
    for a in range(2):
        for p in range(2):
            spectrum_ref[a, p] = spectrum[a][p]
    field = dft_columns(dft_rows(spectrum, rows_ref, 1.0), columns_ref, 1.0)
    energy = inner(spectrum, spectrum)
    tile_ref[...] = tile_of([inner(image, image), energy])
    coarse = lane_sum(energy)
    level = exponent_of(coarse)
    row = lax.broadcasted_iota(jnp.int32, (1, 16, 128), 1)
    extra = jnp.where(row == 1, level * FINE, jnp.exp2(-level) * STEPS * coarse)
    store_image(out_ref, coil_term(maps_ref, field), extra)


def image_kernel(blocks_ref, rhs_rows_ref, tile_ref, copies_ref, sums_ref):
    rhs = rhs_rows_ref[...]
    image = store_copies(copies_ref, sum_blocks(blocks_ref) + LAMBDA * rhs)
    extra = to_float(blocks_ref[:, 64:80, :])
    coarse = jnp.sum(jnp.exp2(extra[:, 1:2, :] * (1.0 / FINE)) * extra[:, 2:3, :], axis=0) * (1.0 / STEPS)
    norm, energy = tile_ref[0:1, :], tile_ref[1:2, :]
    step = slab_step(lane_sum(norm), coarse)
    residual = rhs - step * image
    share = 1.0 / blocks_ref.shape[0]
    rows = [row_sum(residual * residual), row_sum(residual * rhs), share * norm, energy, share * step]
    sums_ref[...] = tile_of(rows)


def lane_sum(values):
    return jnp.sum(values, axis=-1, keepdims=True)


def slab_step(norm, energy):
    curved = energy + LAMBDA * norm
    return jnp.where(curved > 0.0, norm / jnp.where(curved > 0.0, curved, 1.0), 1.0)


def last_kernel(sums_ref, blocks_ref, spectrum_ref, mask_ref, maps_ref, rows_ref, columns_ref, out_ref):
    step = sums_ref[4:5, :] * float(blocks_ref.shape[0])
    field = dft_columns(coil_field(maps_ref, load_image(blocks_ref)), columns_ref, -1.0)
    spectrum = masked(dft_rows(field, rows_ref, -1.0), mask_ref)
    before = [[spectrum_ref[a, p] for p in range(2)] for a in range(2)]
    spectrum = [[before[a][p] - step * spectrum[a][p] for p in range(2)] for a in range(2)]
    tile = tile_of([inner(spectrum, spectrum), inner(spectrum, before)] + [sums_ref[i : i + 1, :] for i in range(5)])
    for k in range(out_ref.shape[0]):
        out_ref[k, 0:8] = tile


def near_kernel(at_ref, blocks_ref, near_ref):
    store_near(near_ref, blocks_ref, at_ref[0])


def pack_kernel(below_ref, near_ref, above_ref, low_ref, high_ref):
    low_ref[0] = below_ref[1]
    low_ref[1:3] = near_ref[...]
    high_ref[0:2] = near_ref[...]
    high_ref[2] = above_ref[0]


def spread_kernel(tiles_ref, out_ref):
    total = jnp.sum(tiles_ref[:, 0:8, :], axis=0)
    for k in range(out_ref.shape[0]):
        out_ref[k] = total


def final_scales(tiles_ref):
    curve, curve_cross, norm, cross, norm_first, energy_first = [
        lane_sum(tiles_ref[:, i, :]) for i in range(6)
    ]
    step_here = tiles_ref[:, 6, 0:1]

    def over_slabs(values):
        return jnp.sum(values, axis=0, keepdims=True)

    all_norm, all_energy = over_slabs(norm_first), over_slabs(energy_first)
    step_first = all_norm / (all_energy + LAMBDA * all_norm)
    here = step_first / step_here
    rest = 1.0 - here
    curve = over_slabs(here * here * curve + rest * (2.0 * here * curve_cross + rest * energy_first))
    curve_cross = over_slabs(here * curve_cross + rest * energy_first)
    norm = over_slabs(here * here * norm + rest * (2.0 * here * cross + rest * norm_first))
    cross = over_slabs(here * cross + rest * norm_first)
    ratio = norm / all_norm
    curvature = curve + ratio * (2.0 * curve_cross + ratio * all_energy)
    curvature = curvature + LAMBDA * (norm + ratio * (2.0 * cross + ratio * all_norm))
    return step_first, norm / curvature, ratio


def starts_of(rows):
    starts = list(range(0, rows - GROUP + 1, GROUP))
    if starts[-1] + GROUP < rows:
        starts.append(rows - GROUP)
    return starts


def shifted_sum(parts):
    before, here, after = parts
    lane = lax.broadcasted_iota(jnp.int32, before.shape[:1] + (128,), 1)
    outs = []
    for h in range(2):
        cut = slice(128 * h, 128 * (h + 1))
        low = jnp.where(lane > 0, pltpu.roll(before[:, cut], 1, 1), 0.0)
        high = jnp.where(lane < 127, pltpu.roll(after[:, cut], 127, 1), 0.0)
        outs.append(here[:, cut] + low + high)
    return jnp.concatenate(outs, axis=1)


def denoise_kernel(coil_count, slab_count, *refs):
    at_ref, last_ref = refs[:2]
    rhs_refs = refs[2:7]
    image_refs = refs[7:12]
    w_first_ref, w_middle_ref, w_last_ref, solution_ref, refined_ref = refs[12:17]
    features_ref = refs[17]
    hidden_refs = refs[18:]
    coil_at = at_ref[0]
    slab_at = at_ref[1]

    step_first, step_last, ratio = final_scales(last_ref)
    scale_rhs = step_first + step_last * ratio

    lane = lax.broadcasted_iota(jnp.int32, (48, 128), 1)
    plane = 0
    brick = None
    for rhs_ref, image_ref in zip(rhs_refs, image_refs):
        for p in range(rhs_ref.shape[0]):
            full = []
            for a in range(2):
                rhs = rhs_ref[p, a]
                full.append(scale_rhs * rhs + step_last * (rhs - step_first * image_ref[p, a]))
            if 5 <= plane < 7:
                for a in range(2):
                    solution_ref[a, plane - 5] = full[a][8:24]
            for h in range(2):
                window = jnp.concatenate([f[8 * h : 8 * h + 24] for f in full], axis=0)
                cut = slice(128 * h, 128 * (h + 1))
                low = jnp.where(lane > 0, pltpu.roll(window, 1, 1), 0.0)
                high = jnp.where(lane < 127, pltpu.roll(window, 127, 1), 0.0)
                features_ref[plane, 0:48, cut] = low.astype(BF16)
                features_ref[plane, 48:96, cut] = window.astype(BF16)
                features_ref[plane, 96:144, cut] = high.astype(BF16)
            plane += 1

    def outside(out_ref, depth):
        planes, cells, _ = out_ref.shape
        extra = 4 - depth
        first = 2 * slab_at - extra

        last_plane = 2 * slab_at + 1 + extra
        edge = (coil_at == 0) | (coil_at == coil_count - 1) | (first < 0) | (last_plane >= 2 * slab_count)

        @pl.when(edge)
        def _():
            blank = jnp.zeros((planes, extra * 32, 128), BF16)

            @pl.when(coil_at == 0)
            def _():
                out_ref[:, 0 : extra * 32, 0:128] = blank

            @pl.when(coil_at == coil_count - 1)
            def _():
                out_ref[:, cells - extra * 32 : cells, 128:256] = blank

            for p in list(range(extra)) + list(range(planes - extra, planes)):

                @pl.when((first + p < 0) | (first + p >= 2 * slab_count))
                def _():
                    out_ref[p] = jnp.zeros(out_ref.shape[1:], BF16)

    first_out = hidden_refs[0]

    for p in range(first_out.shape[0]):
        taps = jnp.concatenate([features_ref[p + u] for u in range(3)], axis=0)
        values = jnp.dot(w_first_ref[:, :432], taps, preferred_element_type=F32)
        first_out[p] = jnp.maximum(values, 0.0).astype(BF16)
    outside(first_out, 0)

    for m in range(len(hidden_refs) - 1):
        in_ref, out_ref = hidden_refs[m], hidden_refs[m + 1]
        starts = starts_of(out_ref.shape[1] // 32)

        cells = GROUP * 32
        for p in range(out_ref.shape[0]):
            for start in starts:
                rows = slice(start * 32, (start + GROUP + 2) * 32)
                taps = jnp.concatenate([in_ref[p + u, rows] for u in range(3)], axis=0)
                sums = jnp.dot(w_middle_ref[m, :, : (GROUP + 2) * 96], taps, preferred_element_type=F32)
                values = shifted_sum([sums[t * cells : (t + 1) * cells] for t in range(3)])
                out_ref[p, start * 32 : start * 32 + cells] = jnp.maximum(values, 0.0).astype(BF16)
        outside(out_ref, m + 1)

    in_ref = hidden_refs[-1]
    for p in range(2):
        taps = jnp.concatenate([in_ref[p + u] for u in range(3)], axis=0)
        sums = jnp.dot(w_last_ref[:, :960], taps, preferred_element_type=F32)
        lane = lax.broadcasted_iota(jnp.int32, (64, 128), 1)
        for h in range(2):
            part = sums[:, 128 * h : 128 * (h + 1)]
            low = jnp.where(lane > 0, pltpu.roll(part, 1, 1), 0.0)
            high = jnp.where(lane < 127, pltpu.roll(part, 127, 1), 0.0)
            for a in range(2):
                rows = []
                for r in range(8):
                    at = 8 * r + a
                    rows.append(low[at : at + 1] + part[at + 2 : at + 3] + high[at + 4 : at + 5])
                piece = jnp.concatenate(rows, axis=0)
                refined_ref[a, p, 8 * h : 8 * h + 8] = solution_ref[a, p, 8 * h : 8 * h + 8] + piece


def tables_kernel(first_ref, middle_ref, w_first_ref, w_middle_ref):
    def spots(size, target, count=512):
        column = lax.broadcasted_iota(jnp.int32, (size, count), 1)
        return jnp.where(column == target(lax.broadcasted_iota(jnp.int32, (size, count), 0)), 1.0, 0.0).astype(BF16)

    def first_target(source):
        channel, u, v, t = source // 27, source // 9 % 3, source // 3 % 3, source % 3
        return ((u * 3 + t) * 2 + channel) * 24 + SIDE - HALO + v

    base = jnp.dot(first_ref[...], spots(54, first_target), preferred_element_type=F32)
    for r in range(16):
        w_first_ref[32 * r : 32 * r + 32] = (pltpu.roll(base, r, 1) if r else base).astype(BF16)
    for m in range(middle_ref.shape[0]):
        base = jnp.zeros((96, 512), F32)
        for u in range(3):
            for v in range(3):
                place = spots(32, lambda source: source + (u * (GROUP + 2) + v) * 32)
                taps = jnp.concatenate([middle_ref[m, u, v, t] for t in range(3)], axis=0)
                base = base + jnp.dot(taps, place, preferred_element_type=F32)
        for r in range(GROUP):
            band = (pltpu.roll(base, 32 * r, 1) if r else base).astype(BF16)
            for t in range(3):
                start = (t * GROUP + r) * 32
                w_middle_ref[m, start : start + 32] = band[32 * t : 32 * t + 32]


def last_table_kernel(last_ref, w_last_ref):
    bands = []
    for r in range(8):
        bands.append(pltpu.roll(last_ref[...], 32 * r, 1) if r else last_ref[...])
    w_last_ref[...] = jnp.concatenate(bands, axis=0).astype(BF16)


def tables(w_first, w_middle, w_last):
    first = w_first.reshape(w_first.shape[0], 54)
    middle = jnp.transpose(w_middle, (0, 3, 4, 5, 1, 2))
    last = jnp.pad(jnp.transpose(w_last, (4, 0, 2, 3, 1)), ((0, 0), (0, 0), (0, 0), (0, 7), (0, 0)))
    last = jnp.pad(last.reshape(6, 960), ((0, 2), (0, 64))).astype(F32)
    pair = call(
        tables_kernel,
        (struct((512, 512), BF16), struct((3, 96 * GROUP, 512), BF16)),
        (first, middle),
    )
    return (*pair, call(last_table_kernel, struct((64, 1024), BF16), (last,))), (first, last)


def swap(blocks, axis):
    return lax.all_to_all(blocks, axis, 0, 0, tiled=True)


def shifted(part, axis, step):
    count = lax.axis_size(axis)
    return lax.ppermute(part, axis, [(i, i + step) for i in range(count) if 0 <= i + step < count])


def near_planes(near):
    below, above = shifted(near, "slab", 1), shifted(near, "slab", -1)
    low, high = call(pack_kernel, (struct((3, 2, 32, 128)),) * 2, (below, near, above))
    return [shifted(low, "slab", 2), below, near, above, shifted(high, "slab", -2)]


def body(sensitivity, kspace, sampling, prior_image, w_first, w_middle, w_last):
    maps = sensitivity[0]
    len_y, len_z = maps.shape[2:]
    coils, slabs = lax.axis_size("coil"), lax.axis_size("slab")
    at = jnp.stack([lax.axis_index("coil"), lax.axis_index("slab")]).astype(jnp.int32)
    rows, columns = left_table(len_y), right_table(len_z)
    weights, prepared = tables(w_first, w_middle, w_last)

    term = adjoint(sampling, kspace[0], rows, columns, maps, coils)
    rhs_rows, copies = call(
        rows_kernel,
        (struct((64, 128)), struct((coils, 80, 128), jnp.int16)),
        (swap(term, "coil"), prior_image),
        after=prepared,
    )
    rhs = swap(copies, "coil")
    near_shape = struct((2, 2, 32, 128))
    term, spectrum, norms, rhs_near = call(
        normal_kernel,
        (
            struct((coils, 80, 128), jnp.int16),
            struct((2, 2, len_y, len_z)),
            struct((8, 128)),
            near_shape,
        ),
        (at, rhs, sampling, maps, rows, columns),
        in_smem=(0,),
    )
    rhs_parts = near_planes(rhs_near)
    copies, sums = call(
        image_kernel,
        (struct((coils, 80, 128), jnp.int16), struct((8, 128))),
        (swap(term, "coil"), rhs_rows, norms),
        after=(rhs_parts[1], rhs_parts[3]),
    )
    image = swap(copies, "coil")
    image_near = call(near_kernel, near_shape, (at, image), in_smem=(0,))
    tiles = call(
        last_kernel,
        struct((coils, 8, 128)),
        (sums, image, spectrum, sampling, maps, rows, columns),
        after=(*weights[2:], rhs_parts[0], rhs_parts[4], image_near),
    )
    image_parts = near_planes(image_near)
    tiles = call(spread_kernel, struct((slabs, 8, 128)), (swap(tiles, "coil"),), after=image_parts[:1])
    last = swap(tiles, "slab")
    scratch = [pltpu.VMEM((12, 144, 256), BF16)]
    scratch += [pltpu.VMEM((10 - 2 * m, (16 - 2 * m) * 32, 256), BF16) for m in range(4)]
    return call(
        functools.partial(denoise_kernel, coils, slabs),
        (struct(prior_image.shape), struct(prior_image.shape)),
        (at, last, *rhs_parts, *image_parts, *weights),
        scratch=scratch,
        in_smem=(0,),
    )


def solution(mesh):
    placed = (
        P("coil", None, "slab", None, None),
        P("coil", None, "slab", None, None),
        P("slab", None, None),
        P(None, "slab", "coil", None),
        P(),
        P(),
        P(),
    )
    return jax.shard_map(
        body,
        mesh=mesh,
        in_specs=placed,
        out_specs=(P(None, "slab", "coil", None), P(None, "slab", "coil", None)),
        check_vma=False,
    )
```
